32 devices in a mesh: chan: 16 (over z, y, core), day: 2 (over x).
Axes of the slice: x: 2, y: 2, z: 4, core: 2. Of those that a mesh axis runs over, the one named last changes fastest.
Arguments:
- spectra: bfloat16 [2, 256, 80, 256], P('day', 'chan'), may hold values from -500 to 500
Outputs:
- stacked: float32 [256, 256, 256], P('day', 'chan')
The draws below stay inside these ranges and needn't reach their ends.
All inputs are finite; a program needn't handle non-finite values.
Results may differ from the reference program's by a relative error of at most 0.0023.
Values may be sent and summed in bfloat16 or wider, within the bound.
No kernel may reach another device: no remote copies, remote signals or barrier semaphores. Data moves between devices by JAX's collectives and lax.ppermute only.
A program may use at most 128 MiB of HBM per device.

```python
import math
import jax
import jax.numpy as jnp
from jax import lax

F = 128
LAGS = 256
W = 80
CH_DEV = 16
C = 256
DAYS = 2
N_CHAN = 16


def draw_spectra(key, part):
    key = jax.random.fold_in(key, 11)
    base_key, row_key, col_key = jax.random.split(key, 3)
    shape = (DAYS, C, W, 2 * F)
    row_scale = jnp.exp(jax.random.uniform(row_key, (DAYS, C, W, 1), jnp.float32, 0.0, math.log(10.0)))
    col_scale = jnp.exp(jax.random.uniform(col_key, (1, C, 1, 2 * F), jnp.float32, 0.0, math.log(10.0)))
    values = jax.random.normal(base_key, shape, jnp.float32)
    return (jnp.clip(values, -5.0, 5.0) * row_scale * col_scale).astype(jnp.bfloat16)


def setup_inputs(seed: int = 0) -> dict:
    splits = jax.random.split(jax.random.key(seed), 2)
    spectra = draw_spectra(jax.random.fold_in(splits[1], 71), 0)
    return dict(spectra=spectra)


def freq_taper(bins):
    freq_index = jnp.arange(bins, dtype=jnp.float32)
    half_taper = 0.54 - 0.46 * jnp.cos(2.0 * jnp.pi * (freq_index + 0.5) / bins)
    return jnp.concatenate([half_taper, half_taper])

def whiten(spectra):
    values = spectra.astype(jnp.float32)
    bins = values.shape[-1] // 2
    band_power = lax.optimization_barrier(jnp.sum(values * values, axis=-1, keepdims=True)) / bins + 1e-06
    return (values * freq_taper(bins) / jnp.sqrt(band_power)).astype(jnp.bfloat16)

def lag_matrix(bins):
    lag_count = 2 * bins
    freq_index = jnp.arange(bins, dtype=jnp.int32)
    lag_index = jnp.arange(lag_count, dtype=jnp.int32) - bins
    wound = jnp.mod(freq_index[:, None] * lag_index[None, :], lag_count)
    phase_angle = 2.0 * jnp.pi / lag_count * wound.astype(jnp.float32)
    return jnp.concatenate([jnp.cos(phase_angle), -jnp.sin(phase_angle)], axis=0)

def cross_spectra(far_rows, near_rows):
    far_vals = far_rows.astype(jnp.float32)
    near_vals = near_rows.astype(jnp.float32)
    bins = far_vals.shape[-1] // 2
    windows = far_vals.shape[-2]
    far_re, far_im = (far_vals[..., :bins], far_vals[..., bins:])
    near_re, near_im = (near_vals[..., :bins], near_vals[..., bins:])
    real_part = jnp.einsum('djwf,diwf->jif', far_re, near_re) + jnp.einsum('djwf,diwf->jif', far_im, near_im)
    imag_part = jnp.einsum('djwf,diwf->jif', far_re, near_im) - jnp.einsum('djwf,diwf->jif', far_im, near_re)
    return jnp.concatenate([real_part, imag_part], axis=-1) / windows

def to_lags(cross, table):
    flat = cross.reshape(-1, cross.shape[-1])
    lagged = jnp.dot(flat, table, precision=lax.Precision.HIGHEST, preferred_element_type=jnp.float32)
    return lagged.reshape(cross.shape[:-1] + (table.shape[1],))

def reference(spectra):
    white = whiten(spectra)
    table = lag_matrix(F)
    blocks = jnp.moveaxis(white.reshape(DAYS, N_CHAN, CH_DEV, W, 2 * F), 1, 0)

    def one_block(far_rows):
        return to_lags(cross_spectra(far_rows, white), table) / DAYS
    stacked = lax.map(one_block, blocks)
    return stacked.reshape(C, C, LAGS)
```

```python
import functools

import jax
import jax.numpy as jnp
import numpy as np
from jax import lax
from jax.experimental import pallas as pl
from jax.experimental.pallas import tpu as pltpu
from jax.sharding import PartitionSpec as P

VMEM_LIMIT = 48 * 1024 * 1024


def taper_row(bins):
    half = 0.54 - 0.46 * np.cos(2.0 * np.pi * (np.arange(bins) + 0.5) / bins)
    return np.concatenate([half, half])[None, :].astype(np.float32)


def lag_table(bins, per_dev, groups, scale):
    lags = 2 * bins
    freq = (np.arange(per_dev)[None, :] * groups + np.arange(groups)[:, None]).reshape(-1)
    wound = (freq[:, None] * (np.arange(lags)[None, :] - bins)) % lags
    angle = 2.0 * np.pi / lags * wound
    table = (np.stack([np.cos(angle), -np.sin(angle)], axis=1) * scale).reshape(2 * bins, lags)
    table = table.astype(np.float32)
    high = table.astype(jnp.bfloat16)
    low = (table - high.astype(np.float32)).astype(jnp.bfloat16)
    return high, low


def pack_kernel(groups, per_dev, spectra_ref, taper_ref, out_ref, rows_ref):
    chans, windows, width = spectra_ref.shape
    bins = width // 2
    head = bins // 2
    stride = (per_dev + 1) * chans
    taper = taper_ref[...]
    for ch in range(chans):
        values = spectra_ref[ch].astype(jnp.float32)
        power = jnp.sum(values * values, axis=-1, keepdims=True) / bins + 1e-06
        white = (values * taper * lax.rsqrt(power)).astype(jnp.bfloat16).astype(jnp.float32)
        real, imag = white[:, :bins], white[:, bins:]
        main = jnp.concatenate([real[:head], imag[:head]], axis=0).T
        tail = jnp.concatenate([real[head:], imag[head:]], axis=0)
        turned = [tail] + [pltpu.roll(tail, bins - slot * groups, 1) for slot in range(1, per_dev)]
        tail = jnp.concatenate(turned, axis=0).T[:groups]
        for slot in range(per_dev):
            part = main[slot * groups:(slot + 1) * groups]
            rows_ref[pl.ds(slot * chans + ch, groups, stride=stride), :] = part
        rows_ref[pl.ds(per_dev * chans + ch, groups, stride=stride), :] = tail
    out_ref[...] = rows_ref[...].astype(jnp.bfloat16).reshape(out_ref.shape)


def swap_parts(rows, half):
    lanes = rows.shape[-1]
    values = rows.astype(jnp.float32)
    lane = lax.broadcasted_iota(jnp.int32, values.shape, 1)
    first = (lane % (2 * half)) < half
    ahead = pltpu.roll(values, lanes - half, 1)
    behind = pltpu.roll(values, half, 1)
    return jnp.where(first, ahead, -behind).astype(jnp.bfloat16)


def cross_kernel(in_ref, out_ref):
    blocks, days, parts, chans, lanes = in_ref.shape
    per_dev = parts - 1
    total = blocks * chans
    far = out_ref.shape[-1]
    narrow = lanes // per_dev // 2

    def rows(day, part):
        return in_ref[:, day, part].reshape(total, lanes)

    tails = [rows(day, per_dev) for day in range(days)]
    tails_swapped = [swap_parts(tail, narrow) for tail in tails]
    far_tail = jnp.concatenate(tails, axis=1)
    lane = lax.broadcasted_iota(jnp.int32, (total, lanes), 1) // (2 * narrow)
    dims = (((1,), (1,)), ((), ()))
    for slot in range(per_dev):
        mains = [rows(day, slot) for day in range(days)]
        far_main = jnp.concatenate(mains, axis=1)
        for kind in range(2):
            if kind == 0:
                near_main, near_tail = mains, tails
            else:
                near_main, near_tail = [swap_parts(m, lanes // 2) for m in mains], tails_swapped
            near_tail = [jnp.where(lane == slot, t, jnp.zeros_like(t)) for t in near_tail]
            cross = lax.dot_general(
                jnp.concatenate(near_main, axis=1), far_main, dims, preferred_element_type=jnp.float32
            ) + lax.dot_general(
                jnp.concatenate(near_tail, axis=1), far_tail, dims, preferred_element_type=jnp.float32
            )
            for half in range(out_ref.shape[1]):
                block = cross[:, half * far:(half + 1) * far].reshape(blocks, chans, far)
                out_ref[:, half, 2 * slot + kind] = block.astype(out_ref.dtype)


def lags_kernel(chans, cross_ref, high_ref, low_ref, out_ref, rows_ref):
    depth = high_ref.shape[0]
    rows_ref[...] = cross_ref[...].astype(jnp.float32)
    high, low = high_ref[...], low_ref[...]
    dims = (((0,), (0,)), ((), ()))
    for ch in range(chans):
        part = rows_ref[pl.ds(ch, depth, stride=chans), :].astype(jnp.bfloat16)
        lag = lax.dot_general(part, high, dims, preferred_element_type=jnp.float32)
        lag = lag + lax.dot_general(part, low, dims, preferred_element_type=jnp.float32)
        out_ref[:, ch, :] = lag


def call(kernel, out_shape, scratch, *operands):
    return pl.pallas_call(
        kernel,
        out_shape=out_shape,
        scratch_shapes=scratch,
        compiler_params=pltpu.CompilerParams(vmem_limit_bytes=VMEM_LIMIT),
    )(*operands)


def shards(both, n_chan, n_day, spectra):
    _, chans, windows, width = spectra.shape
    bins = width // 2
    axes = ("chan", "day") if both else ("chan",)
    days = n_day if both else 1
    groups = n_chan * days
    per_dev = bins // groups
    total = n_chan * chans
    far = total // n_day

    packed = call(
        functools.partial(pack_kernel, groups, per_dev),
        jax.ShapeDtypeStruct((groups, per_dev + 1, chans, bins), jnp.bfloat16),
        [pltpu.VMEM((groups * (per_dev + 1) * chans, bins), jnp.float32)],
        spectra[0],
        jnp.asarray(taper_row(bins)),
    )
    mine = lax.all_to_all(packed, axes, 0, 0, tiled=True)
    mine = mine.reshape(n_chan, days, per_dev + 1, chans, bins)
    kind = jnp.bfloat16 if both else jnp.float32
    cross = call(
        cross_kernel,
        jax.ShapeDtypeStruct((n_chan, n_day, 2 * per_dev, chans, far), kind),
        [],
        mine,
    )
    if both:
        cross = cross.reshape(groups, 2 * per_dev, chans, far)
    else:
        cross = lax.psum_scatter(cross, "day", scatter_dimension=1, tiled=False).astype(jnp.bfloat16)
    cross = lax.all_to_all(cross, axes, 0, 0, tiled=True)
    high, low = lag_table(bins, per_dev, groups, 1.0 / (windows * n_day))
    return call(
        functools.partial(lags_kernel, chans),
        jax.ShapeDtypeStruct((far, chans, width), jnp.float32),
        [pltpu.VMEM((width * chans, far), jnp.float32)],
        cross.reshape(width * chans, far),
        jnp.asarray(high),
        jnp.asarray(low),
    )


def solution(mesh):
    n_chan, n_day = mesh.shape["chan"], mesh.shape["day"]

    def run(spectra):
        bins = spectra.shape[-1] // 2
        both = bins % (n_chan * n_day) == 0
        return jax.shard_map(
            functools.partial(shards, both, n_chan, n_day),
            mesh=mesh,
            in_specs=(P("day", "chan", None, None),),
            out_specs=P("day", "chan", None),
            check_vma=False,
        )(spectra)

    return run
```

```python
import functools

import jax
import jax.numpy as jnp
import numpy as np
from jax import lax
from jax.experimental import pallas as pl
from jax.experimental.pallas import tpu as pltpu
from jax.sharding import PartitionSpec as P

VMEM_LIMIT = 48 * 1024 * 1024


def freq_taper(bins):
    freq_index = jnp.arange(bins, dtype=jnp.float32)
    half_taper = 0.54 - 0.46 * jnp.cos(2.0 * jnp.pi * (freq_index + 0.5) / bins)
    return jnp.concatenate([half_taper, half_taper])


def whiten(spectra):
    values = spectra.astype(jnp.float32)
    bins = values.shape[-1] // 2
    band_power = jnp.sum(values * values, axis=-1, keepdims=True) / bins + 1e-06
    return (values * freq_taper(bins) / jnp.sqrt(band_power)).astype(jnp.bfloat16)


def lag_matrix(bins):
    lag_count = 2 * bins
    freq_index = jnp.arange(bins, dtype=jnp.int32)
    lag_index = jnp.arange(lag_count, dtype=jnp.int32) - bins
    wound = jnp.mod(freq_index[:, None] * lag_index[None, :], lag_count)
    phase_angle = 2.0 * jnp.pi / lag_count * wound.astype(jnp.float32)
    return jnp.concatenate([jnp.cos(phase_angle), -jnp.sin(phase_angle)], axis=0)


def cross_spectra(far_rows, near_rows):
    bins = far_rows.shape[-1] // 2
    windows = far_rows.shape[-2]
    far_re, far_im = (far_rows[..., :bins], far_rows[..., bins:])
    near_re, near_im = (near_rows[..., :bins], near_rows[..., bins:])
    real_part = jnp.einsum("jwf,iwf->jif", far_re, near_re, preferred_element_type=jnp.float32)
    real_part = real_part + jnp.einsum(
        "jwf,iwf->jif", far_im, near_im, preferred_element_type=jnp.float32
    )
    imag_part = jnp.einsum("jwf,iwf->jif", far_re, near_im, preferred_element_type=jnp.float32)
    imag_part = imag_part - jnp.einsum(
        "jwf,iwf->jif", far_im, near_re, preferred_element_type=jnp.float32
    )
    return jnp.concatenate([real_part, imag_part], axis=-1) / windows


def to_lags(cross, table):
    flat = cross.reshape(-1, cross.shape[-1])
    lagged = jnp.dot(
        flat, table, precision=lax.Precision.HIGHEST, preferred_element_type=jnp.float32
    )
    return lagged.reshape(cross.shape[:-1] + (table.shape[1],))


def gathered_shards(spectra):
    local_white = whiten(spectra)[0]
    gathered = lax.all_gather(local_white, "chan", axis=0, tiled=True)
    table = lag_matrix(local_white.shape[-1] // 2)
    day_count = lax.axis_size("day")
    return lax.psum_scatter(
        to_lags(cross_spectra(gathered, local_white), table) / day_count,
        "day",
        scatter_dimension=0,
        tiled=True,
    )


def taper_row(bins):
    half = 0.54 - 0.46 * np.cos(2.0 * np.pi * (np.arange(bins) + 0.5) / bins)
    return np.concatenate([half, half])[None, :].astype(np.float32)


def lag_table(bins, per_dev, groups, scale):
    lags = 2 * bins
    freq = (np.arange(per_dev)[None, :] * groups + np.arange(groups)[:, None]).reshape(-1)
    wound = (freq[:, None] * (np.arange(lags)[None, :] - bins)) % lags
    angle = 2.0 * np.pi / lags * wound
    table = (np.stack([np.cos(angle), -np.sin(angle)], axis=1) * scale).reshape(2 * bins, lags)
    table = table.astype(np.float32)
    high = table.astype(jnp.bfloat16)
    low = (table - high.astype(np.float32)).astype(jnp.bfloat16)
    return high, low


def pack_kernel(groups, per_dev, me_ref, spectra_ref, taper_ref, *refs):
    out_refs, rows_ref = refs[:-1], refs[-1]
    chans, windows, width = spectra_ref.shape
    bins = width // 2
    head = bins // 2
    stride = (per_dev + 1) * chans
    taper = taper_ref[...]
    for ch in range(chans):
        values = spectra_ref[ch].astype(jnp.float32)
        power = jnp.sum(values * values, axis=-1, keepdims=True) / bins + 1e-06
        white = (values * taper * lax.rsqrt(power)).astype(jnp.bfloat16).astype(jnp.float32)
        real, imag = white[:, :bins], white[:, bins:]
        main = jnp.concatenate([real[:head], imag[:head]], axis=0).T
        tail = jnp.concatenate([real[head:], imag[head:]], axis=0)
        turned = [tail] + [pltpu.roll(tail, bins - slot * groups, 1) for slot in range(1, per_dev)]
        tail = jnp.concatenate(turned, axis=0).T[:groups]
        for slot in range(per_dev):
            part = main[slot * groups:(slot + 1) * groups]
            rows_ref[pl.ds(slot * chans + ch, groups, stride=stride), :] = part
        rows_ref[pl.ds(per_dev * chans + ch, groups, stride=stride), :] = tail
    for step, out_ref in enumerate(out_refs):
        start = pl.multiple_of((me_ref[0] ^ step) * stride, stride)
        out_ref[...] = rows_ref[pl.ds(start, stride), :].astype(jnp.bfloat16).reshape(out_ref.shape)


def swap_parts(rows, half):
    lanes = rows.shape[-1]
    values = rows.astype(jnp.float32)
    lane = lax.broadcasted_iota(jnp.int32, values.shape, 1)
    first = (lane % (2 * half)) < half
    ahead = pltpu.roll(values, lanes - half, 1)
    behind = pltpu.roll(values, half, 1)
    return jnp.where(first, ahead, -behind).astype(jnp.bfloat16)


def cross_kernel(days, me_ref, *refs):
    groups = (len(refs) - 2) // 2
    in_refs, out_refs, (held_ref, cross_ref) = refs[:groups], refs[groups:2 * groups], refs[2 * groups:]
    parts, chans, lanes = in_refs[0].shape
    blocks = groups // days
    per_dev = parts - 1
    total = blocks * chans
    far = cross_ref.shape[-1]
    narrow = lanes // per_dev // 2
    for step, in_ref in enumerate(in_refs):
        held_ref[me_ref[0] ^ step] = in_ref[...]

    def rows(day, part):
        return jnp.concatenate([held_ref[block * days + day, part] for block in range(blocks)], axis=0)

    tails = [rows(day, per_dev) for day in range(days)]
    tails_swapped = [swap_parts(tail, narrow) for tail in tails]
    far_tail = jnp.concatenate(tails, axis=1)
    lane = lax.broadcasted_iota(jnp.int32, (total, lanes), 1) // (2 * narrow)
    dims = (((1,), (1,)), ((), ()))
    for slot in range(per_dev):
        mains = [rows(day, slot) for day in range(days)]
        far_main = jnp.concatenate(mains, axis=1)
        for kind in range(2):
            if kind == 0:
                near_main, near_tail = mains, tails
            else:
                near_main, near_tail = [swap_parts(m, lanes // 2) for m in mains], tails_swapped
            near_tail = [jnp.where(lane == slot, t, jnp.zeros_like(t)) for t in near_tail]
            cross = lax.dot_general(
                jnp.concatenate(near_main, axis=1), far_main, dims, preferred_element_type=jnp.float32
            ) + lax.dot_general(
                jnp.concatenate(near_tail, axis=1), far_tail, dims, preferred_element_type=jnp.float32
            )
            cross = cross.astype(cross_ref.dtype)
            for group in range(groups):
                block, half = divmod(group, days)
                piece = cross[block * chans:(block + 1) * chans, half * far:(half + 1) * far]
                cross_ref[group, 2 * slot + kind] = piece
    for step, out_ref in enumerate(out_refs):
        out_ref[...] = cross_ref[me_ref[0] ^ step]


def lags_kernel(me_ref, *refs):
    in_refs, (high_ref, low_ref, out_ref, rows_ref) = refs[:-4], refs[-4:]
    kinds, chans, far = in_refs[0].shape
    depth = high_ref.shape[0]
    size = kinds * chans
    for step, in_ref in enumerate(in_refs):
        start = pl.multiple_of((me_ref[0] ^ step) * size, size)
        rows_ref[pl.ds(start, size), :] = in_ref[...].reshape(size, far).astype(jnp.float32)
    high, low = high_ref[...], low_ref[...]
    dims = (((0,), (0,)), ((), ()))
    for ch in range(chans):
        part = rows_ref[pl.ds(ch, depth, stride=chans), :].astype(jnp.bfloat16)
        lag = lax.dot_general(part, high, dims, preferred_element_type=jnp.float32)
        lag = lag + lax.dot_general(part, low, dims, preferred_element_type=jnp.float32)
        out_ref[:, ch, :] = lag


def call(kernel, out_shape, scratch, me, *operands):
    vmem = pl.BlockSpec(memory_space=pltpu.VMEM)
    return pl.pallas_call(
        kernel,
        out_shape=out_shape,
        in_specs=[pl.BlockSpec(memory_space=pltpu.SMEM)] + [vmem] * len(operands),
        out_specs=jax.tree.map(lambda _: vmem, out_shape),
        scratch_shapes=scratch,
        compiler_params=pltpu.CompilerParams(vmem_limit_bytes=VMEM_LIMIT),
    )(me, *operands)


def exchange(pieces, axes):
    groups = len(pieces)
    order = sorted(range(1, groups), key=lambda m: -m)
    moved = list(pieces)
    for m in order:
        moved[m] = lax.ppermute(pieces[m], axes, [(i, i ^ m) for i in range(groups)])
    return moved


def shards(n_chan, n_day, spectra):
    _, chans, windows, width = spectra.shape
    bins = width // 2
    axes = ("chan", "day")
    groups = n_chan * n_day
    per_dev = bins // groups
    far = n_chan * chans // n_day
    me = (lax.axis_index("chan") * n_day + lax.axis_index("day")).astype(jnp.int32).reshape(1)

    packed = call(
        functools.partial(pack_kernel, groups, per_dev),
        [jax.ShapeDtypeStruct((per_dev + 1, chans, bins), jnp.bfloat16)] * groups,
        [pltpu.VMEM((groups * (per_dev + 1) * chans, bins), jnp.float32)],
        me,
        spectra[0],
        jnp.asarray(taper_row(bins)),
    )
    cross = call(
        functools.partial(cross_kernel, n_day),
        [jax.ShapeDtypeStruct((2 * per_dev, chans, far), jnp.bfloat16)] * groups,
        [
            pltpu.VMEM((groups, per_dev + 1, chans, bins), jnp.bfloat16),
            pltpu.VMEM((groups, 2 * per_dev, chans, far), jnp.bfloat16),
        ],
        me,
        *exchange(packed, axes),
    )
    high, low = lag_table(bins, per_dev, groups, 1.0 / (windows * n_day))
    return call(
        lags_kernel,
        jax.ShapeDtypeStruct((far, chans, width), jnp.float32),
        [pltpu.VMEM((width * chans, far), jnp.float32)],
        me,
        *exchange(cross, axes),
        jnp.asarray(high),
        jnp.asarray(low),
    )


def solution(mesh):
    n_chan, n_day = mesh.shape["chan"], mesh.shape["day"]

    def run(spectra):
        bins = spectra.shape[-1] // 2
        split = bins % (n_chan * n_day) == 0
        return jax.shard_map(
            functools.partial(shards, n_chan, n_day) if split else gathered_shards,
            mesh=mesh,
            in_specs=(P("day", "chan", None, None),),
            out_specs=P("day", "chan", None),
            check_vma=False,
        )(spectra)

    return run
```

```python
import functools

import jax
import jax.numpy as jnp
import numpy as np
from jax import lax
from jax.experimental import pallas as pl
from jax.experimental.pallas import tpu as pltpu
from jax.sharding import PartitionSpec as P

VMEM_LIMIT = 48 * 1024 * 1024
PACK_VMEM_LIMIT = 53 * 1024 * 1024
FETCHES = 4
SENDS = 2


def freq_taper(bins):
    freq_index = jnp.arange(bins, dtype=jnp.float32)
    half_taper = 0.54 - 0.46 * jnp.cos(2.0 * jnp.pi * (freq_index + 0.5) / bins)
    return jnp.concatenate([half_taper, half_taper])


def whiten(spectra):
    values = spectra.astype(jnp.float32)
    bins = values.shape[-1] // 2
    band_power = jnp.sum(values * values, axis=-1, keepdims=True) / bins + 1e-06
    return (values * freq_taper(bins) / jnp.sqrt(band_power)).astype(jnp.bfloat16)


def lag_matrix(bins):
    lag_count = 2 * bins
    freq_index = jnp.arange(bins, dtype=jnp.int32)
    lag_index = jnp.arange(lag_count, dtype=jnp.int32) - bins
    wound = jnp.mod(freq_index[:, None] * lag_index[None, :], lag_count)
    phase_angle = 2.0 * jnp.pi / lag_count * wound.astype(jnp.float32)
    return jnp.concatenate([jnp.cos(phase_angle), -jnp.sin(phase_angle)], axis=0)


def cross_spectra(far_rows, near_rows):
    bins = far_rows.shape[-1] // 2
    windows = far_rows.shape[-2]
    far_re, far_im = (far_rows[..., :bins], far_rows[..., bins:])
    near_re, near_im = (near_rows[..., :bins], near_rows[..., bins:])
    real_part = jnp.einsum("jwf,iwf->jif", far_re, near_re, preferred_element_type=jnp.float32)
    real_part = real_part + jnp.einsum(
        "jwf,iwf->jif", far_im, near_im, preferred_element_type=jnp.float32
    )
    imag_part = jnp.einsum("jwf,iwf->jif", far_re, near_im, preferred_element_type=jnp.float32)
    imag_part = imag_part - jnp.einsum(
        "jwf,iwf->jif", far_im, near_re, preferred_element_type=jnp.float32
    )
    return jnp.concatenate([real_part, imag_part], axis=-1) / windows


def to_lags(cross, table):
    flat = cross.reshape(-1, cross.shape[-1])
    lagged = jnp.dot(
        flat, table, precision=lax.Precision.HIGHEST, preferred_element_type=jnp.float32
    )
    return lagged.reshape(cross.shape[:-1] + (table.shape[1],))


def gathered_shards(spectra):
    local_white = whiten(spectra)[0]
    gathered = lax.all_gather(local_white, "chan", axis=0, tiled=True)
    table = lag_matrix(local_white.shape[-1] // 2)
    day_count = lax.axis_size("day")
    return lax.psum_scatter(
        to_lags(cross_spectra(gathered, local_white), table) / day_count,
        "day",
        scatter_dimension=0,
        tiled=True,
    )


def lag_table(bins, per_dev, groups, scale):
    lags = 2 * bins
    freq = (np.arange(per_dev)[None, :] * groups + np.arange(groups)[:, None]).reshape(-1)
    wound = (freq[:, None] * (np.arange(lags)[None, :] - bins)) % lags
    angle = 2.0 * np.pi / lags * wound
    table = (np.stack([np.cos(angle), -np.sin(angle)], axis=1) * scale).reshape(2 * bins, lags)
    table = table.astype(np.float32)
    high = table.astype(jnp.bfloat16)
    low = (table - high.astype(np.float32)).astype(jnp.bfloat16)
    return high, low


def pack_kernel(groups, per_dev, spectra_ref, out_ref, held_ref, rows_ref, arrived):
    chans, windows, width = held_ref.shape
    bins = width // 2
    head = bins // 2
    stride = (per_dev + 1) * chans
    fetches = arrived.shape[0]
    batch = chans // fetches
    copies = []
    for step in range(fetches):
        part = pl.ds(step * batch, batch)
        copies.append(pltpu.make_async_copy(spectra_ref.at[part], held_ref.at[part], arrived.at[step]))
        copies[-1].start()
    freq = (lax.broadcasted_iota(jnp.int32, (1, width), 1) % bins).astype(jnp.float32)
    taper = 0.54 - 0.46 * jnp.cos(2.0 * jnp.pi * (freq + 0.5) / bins)
    for ch in range(chans):
        if ch % batch == 0:
            copies[ch // batch].wait()
        values = held_ref[ch].astype(jnp.float32)
        power = jnp.sum(values * values, axis=-1, keepdims=True) / bins + 1e-06
        white = (values * taper * lax.rsqrt(power)).astype(jnp.bfloat16).astype(jnp.float32)
        real, imag = white[:, :bins], white[:, bins:]
        main = jnp.concatenate([real[:head], imag[:head]], axis=0).T
        tail = jnp.concatenate([real[head:], imag[head:]], axis=0)
        turned = [tail] + [pltpu.roll(tail, bins - slot * groups, 1) for slot in range(1, per_dev)]
        tail = jnp.concatenate(turned, axis=0).T[:groups]
        for slot in range(per_dev):
            part = main[slot * groups:(slot + 1) * groups]
            rows_ref[pl.ds(slot * chans + ch, groups, stride=stride), :] = part
        rows_ref[pl.ds(per_dev * chans + ch, groups, stride=stride), :] = tail
    out_ref[...] = rows_ref[...].astype(jnp.bfloat16).reshape(out_ref.shape)


def swap_parts(rows, half):
    lanes = rows.shape[-1]
    values = rows.astype(jnp.float32)
    lane = lax.broadcasted_iota(jnp.int32, values.shape, 1)
    first = (lane % (2 * half)) < half
    ahead = pltpu.roll(values, lanes - half, 1)
    behind = pltpu.roll(values, half, 1)
    return jnp.where(first, ahead, -behind).astype(jnp.bfloat16)


def cross_kernel(order, days, in_ref, out_ref):
    groups, parts, chans, lanes = in_ref.shape
    blocks = groups // days
    per_dev = parts - 1
    total = blocks * chans
    far = out_ref.shape[-1]
    narrow = lanes // per_dev // 2

    def rows(day, part):
        return jnp.concatenate([in_ref[order[block][day], part] for block in range(blocks)], axis=0)

    tails = [rows(day, per_dev) for day in range(days)]
    tails_swapped = [swap_parts(tail, narrow) for tail in tails]
    far_tail = jnp.concatenate(tails, axis=1)
    lane = lax.broadcasted_iota(jnp.int32, (total, lanes), 1) // (2 * narrow)
    dims = (((1,), (1,)), ((), ()))
    for slot in range(per_dev):
        mains = [rows(day, slot) for day in range(days)]
        far_main = jnp.concatenate(mains, axis=1)
        for kind in range(2):
            if kind == 0:
                near_main, near_tail = mains, tails
            else:
                near_main, near_tail = [swap_parts(m, lanes // 2) for m in mains], tails_swapped
            near_tail = [jnp.where(lane == slot, t, jnp.zeros_like(t)) for t in near_tail]
            cross = lax.dot_general(
                jnp.concatenate(near_main, axis=1), far_main, dims, preferred_element_type=jnp.float32
            ) + lax.dot_general(
                jnp.concatenate(near_tail, axis=1), far_tail, dims, preferred_element_type=jnp.float32
            )
            cross = cross.astype(out_ref.dtype)
            for block in range(blocks):
                for half in range(days):
                    piece = cross[block * chans:(block + 1) * chans, half * far:(half + 1) * far]
                    out_ref[order[block][half], 2 * slot + kind] = piece


def lags_kernel(cross_ref, high_ref, low_ref, out_ref, rows_ref, lag_ref, sent):
    far, chans, _ = out_ref.shape
    depth = high_ref.shape[0]
    rows_ref[...] = cross_ref[...].astype(jnp.float32)
    high, low = high_ref[...], low_ref[...]
    dims = (((0,), (0,)), ((), ()))
    parts = sent.shape[0]
    batch = chans // parts
    copies = []
    for step in range(parts):
        for ch in range(step * batch, (step + 1) * batch):
            part = rows_ref[pl.ds(ch, depth, stride=chans), :].astype(jnp.bfloat16)
            lag = lax.dot_general(part, high, dims, preferred_element_type=jnp.float32)
            lag = lag + lax.dot_general(part, low, dims, preferred_element_type=jnp.float32)
            lag_ref[:, ch, :] = lag
        done = pl.ds(step * batch, batch)
        copies.append(pltpu.make_async_copy(lag_ref.at[:, done], out_ref.at[:, done], sent.at[step]))
        copies[-1].start()
    for copy in copies:
        copy.wait()


def call(kernel, out_shape, scratch, in_spaces, out_space, *operands, vmem=VMEM_LIMIT):
    return pl.pallas_call(
        kernel,
        out_shape=out_shape,
        in_specs=[pl.BlockSpec(memory_space=space) for space in in_spaces],
        out_specs=pl.BlockSpec(memory_space=out_space),
        scratch_shapes=scratch,
        compiler_params=pltpu.CompilerParams(vmem_limit_bytes=vmem),
    )(*operands)


def shards(axes, order, spectra):
    _, chans, windows, width = spectra.shape
    bins = width // 2
    n_chan, n_day = order.shape
    groups = n_chan * n_day
    per_dev = bins // groups
    far = n_chan * chans // n_day

    packed = call(
        functools.partial(pack_kernel, groups, per_dev),
        jax.ShapeDtypeStruct((groups, per_dev + 1, chans, bins), jnp.bfloat16),
        [
            pltpu.VMEM((chans, windows, width), jnp.bfloat16),
            pltpu.VMEM((groups * (per_dev + 1) * chans, bins), jnp.float32),
            pltpu.SemaphoreType.DMA((FETCHES,)),
        ],
        [pltpu.HBM],
        pltpu.VMEM,
        spectra[0],
        vmem=PACK_VMEM_LIMIT,
    )
    mine = lax.all_to_all(packed, axes, 0, 0, tiled=True)
    cross = call(
        functools.partial(cross_kernel, order.tolist(), n_day),
        jax.ShapeDtypeStruct((groups, 2 * per_dev, chans, far), jnp.bfloat16),
        [],
        [pltpu.VMEM],
        pltpu.VMEM,
        mine,
    )
    cross = lax.all_to_all(cross, axes, 0, 0, tiled=True)
    high, low = lag_table(bins, per_dev, groups, 1.0 / (windows * n_day))
    return call(
        lags_kernel,
        jax.ShapeDtypeStruct((far, chans, width), jnp.float32),
        [
            pltpu.VMEM((width * chans, far), jnp.float32),
            pltpu.VMEM((far, chans, width), jnp.float32),
            pltpu.SemaphoreType.DMA((SENDS,)),
        ],
        [pltpu.VMEM] * 3,
        pltpu.HBM,
        cross.reshape(width * chans, far),
        jnp.asarray(high),
        jnp.asarray(low),
    )


def solution(mesh):
    n_chan, n_day = mesh.shape["chan"], mesh.shape["day"]
    outer = 4 if n_chan % 4 == 0 else 1
    inner = n_chan // outer
    split_mesh = jax.sharding.Mesh(mesh.devices.reshape(outer, inner, n_day), ("outer", "inner", "day"))
    order = np.arange(n_chan * n_day).reshape(n_day, inner, outer).transpose(2, 1, 0).reshape(n_chan, n_day)

    def run(spectra):
        bins = spectra.shape[-1] // 2
        if bins % (n_chan * n_day):
            return jax.shard_map(
                gathered_shards,
                mesh=mesh,
                in_specs=(P("day", "chan", None, None),),
                out_specs=P("day", "chan", None),
                check_vma=False,
            )(spectra)
        return jax.shard_map(
            functools.partial(shards, ("day", "inner", "outer"), order),
            mesh=split_mesh,
            in_specs=(P("day", ("outer", "inner"), None, None),),
            out_specs=P("day", ("outer", "inner"), None),
            check_vma=False,
        )(spectra)

    return run
```

```python
import functools

import jax
import jax.numpy as jnp
import numpy as np
from jax import lax
from jax.experimental import pallas as pl
from jax.experimental.pallas import tpu as pltpu
from jax.sharding import PartitionSpec as P

VMEM_LIMIT = 48 * 1024 * 1024
PACK_VMEM_LIMIT = 53 * 1024 * 1024
FETCHES = 4
SENDS = 2


def freq_taper(bins):
    freq_index = jnp.arange(bins, dtype=jnp.float32)
    half_taper = 0.54 - 0.46 * jnp.cos(2.0 * jnp.pi * (freq_index + 0.5) / bins)
    return jnp.concatenate([half_taper, half_taper])


def whiten(spectra):
    values = spectra.astype(jnp.float32)
    bins = values.shape[-1] // 2
    band_power = jnp.sum(values * values, axis=-1, keepdims=True) / bins + 1e-06
    return (values * freq_taper(bins) / jnp.sqrt(band_power)).astype(jnp.bfloat16)


def lag_matrix(bins):
    lag_count = 2 * bins
    freq_index = jnp.arange(bins, dtype=jnp.int32)
    lag_index = jnp.arange(lag_count, dtype=jnp.int32) - bins
    wound = jnp.mod(freq_index[:, None] * lag_index[None, :], lag_count)
    phase_angle = 2.0 * jnp.pi / lag_count * wound.astype(jnp.float32)
    return jnp.concatenate([jnp.cos(phase_angle), -jnp.sin(phase_angle)], axis=0)


def cross_spectra(far_rows, near_rows):
    bins = far_rows.shape[-1] // 2
    windows = far_rows.shape[-2]
    far_re, far_im = (far_rows[..., :bins], far_rows[..., bins:])
    near_re, near_im = (near_rows[..., :bins], near_rows[..., bins:])
    real_part = jnp.einsum("jwf,iwf->jif", far_re, near_re, preferred_element_type=jnp.float32)
    real_part = real_part + jnp.einsum(
        "jwf,iwf->jif", far_im, near_im, preferred_element_type=jnp.float32
    )
    imag_part = jnp.einsum("jwf,iwf->jif", far_re, near_im, preferred_element_type=jnp.float32)
    imag_part = imag_part - jnp.einsum(
        "jwf,iwf->jif", far_im, near_re, preferred_element_type=jnp.float32
    )
    return jnp.concatenate([real_part, imag_part], axis=-1) / windows


def to_lags(cross, table):
    flat = cross.reshape(-1, cross.shape[-1])
    lagged = jnp.dot(
        flat, table, precision=lax.Precision.HIGHEST, preferred_element_type=jnp.float32
    )
    return lagged.reshape(cross.shape[:-1] + (table.shape[1],))


def gathered_shards(spectra):
    local_white = whiten(spectra)[0]
    gathered = lax.all_gather(local_white, "chan", axis=0, tiled=True)
    table = lag_matrix(local_white.shape[-1] // 2)
    day_count = lax.axis_size("day")
    return lax.psum_scatter(
        to_lags(cross_spectra(gathered, local_white), table) / day_count,
        "day",
        scatter_dimension=0,
        tiled=True,
    )


def lag_table(bins, per_dev, groups, scale):
    lags = 2 * bins
    freq = (np.arange(per_dev)[None, :] * groups + np.arange(groups)[:, None]).reshape(-1)
    wound = (freq[:, None] * (np.arange(lags)[None, :] - bins)) % lags
    angle = 2.0 * np.pi / lags * wound
    table = (np.stack([np.cos(angle), -np.sin(angle)], axis=1) * scale).reshape(2 * bins, lags)
    table = table.astype(np.float32)
    high = table.astype(jnp.bfloat16)
    low = (table - high.astype(np.float32)).astype(jnp.bfloat16)
    return high, low


def pack_kernel(groups, per_dev, spectra_ref, out_ref, held_ref, rows_ref, arrived):
    chans, windows, width = held_ref.shape
    bins = width // 2
    head = bins // 2
    shared = bins // (windows - head) // 2
    tails = per_dev // shared
    stride = (per_dev + tails) * chans
    fetches = arrived.shape[0]
    batch = chans // fetches
    copies = []
    for step in range(fetches):
        part = pl.ds(step * batch, batch)
        copies.append(pltpu.make_async_copy(spectra_ref.at[part], held_ref.at[part], arrived.at[step]))
        copies[-1].start()
    freq = (lax.broadcasted_iota(jnp.int32, (1, width), 1) % bins).astype(jnp.float32)
    taper = 0.54 - 0.46 * jnp.cos(2.0 * jnp.pi * (freq + 0.5) / bins)
    for ch in range(chans):
        if ch % batch == 0:
            copies[ch // batch].wait()
        values = held_ref[ch].astype(jnp.float32)
        power = jnp.sum(values * values, axis=-1, keepdims=True) / bins + 1e-06
        white = (values * taper * lax.rsqrt(power)).astype(jnp.bfloat16).astype(jnp.float32)
        real, imag = white[:, :bins], white[:, bins:]
        main = jnp.concatenate([real[:head], imag[:head]], axis=0).T
        tail = jnp.concatenate([real[head:], imag[head:]], axis=0)
        turned = [tail] + [pltpu.roll(tail, bins - slot * groups, 1) for slot in range(1, per_dev)]
        for slot in range(per_dev):
            part = main[slot * groups:(slot + 1) * groups]
            rows_ref[pl.ds(slot * chans + ch, groups, stride=stride), :] = part
        for step in range(tails):
            part = jnp.concatenate(turned[step * shared:(step + 1) * shared], axis=0).T[:groups]
            rows_ref[pl.ds((per_dev + step) * chans + ch, groups, stride=stride), :] = part
    out_ref[...] = rows_ref[...].astype(jnp.bfloat16).reshape(out_ref.shape)


def swap_parts(rows, half):
    lanes = rows.shape[-1]
    values = rows.astype(jnp.float32)
    lane = lax.broadcasted_iota(jnp.int32, values.shape, 1)
    first = (lane % (2 * half)) < half
    ahead = pltpu.roll(values, lanes - half, 1)
    behind = pltpu.roll(values, half, 1)
    return jnp.where(first, ahead, -behind).astype(jnp.bfloat16)


def cross_kernel(order, days, shared, own_ref, other_ref, out_ref):
    groups, parts, chans, lanes = own_ref.shape
    blocks = groups // days
    per_dev = parts * shared // (shared + 1)
    far = out_ref.shape[-1]
    half_blocks = blocks // days
    narrow = lanes // shared // 2

    def rows(ref, day, part, first, count):
        return jnp.concatenate([ref[order[block][day], part] for block in range(first, first + count)], axis=0)

    def near_rows(part):
        return [rows(own_ref, day, part, 0, blocks) for day in range(days)]

    def far_rows(part):
        pieces = []
        for day in range(days):
            column = []
            for half in range(days):
                for ref in (own_ref, other_ref):
                    column.append(rows(ref, day, part, half * half_blocks, half_blocks))
            pieces.append(jnp.concatenate(column, axis=0))
        return jnp.concatenate(pieces, axis=1)

    dims = (((1,), (1,)), ((), ()))
    for group in range(per_dev // shared):
        tails = near_rows(per_dev + group)
        tails_swapped = [swap_parts(tail, narrow) for tail in tails]
        far_tail = far_rows(per_dev + group)
        lane = lax.broadcasted_iota(jnp.int32, tails[0].shape, 1) // (2 * narrow)
        for place in range(shared):
            slot = group * shared + place
            mains = near_rows(slot)
            far_main = far_rows(slot)
            for kind in range(2):
                if kind == 0:
                    near_main, near_tail = mains, tails
                else:
                    near_main, near_tail = [swap_parts(m, lanes // 2) for m in mains], tails_swapped
                near_tail = [jnp.where(lane == place, t, jnp.zeros_like(t)) for t in near_tail]
                cross = lax.dot_general(
                    jnp.concatenate(near_main, axis=1), far_main, dims, preferred_element_type=jnp.float32
                ) + lax.dot_general(
                    jnp.concatenate(near_tail, axis=1), far_tail, dims, preferred_element_type=jnp.float32
                )
                cross = cross.astype(out_ref.dtype)
                for block in range(blocks):
                    for half in range(days):
                        piece = cross[block * chans:(block + 1) * chans, half * far:(half + 1) * far]
                        out_ref[order[block][half], 2 * slot + kind] = piece


def lags_kernel(core_ref, cross_ref, high_ref, low_ref, out_ref, rows_ref, lag_ref, sent):
    far, chans, _ = out_ref.shape
    depth = high_ref.shape[0]
    rows_ref[...] = cross_ref[...].astype(jnp.float32)
    high, low = high_ref[...], low_ref[...]
    dims = (((0,), (0,)), ((), ()))
    parts = sent.shape[0]
    batch = chans // parts
    copies = []
    runs = far // chans
    for step in range(parts):
        for ch in range(step * batch, (step + 1) * batch):
            part = rows_ref[pl.ds(ch, depth, stride=chans), :].astype(jnp.bfloat16)
            lag = lax.dot_general(part, high, dims, preferred_element_type=jnp.float32)
            lag = lag + lax.dot_general(part, low, dims, preferred_element_type=jnp.float32)
            for run in range(runs):
                core = (core_ref[0] + 2 * run // runs) % 2
                place = 2 * (run % (runs // 2)) + core
                lag_ref[pl.ds(place * chans, chans), ch, :] = lag[run * chans:(run + 1) * chans]
        done = pl.ds(step * batch, batch)
        copies.append(pltpu.make_async_copy(lag_ref.at[:, done], out_ref.at[:, done], sent.at[step]))
        copies[-1].start()
    for copy in copies:
        copy.wait()


def call(kernel, out_shape, scratch, in_spaces, out_space, *operands, vmem=VMEM_LIMIT):
    return pl.pallas_call(
        kernel,
        out_shape=out_shape,
        in_specs=[pl.BlockSpec(memory_space=space) for space in in_spaces],
        out_specs=pl.BlockSpec(memory_space=out_space),
        scratch_shapes=scratch,
        compiler_params=pltpu.CompilerParams(vmem_limit_bytes=vmem),
    )(*operands)


def shards(axes, order, spectra):
    _, chans, windows, width = spectra.shape
    bins = width // 2
    n_chip, n_day = order.shape
    groups = n_chip * n_day
    per_dev = bins // groups
    shared = bins // (windows - bins // 2) // 2
    parts = per_dev + per_dev // shared
    far = 2 * n_chip * chans // n_day

    packed = call(
        functools.partial(pack_kernel, groups, per_dev),
        jax.ShapeDtypeStruct((groups, parts, chans, bins), jnp.bfloat16),
        [
            pltpu.VMEM((chans, windows, width), jnp.bfloat16),
            pltpu.VMEM((groups * parts * chans, bins), jnp.float32),
            pltpu.SemaphoreType.DMA((FETCHES,)),
        ],
        [pltpu.HBM],
        pltpu.VMEM,
        spectra[0],
        vmem=PACK_VMEM_LIMIT,
    )
    own = lax.all_to_all(packed, axes, 0, 0, tiled=True)
    other = lax.ppermute(own, "core", [(0, 1), (1, 0)])
    cross = call(
        functools.partial(cross_kernel, order.tolist(), n_day, shared),
        jax.ShapeDtypeStruct((groups, 2 * per_dev, chans, far), jnp.bfloat16),
        [],
        [pltpu.VMEM] * 2,
        pltpu.VMEM,
        own,
        other,
    )
    cross = lax.all_to_all(cross, axes, 0, 0, tiled=True)
    high, low = lag_table(bins, per_dev, groups, 1.0 / (windows * n_day))
    return call(
        lags_kernel,
        jax.ShapeDtypeStruct((far, chans, width), jnp.float32),
        [
            pltpu.VMEM((width * chans, far), jnp.float32),
            pltpu.VMEM((far, chans, width), jnp.float32),
            pltpu.SemaphoreType.DMA((SENDS,)),
        ],
        [pltpu.SMEM] + [pltpu.VMEM] * 3,
        pltpu.HBM,
        lax.axis_index("core").astype(jnp.int32).reshape(1),
        cross.reshape(width * chans, far),
        jnp.asarray(high),
        jnp.asarray(low),
    )


def solution(mesh):
    n_chan, n_day = mesh.shape["chan"], mesh.shape["day"]
    split_mesh = jax.sharding.Mesh(mesh.devices.reshape(n_chan // 2, 2, n_day), ("chip", "core", "day"))
    order = np.arange(n_chan // 2 * n_day).reshape(n_chan // 2, n_day)

    def run(spectra):
        bins = spectra.shape[-1] // 2
        if bins % (n_chan * n_day):
            return jax.shard_map(
                gathered_shards,
                mesh=mesh,
                in_specs=(P("day", "chan", None, None),),
                out_specs=P("day", "chan", None),
                check_vma=False,
            )(spectra)
        return jax.shard_map(
            functools.partial(shards, ("chip", "day"), order),
            mesh=split_mesh,
            in_specs=(P("day", ("chip", "core"), None, None),),
            out_specs=P("day", ("chip", "core"), None),
            check_vma=False,
        )(spectra)

    return run
```

```python
import functools

import jax
import jax.numpy as jnp
import numpy as np
from jax import lax
from jax.experimental import pallas as pl
from jax.experimental.pallas import tpu as pltpu
from jax.sharding import PartitionSpec as P

VMEM_LIMIT = 48 * 1024 * 1024
PACK_VMEM_LIMIT = 53 * 1024 * 1024
FETCHES = 8
SENDS = 2


def freq_taper(bins):
    freq_index = jnp.arange(bins, dtype=jnp.float32)
    half_taper = 0.54 - 0.46 * jnp.cos(2.0 * jnp.pi * (freq_index + 0.5) / bins)
    return jnp.concatenate([half_taper, half_taper])


def whiten(spectra):
    values = spectra.astype(jnp.float32)
    bins = values.shape[-1] // 2
    band_power = jnp.sum(values * values, axis=-1, keepdims=True) / bins + 1e-06
    return (values * freq_taper(bins) / jnp.sqrt(band_power)).astype(jnp.bfloat16)


def lag_matrix(bins):
    lag_count = 2 * bins
    freq_index = jnp.arange(bins, dtype=jnp.int32)
    lag_index = jnp.arange(lag_count, dtype=jnp.int32) - bins
    wound = jnp.mod(freq_index[:, None] * lag_index[None, :], lag_count)
    phase_angle = 2.0 * jnp.pi / lag_count * wound.astype(jnp.float32)
    return jnp.concatenate([jnp.cos(phase_angle), -jnp.sin(phase_angle)], axis=0)


def cross_spectra(far_rows, near_rows):
    bins = far_rows.shape[-1] // 2
    windows = far_rows.shape[-2]
    far_re, far_im = (far_rows[..., :bins], far_rows[..., bins:])
    near_re, near_im = (near_rows[..., :bins], near_rows[..., bins:])
    real_part = jnp.einsum("jwf,iwf->jif", far_re, near_re, preferred_element_type=jnp.float32)
    real_part = real_part + jnp.einsum(
        "jwf,iwf->jif", far_im, near_im, preferred_element_type=jnp.float32
    )
    imag_part = jnp.einsum("jwf,iwf->jif", far_re, near_im, preferred_element_type=jnp.float32)
    imag_part = imag_part - jnp.einsum(
        "jwf,iwf->jif", far_im, near_re, preferred_element_type=jnp.float32
    )
    return jnp.concatenate([real_part, imag_part], axis=-1) / windows


def to_lags(cross, table):
    flat = cross.reshape(-1, cross.shape[-1])
    lagged = jnp.dot(
        flat, table, precision=lax.Precision.HIGHEST, preferred_element_type=jnp.float32
    )
    return lagged.reshape(cross.shape[:-1] + (table.shape[1],))


def gathered_shards(spectra):
    local_white = whiten(spectra)[0]
    gathered = lax.all_gather(local_white, "chan", axis=0, tiled=True)
    table = lag_matrix(local_white.shape[-1] // 2)
    day_count = lax.axis_size("day")
    return lax.psum_scatter(
        to_lags(cross_spectra(gathered, local_white), table) / day_count,
        "day",
        scatter_dimension=0,
        tiled=True,
    )


def lag_table(bins, per_dev, groups, scale):
    lags = 2 * bins
    freq = (np.arange(per_dev)[None, :] * groups + np.arange(groups)[:, None]).reshape(-1)
    wound = (freq[:, None] * (np.arange(lags)[None, :] - bins)) % lags
    angle = 2.0 * np.pi / lags * wound
    table = (np.stack([np.cos(angle), -np.sin(angle)], axis=1) * scale).reshape(2 * bins, lags)
    table = table.astype(np.float32)
    high = table.astype(jnp.bfloat16)
    low = (table - high.astype(np.float32)).astype(jnp.bfloat16)
    return high, low


def pack_kernel(groups, per_dev, spectra_ref, out_ref, held_ref, rows_ref, arrived):
    chans, windows, width = held_ref.shape
    bins = width // 2
    head = bins // 2
    stride = (per_dev + 1) * chans
    fetches = arrived.shape[0]
    batch = chans // fetches
    copies = []
    for step in range(fetches):
        part = pl.ds(step * batch, batch)
        copies.append(pltpu.make_async_copy(spectra_ref.at[part], held_ref.at[part], arrived.at[step]))
        copies[-1].start()
    freq = (lax.broadcasted_iota(jnp.int32, (1, width), 1) % bins).astype(jnp.float32)
    taper = 0.54 - 0.46 * jnp.cos(2.0 * jnp.pi * (freq + 0.5) / bins)
    for ch in range(chans):
        if ch % batch == 0:
            copies[ch // batch].wait()
        values = held_ref[ch].astype(jnp.float32)
        power = jnp.sum(values * values, axis=-1, keepdims=True) / bins + 1e-06
        white = (values * taper * lax.rsqrt(power)).astype(jnp.bfloat16)
        real, imag = white[:, :bins], white[:, bins:]
        main = jnp.concatenate([real[:head], imag[:head]], axis=0).T.astype(jnp.float32)
        tail = jnp.concatenate([real[head:], imag[head:]], axis=0).astype(jnp.float32)
        turned = [tail] + [pltpu.roll(tail, bins - slot * groups, 1) for slot in range(1, per_dev)]
        tail = jnp.concatenate(turned, axis=0).astype(jnp.bfloat16).T[:groups].astype(jnp.float32)
        for slot in range(per_dev):
            part = main[slot * groups:(slot + 1) * groups]
            rows_ref[pl.ds(slot * chans + ch, groups, stride=stride), :] = part
        rows_ref[pl.ds(per_dev * chans + ch, groups, stride=stride), :] = tail
    out_ref[...] = rows_ref[...].astype(jnp.bfloat16).reshape(out_ref.shape)


def swap_parts(rows, half):
    lanes = rows.shape[-1]
    values = rows.astype(jnp.float32)
    lane = lax.broadcasted_iota(jnp.int32, values.shape, 1)
    first = (lane % (2 * half)) < half
    ahead = pltpu.roll(values, lanes - half, 1)
    behind = pltpu.roll(values, half, 1)
    return jnp.where(first, ahead, -behind).astype(jnp.bfloat16)


def cross_kernel(order, days, in_ref, out_ref):
    groups, parts, chans, lanes = in_ref.shape
    blocks = groups // days
    per_dev = parts - 1
    total = blocks * chans
    far = out_ref.shape[-1]
    narrow = lanes // per_dev // 2

    def rows(day, part):
        return jnp.concatenate([in_ref[order[block][day], part] for block in range(blocks)], axis=0)

    tails = [rows(day, per_dev) for day in range(days)]
    tails_swapped = [swap_parts(tail, narrow) for tail in tails]
    far_tail = jnp.concatenate(tails, axis=1)
    lane = lax.broadcasted_iota(jnp.int32, (total, lanes), 1) // (2 * narrow)
    dims = (((1,), (1,)), ((), ()))
    for slot in range(per_dev):
        mains = [rows(day, slot) for day in range(days)]
        far_main = jnp.concatenate(mains, axis=1)
        for kind in range(2):
            if kind == 0:
                near_main, near_tail = mains, tails
            else:
                near_main, near_tail = [swap_parts(m, lanes // 2) for m in mains], tails_swapped
            near_tail = [jnp.where(lane == slot, t, jnp.zeros_like(t)) for t in near_tail]
            cross = lax.dot_general(
                jnp.concatenate(near_main, axis=1), far_main, dims, preferred_element_type=jnp.float32
            ) + lax.dot_general(
                jnp.concatenate(near_tail, axis=1), far_tail, dims, preferred_element_type=jnp.float32
            )
            cross = cross.astype(out_ref.dtype)
            for block in range(blocks):
                for half in range(days):
                    piece = cross[block * chans:(block + 1) * chans, half * far:(half + 1) * far]
                    out_ref[order[block][half], 2 * slot + kind] = piece


def lags_kernel(cross_ref, high_ref, low_ref, out_ref, rows_ref, lag_ref, sent):
    far, chans, _ = out_ref.shape
    halves, lanes = lag_ref.shape[0], lag_ref.shape[-1]
    depth = high_ref.shape[0]
    rows_ref[...] = cross_ref[...].astype(jnp.float32)
    high, low = high_ref[...], low_ref[...]
    dims = (((0,), (0,)), ((), ()))
    parts = sent.shape[0]
    batch = chans // parts
    copies = []
    for step in range(parts):
        for ch in range(step * batch, (step + 1) * batch):
            part = rows_ref[pl.ds(ch, depth, stride=chans), :].astype(jnp.bfloat16)
            lag = lax.dot_general(part, high, dims, preferred_element_type=jnp.float32)
            lag = lag + lax.dot_general(part, low, dims, preferred_element_type=jnp.float32)
            for half in range(halves):
                lag_ref[half, pl.ds(ch, far, stride=chans), :] = lag[:, half * lanes:(half + 1) * lanes]
        done = pl.ds(step * batch, batch)
        for half in range(halves):
            copies.append(
                pltpu.make_async_copy(
                    lag_ref.at[half].reshape(far, chans, lanes).at[:, done],
                    out_ref.at[:, done, pl.ds(half * lanes, lanes)],
                    sent.at[step, half],
                )
            )
            copies[-1].start()
    for copy in copies:
        copy.wait()


def call(kernel, out_shape, scratch, in_spaces, out_space, *operands, vmem=VMEM_LIMIT):
    return pl.pallas_call(
        kernel,
        out_shape=out_shape,
        in_specs=[pl.BlockSpec(memory_space=space) for space in in_spaces],
        out_specs=pl.BlockSpec(memory_space=out_space),
        scratch_shapes=scratch,
        compiler_params=pltpu.CompilerParams(vmem_limit_bytes=vmem),
    )(*operands)


def shards(axes, order, spectra):
    _, chans, windows, width = spectra.shape
    bins = width // 2
    n_chan, n_day = order.shape
    groups = n_chan * n_day
    per_dev = bins // groups
    far = n_chan * chans // n_day

    packed = call(
        functools.partial(pack_kernel, groups, per_dev),
        jax.ShapeDtypeStruct((groups, per_dev + 1, chans, bins), jnp.bfloat16),
        [
            pltpu.VMEM((chans, windows, width), jnp.bfloat16),
            pltpu.VMEM((groups * (per_dev + 1) * chans, bins), jnp.float32),
            pltpu.SemaphoreType.DMA((FETCHES,)),
        ],
        [pltpu.HBM],
        pltpu.VMEM,
        spectra[0],
        vmem=PACK_VMEM_LIMIT,
    )
    mine = lax.all_to_all(packed, axes, 0, 0, tiled=True)
    cross = call(
        functools.partial(cross_kernel, order.tolist(), n_day),
        jax.ShapeDtypeStruct((groups, 2 * per_dev, chans, far), jnp.bfloat16),
        [],
        [pltpu.VMEM],
        pltpu.VMEM,
        mine,
    )
    cross = lax.all_to_all(cross, axes, 0, 0, tiled=True)
    high, low = lag_table(bins, per_dev, groups, 1.0 / (windows * n_day))
    return call(
        lags_kernel,
        jax.ShapeDtypeStruct((far, chans, width), jnp.float32),
        [
            pltpu.VMEM((width * chans, far), jnp.float32),
            pltpu.VMEM((width // bins, far * chans, bins), jnp.float32),
            pltpu.SemaphoreType.DMA((SENDS, width // bins)),
        ],
        [pltpu.VMEM] * 3,
        pltpu.HBM,
        cross.reshape(width * chans, far),
        jnp.asarray(high),
        jnp.asarray(low),
    )


def solution(mesh):
    n_chan, n_day = mesh.shape["chan"], mesh.shape["day"]
    outer = 4 if n_chan % 4 == 0 else 1
    inner = n_chan // outer
    split_mesh = jax.sharding.Mesh(mesh.devices.reshape(outer, inner, n_day), ("outer", "inner", "day"))
    order = np.arange(n_chan * n_day).reshape(n_day, inner, outer).transpose(2, 1, 0).reshape(n_chan, n_day)

    def run(spectra):
        bins = spectra.shape[-1] // 2
        if bins % (n_chan * n_day):
            return jax.shard_map(
                gathered_shards,
                mesh=mesh,
                in_specs=(P("day", "chan", None, None),),
                out_specs=P("day", "chan", None),
                check_vma=False,
            )(spectra)
        return jax.shard_map(
            functools.partial(shards, ("day", "inner", "outer"), order),
            mesh=split_mesh,
            in_specs=(P("day", ("outer", "inner"), None, None),),
            out_specs=P("day", ("outer", "inner"), None),
            check_vma=False,
        )(spectra)

    return run
```

```python
import functools

import jax
import jax.numpy as jnp
import numpy as np
from jax import lax
from jax.experimental import pallas as pl
from jax.experimental.pallas import tpu as pltpu
from jax.sharding import PartitionSpec as P

VMEM_LIMIT = 48 * 1024 * 1024
PACK_VMEM_LIMIT = 53 * 1024 * 1024
FETCHES = 4
SENDS = 2


def freq_taper(bins):
    freq_index = jnp.arange(bins, dtype=jnp.float32)
    half_taper = 0.54 - 0.46 * jnp.cos(2.0 * jnp.pi * (freq_index + 0.5) / bins)
    return jnp.concatenate([half_taper, half_taper])


def whiten(spectra):
    values = spectra.astype(jnp.float32)
    bins = values.shape[-1] // 2
    band_power = jnp.sum(values * values, axis=-1, keepdims=True) / bins + 1e-06
    return (values * freq_taper(bins) / jnp.sqrt(band_power)).astype(jnp.bfloat16)


def lag_matrix(bins):
    lag_count = 2 * bins
    freq_index = jnp.arange(bins, dtype=jnp.int32)
    lag_index = jnp.arange(lag_count, dtype=jnp.int32) - bins
    wound = jnp.mod(freq_index[:, None] * lag_index[None, :], lag_count)
    phase_angle = 2.0 * jnp.pi / lag_count * wound.astype(jnp.float32)
    return jnp.concatenate([jnp.cos(phase_angle), -jnp.sin(phase_angle)], axis=0)


def cross_spectra(far_rows, near_rows):
    bins = far_rows.shape[-1] // 2
    windows = far_rows.shape[-2]
    far_re, far_im = (far_rows[..., :bins], far_rows[..., bins:])
    near_re, near_im = (near_rows[..., :bins], near_rows[..., bins:])
    real_part = jnp.einsum("jwf,iwf->jif", far_re, near_re, preferred_element_type=jnp.float32)
    real_part = real_part + jnp.einsum(
        "jwf,iwf->jif", far_im, near_im, preferred_element_type=jnp.float32
    )
    imag_part = jnp.einsum("jwf,iwf->jif", far_re, near_im, preferred_element_type=jnp.float32)
    imag_part = imag_part - jnp.einsum(
        "jwf,iwf->jif", far_im, near_re, preferred_element_type=jnp.float32
    )
    return jnp.concatenate([real_part, imag_part], axis=-1) / windows


def to_lags(cross, table):
    flat = cross.reshape(-1, cross.shape[-1])
    lagged = jnp.dot(
        flat, table, precision=lax.Precision.HIGHEST, preferred_element_type=jnp.float32
    )
    return lagged.reshape(cross.shape[:-1] + (table.shape[1],))


def gathered_shards(spectra):
    local_white = whiten(spectra)[0]
    gathered = lax.all_gather(local_white, "chan", axis=0, tiled=True)
    table = lag_matrix(local_white.shape[-1] // 2)
    day_count = lax.axis_size("day")
    return lax.psum_scatter(
        to_lags(cross_spectra(gathered, local_white), table) / day_count,
        "day",
        scatter_dimension=0,
        tiled=True,
    )


def lag_table(bins, per_dev, groups, scale):
    lags = 2 * bins
    freq = (np.arange(per_dev)[None, :] * groups + np.arange(groups)[:, None]).reshape(-1)
    wound = (freq[:, None] * (np.arange(lags)[None, :] - bins)) % lags
    angle = 2.0 * np.pi / lags * wound
    table = (np.stack([np.cos(angle), -np.sin(angle)], axis=1) * scale).reshape(2 * bins, lags)
    table = table.astype(np.float32)
    high = table.astype(jnp.bfloat16)
    low = (table - high.astype(np.float32)).astype(jnp.bfloat16)
    return high, low


def pack_kernel(groups, per_dev, spectra_ref, out_ref, held_ref, rows_ref, arrived):
    chans, windows, width = held_ref.shape
    bins = width // 2
    head = bins // 2
    size = (per_dev + 1) * chans
    stride = size + 1
    fetches = arrived.shape[0]
    batch = chans // fetches
    copies = []
    for step in range(fetches):
        part = pl.ds(step * batch, batch)
        copies.append(pltpu.make_async_copy(spectra_ref.at[part], held_ref.at[part], arrived.at[step]))
        copies[-1].start()
    freq = (lax.broadcasted_iota(jnp.int32, (1, width), 1) % bins).astype(jnp.float32)
    taper = 0.54 - 0.46 * jnp.cos(2.0 * jnp.pi * (freq + 0.5) / bins)
    for ch in range(chans):
        if ch % batch == 0:
            copies[ch // batch].wait()
        values = held_ref[ch].astype(jnp.float32)
        power = jnp.sum(values * values, axis=-1, keepdims=True) / bins + 1e-06
        white = (values * taper * lax.rsqrt(power)).astype(jnp.bfloat16).astype(jnp.float32)
        real, imag = white[:, :bins], white[:, bins:]
        main = jnp.concatenate([real[:head], imag[:head]], axis=0).T
        tail = jnp.concatenate([real[head:], imag[head:]], axis=0)
        turned = [tail] + [pltpu.roll(tail, bins - slot * groups, 1) for slot in range(1, per_dev)]
        tail = jnp.concatenate(turned, axis=0).T[:groups]
        for slot in range(per_dev):
            part = main[slot * groups:(slot + 1) * groups]
            rows_ref[pl.ds(slot * chans + ch, groups, stride=stride), :] = part
        rows_ref[pl.ds(per_dev * chans + ch, groups, stride=stride), :] = tail
    for group in range(groups):
        rows = rows_ref[pl.ds(group * stride, size), :]
        out_ref[group] = rows.astype(jnp.bfloat16).reshape(out_ref.shape[1:])


def swap_parts(rows, half):
    lanes = rows.shape[-1]
    values = rows.astype(jnp.float32)
    lane = lax.broadcasted_iota(jnp.int32, values.shape, 1)
    first = (lane % (2 * half)) < half
    ahead = pltpu.roll(values, lanes - half, 1)
    behind = pltpu.roll(values, half, 1)
    return jnp.where(first, ahead, -behind).astype(jnp.bfloat16)


def cross_kernel(order, days, in_ref, out_ref):
    groups, parts, chans, lanes = in_ref.shape
    blocks = groups // days
    per_dev = parts - 1
    total = blocks * chans
    far = out_ref.shape[-1]
    narrow = lanes // per_dev // 2

    def rows(day, part):
        return jnp.concatenate([in_ref[order[block][day], part] for block in range(blocks)], axis=0)

    tails = [rows(day, per_dev) for day in range(days)]
    tails_swapped = [swap_parts(tail, narrow) for tail in tails]
    far_tail = jnp.concatenate(tails, axis=1)
    lane = lax.broadcasted_iota(jnp.int32, (total, lanes), 1) // (2 * narrow)
    dims = (((1,), (1,)), ((), ()))
    for slot in range(per_dev):
        mains = [rows(day, slot) for day in range(days)]
        far_main = jnp.concatenate(mains, axis=1)
        for kind in range(2):
            if kind == 0:
                near_main, near_tail = mains, tails
            else:
                near_main, near_tail = [swap_parts(m, lanes // 2) for m in mains], tails_swapped
            near_tail = [jnp.where(lane == slot, t, jnp.zeros_like(t)) for t in near_tail]
            cross = lax.dot_general(
                jnp.concatenate(near_main, axis=1), far_main, dims, preferred_element_type=jnp.float32
            ) + lax.dot_general(
                jnp.concatenate(near_tail, axis=1), far_tail, dims, preferred_element_type=jnp.float32
            )
            cross = cross.astype(out_ref.dtype)
            for block in range(blocks):
                for half in range(days):
                    piece = cross[block * chans:(block + 1) * chans, half * far:(half + 1) * far]
                    out_ref[order[block][half], 2 * slot + kind] = piece


def lags_kernel(cross_ref, high_ref, low_ref, out_ref, rows_ref, lag_ref, sent):
    far, chans, _ = out_ref.shape
    depth = high_ref.shape[0]
    stride = chans + 1
    for row in range(depth):
        rows_ref[pl.ds(row * stride, chans), :] = cross_ref[pl.ds(row * chans, chans), :].astype(jnp.float32)
    high, low = high_ref[...], low_ref[...]
    dims = (((0,), (0,)), ((), ()))
    parts = sent.shape[0]
    batch = chans // parts
    copies = []
    for step in range(parts):
        for ch in range(step * batch, (step + 1) * batch):
            part = rows_ref[pl.ds(ch, depth, stride=stride), :].astype(jnp.bfloat16)
            lag = lax.dot_general(part, high, dims, preferred_element_type=jnp.float32)
            lag = lag + lax.dot_general(part, low, dims, preferred_element_type=jnp.float32)
            lag_ref[:, ch, :] = lag
        done = pl.ds(step * batch, batch)
        copies.append(pltpu.make_async_copy(lag_ref.at[:, done], out_ref.at[:, done], sent.at[step]))
        copies[-1].start()
    for copy in copies:
        copy.wait()


def call(kernel, out_shape, scratch, in_spaces, out_space, *operands, vmem=VMEM_LIMIT):
    return pl.pallas_call(
        kernel,
        out_shape=out_shape,
        in_specs=[pl.BlockSpec(memory_space=space) for space in in_spaces],
        out_specs=pl.BlockSpec(memory_space=out_space),
        scratch_shapes=scratch,
        compiler_params=pltpu.CompilerParams(vmem_limit_bytes=vmem),
    )(*operands)


def shards(axes, order, spectra):
    _, chans, windows, width = spectra.shape
    bins = width // 2
    n_chan, n_day = order.shape
    groups = n_chan * n_day
    per_dev = bins // groups
    far = n_chan * chans // n_day

    packed = call(
        functools.partial(pack_kernel, groups, per_dev),
        jax.ShapeDtypeStruct((groups, per_dev + 1, chans, bins), jnp.bfloat16),
        [
            pltpu.VMEM((chans, windows, width), jnp.bfloat16),
            pltpu.VMEM((groups * ((per_dev + 1) * chans + 1), bins), jnp.float32),
            pltpu.SemaphoreType.DMA((FETCHES,)),
        ],
        [pltpu.HBM],
        pltpu.VMEM,
        spectra[0],
        vmem=PACK_VMEM_LIMIT,
    )
    mine = lax.all_to_all(packed, axes, 0, 0, tiled=True)
    cross = call(
        functools.partial(cross_kernel, order.tolist(), n_day),
        jax.ShapeDtypeStruct((groups, 2 * per_dev, chans, far), jnp.bfloat16),
        [],
        [pltpu.VMEM],
        pltpu.VMEM,
        mine,
    )
    cross = lax.all_to_all(cross, axes, 0, 0, tiled=True)
    high, low = lag_table(bins, per_dev, groups, 1.0 / (windows * n_day))
    return call(
        lags_kernel,
        jax.ShapeDtypeStruct((far, chans, width), jnp.float32),
        [
            pltpu.VMEM((width * (chans + 1), far), jnp.float32),
            pltpu.VMEM((far, chans, width), jnp.float32),
            pltpu.SemaphoreType.DMA((SENDS,)),
        ],
        [pltpu.VMEM] * 3,
        pltpu.HBM,
        cross.reshape(width * chans, far),
        jnp.asarray(high),
        jnp.asarray(low),
    )


def solution(mesh):
    n_chan, n_day = mesh.shape["chan"], mesh.shape["day"]
    outer = 4 if n_chan % 4 == 0 else 1
    inner = n_chan // outer
    split_mesh = jax.sharding.Mesh(mesh.devices.reshape(outer, inner, n_day), ("outer", "inner", "day"))
    order = np.arange(n_chan * n_day).reshape(n_day, inner, outer).transpose(2, 1, 0).reshape(n_chan, n_day)

    def run(spectra):
        bins = spectra.shape[-1] // 2
        if bins % (n_chan * n_day):
            return jax.shard_map(
                gathered_shards,
                mesh=mesh,
                in_specs=(P("day", "chan", None, None),),
                out_specs=P("day", "chan", None),
                check_vma=False,
            )(spectra)
        return jax.shard_map(
            functools.partial(shards, ("day", "inner", "outer"), order),
            mesh=split_mesh,
            in_specs=(P("day", ("outer", "inner"), None, None),),
            out_specs=P("day", ("outer", "inner"), None),
            check_vma=False,
        )(spectra)

    return run
```

```python
import functools

import jax
import jax.numpy as jnp
import numpy as np
from jax import lax
from jax.experimental import pallas as pl
from jax.experimental.pallas import tpu as pltpu
from jax.sharding import PartitionSpec as P

VMEM_LIMIT = 48 * 1024 * 1024
PACK_VMEM_LIMIT = 53 * 1024 * 1024
FETCHES = 4
SENDS = 2


def freq_taper(bins):
    freq_index = jnp.arange(bins, dtype=jnp.float32)
    half_taper = 0.54 - 0.46 * jnp.cos(2.0 * jnp.pi * (freq_index + 0.5) / bins)
    return jnp.concatenate([half_taper, half_taper])


def whiten(spectra):
    values = spectra.astype(jnp.float32)
    bins = values.shape[-1] // 2
    band_power = jnp.sum(values * values, axis=-1, keepdims=True) / bins + 1e-06
    return (values * freq_taper(bins) / jnp.sqrt(band_power)).astype(jnp.bfloat16)


def lag_matrix(bins):
    lag_count = 2 * bins
    freq_index = jnp.arange(bins, dtype=jnp.int32)
    lag_index = jnp.arange(lag_count, dtype=jnp.int32) - bins
    wound = jnp.mod(freq_index[:, None] * lag_index[None, :], lag_count)
    phase_angle = 2.0 * jnp.pi / lag_count * wound.astype(jnp.float32)
    return jnp.concatenate([jnp.cos(phase_angle), -jnp.sin(phase_angle)], axis=0)


def cross_spectra(far_rows, near_rows):
    bins = far_rows.shape[-1] // 2
    windows = far_rows.shape[-2]
    far_re, far_im = (far_rows[..., :bins], far_rows[..., bins:])
    near_re, near_im = (near_rows[..., :bins], near_rows[..., bins:])
    real_part = jnp.einsum("jwf,iwf->jif", far_re, near_re, preferred_element_type=jnp.float32)
    real_part = real_part + jnp.einsum(
        "jwf,iwf->jif", far_im, near_im, preferred_element_type=jnp.float32
    )
    imag_part = jnp.einsum("jwf,iwf->jif", far_re, near_im, preferred_element_type=jnp.float32)
    imag_part = imag_part - jnp.einsum(
        "jwf,iwf->jif", far_im, near_re, preferred_element_type=jnp.float32
    )
    return jnp.concatenate([real_part, imag_part], axis=-1) / windows


def to_lags(cross, table):
    flat = cross.reshape(-1, cross.shape[-1])
    lagged = jnp.dot(
        flat, table, precision=lax.Precision.HIGHEST, preferred_element_type=jnp.float32
    )
    return lagged.reshape(cross.shape[:-1] + (table.shape[1],))


def gathered_shards(spectra):
    local_white = whiten(spectra)[0]
    gathered = lax.all_gather(local_white, "chan", axis=0, tiled=True)
    table = lag_matrix(local_white.shape[-1] // 2)
    day_count = lax.axis_size("day")
    return lax.psum_scatter(
        to_lags(cross_spectra(gathered, local_white), table) / day_count,
        "day",
        scatter_dimension=0,
        tiled=True,
    )


def lag_table(bins, per_dev, groups, scale):
    lags = 2 * bins
    freq = (np.arange(per_dev)[None, :] * groups + np.arange(groups)[:, None]).reshape(-1)
    wound = (freq[:, None] * (np.arange(lags)[None, :] - bins)) % lags
    angle = 2.0 * np.pi / lags * wound
    table = (np.stack([np.cos(angle), -np.sin(angle)], axis=1) * scale).reshape(2 * bins, lags)
    table = table.astype(np.float32)
    high = table.astype(jnp.bfloat16)
    low = (table - high.astype(np.float32)).astype(jnp.bfloat16)
    return high, low


def pack_kernel(groups, per_dev, spectra_ref, first_ref, second_ref, held_ref, rows_ref, arrived):
    chans, windows, width = held_ref.shape
    bins = width // 2
    head = bins // 2
    size = (per_dev + 1) * chans
    stride = size + 1
    fetches = arrived.shape[0]
    batch = chans // fetches
    copies = []
    for step in range(fetches):
        part = pl.ds(step * batch, batch)
        copies.append(pltpu.make_async_copy(spectra_ref.at[part], held_ref.at[part], arrived.at[step]))
        copies[-1].start()
    freq = (lax.broadcasted_iota(jnp.int32, (1, width), 1) % bins).astype(jnp.float32)
    taper = 0.54 - 0.46 * jnp.cos(2.0 * jnp.pi * (freq + 0.5) / bins)
    for ch in range(chans):
        if ch % batch == 0:
            copies[ch // batch].wait()
        values = held_ref[ch].astype(jnp.float32)
        power = jnp.sum(values * values, axis=-1, keepdims=True) / bins + 1e-06
        white = (values * taper * lax.rsqrt(power)).astype(jnp.bfloat16).astype(jnp.float32)
        real, imag = white[:, :bins], white[:, bins:]
        main = jnp.concatenate([real[:head], imag[:head]], axis=0).T
        tail = jnp.concatenate([real[head:], imag[head:]], axis=0)
        turned = [tail] + [pltpu.roll(tail, bins - slot * groups, 1) for slot in range(1, per_dev)]
        tail = jnp.concatenate(turned, axis=0).T[:groups]
        for slot in range(per_dev):
            part = main[slot * groups:(slot + 1) * groups]
            rows_ref[pl.ds(slot * chans + ch, groups, stride=stride), :] = part
        rows_ref[pl.ds(per_dev * chans + ch, groups, stride=stride), :] = tail
    late = second_ref.shape[1]
    for group in range(groups):
        rows = rows_ref[pl.ds(group * stride, size), :].astype(jnp.bfloat16).reshape(per_dev + 1, chans, bins)
        second_ref[group] = rows[:late]
        first_ref[group] = rows[late:]


def swap_parts(rows, half):
    lanes = rows.shape[-1]
    values = rows.astype(jnp.float32)
    lane = lax.broadcasted_iota(jnp.int32, values.shape, 1)
    first = (lane % (2 * half)) < half
    ahead = pltpu.roll(values, lanes - half, 1)
    behind = pltpu.roll(values, half, 1)
    return jnp.where(first, ahead, -behind).astype(jnp.bfloat16)


def cross_kernel(order, days, per_dev, slots, main_ref, tail_ref, out_ref):
    groups, _, chans, lanes = main_ref.shape
    blocks = groups // days
    total = blocks * chans
    far = out_ref.shape[-1]
    narrow = lanes // per_dev // 2

    def rows(ref, day, part):
        return jnp.concatenate([ref[order[block][day], part] for block in range(blocks)], axis=0)

    tails = [rows(tail_ref, day, tail_ref.shape[1] - 1) for day in range(days)]
    tails_swapped = [swap_parts(tail, narrow) for tail in tails]
    far_tail = jnp.concatenate(tails, axis=1)
    lane = lax.broadcasted_iota(jnp.int32, (total, lanes), 1) // (2 * narrow)
    dims = (((1,), (1,)), ((), ()))
    for part, slot in enumerate(slots):
        mains = [rows(main_ref, day, part) for day in range(days)]
        far_main = jnp.concatenate(mains, axis=1)
        for kind in range(2):
            if kind == 0:
                near_main, near_tail = mains, tails
            else:
                near_main, near_tail = [swap_parts(m, lanes // 2) for m in mains], tails_swapped
            near_tail = [jnp.where(lane == slot, t, jnp.zeros_like(t)) for t in near_tail]
            cross = lax.dot_general(
                jnp.concatenate(near_main, axis=1), far_main, dims, preferred_element_type=jnp.float32
            ) + lax.dot_general(
                jnp.concatenate(near_tail, axis=1), far_tail, dims, preferred_element_type=jnp.float32
            )
            cross = cross.astype(out_ref.dtype)
            for block in range(blocks):
                for half in range(days):
                    piece = cross[block * chans:(block + 1) * chans, half * far:(half + 1) * far]
                    out_ref[order[block][half], 2 * part + kind] = piece


def lag_part(cross_ref, rows_ref, chans):
    depth = cross_ref.shape[0] // chans
    stride = chans + 1
    for row in range(depth):
        rows_ref[pl.ds(row * stride, chans), :] = cross_ref[pl.ds(row * chans, chans), :].astype(jnp.float32)
    dims = (((0,), (0,)), ((), ()))

    def channel(ch, high, low):
        part = rows_ref[pl.ds(ch, depth, stride=stride), :].astype(jnp.bfloat16)
        lag = lax.dot_general(part, high, dims, preferred_element_type=jnp.float32)
        return lag + lax.dot_general(part, low, dims, preferred_element_type=jnp.float32)

    return channel


def first_lags_kernel(cross_ref, high_ref, low_ref, out_ref, rows_ref):
    chans = out_ref.shape[0]
    channel = lag_part(cross_ref, rows_ref, chans)
    high, low = high_ref[...], low_ref[...]
    for ch in range(chans):
        out_ref[ch] = channel(ch, high, low)


def lags_kernel(cross_ref, sum_ref, high_ref, low_ref, out_ref, rows_ref, lag_ref, sent):
    chans = out_ref.shape[1]
    channel = lag_part(cross_ref, rows_ref, chans)
    high, low = high_ref[...], low_ref[...]
    parts = sent.shape[0]
    batch = chans // parts
    copies = []
    for step in range(parts):
        for ch in range(step * batch, (step + 1) * batch):
            lag_ref[:, ch, :] = sum_ref[ch] + channel(ch, high, low)
        done = pl.ds(step * batch, batch)
        copies.append(pltpu.make_async_copy(lag_ref.at[:, done], out_ref.at[:, done], sent.at[step]))
        copies[-1].start()
    for copy in copies:
        copy.wait()


def call(kernel, out_shape, scratch, in_spaces, out_space, cost, *operands, vmem=VMEM_LIMIT):
    space = pl.BlockSpec(memory_space=out_space)
    return pl.pallas_call(
        kernel,
        out_shape=out_shape,
        in_specs=[pl.BlockSpec(memory_space=space) for space in in_spaces],
        out_specs=jax.tree.map(lambda _: space, out_shape),
        scratch_shapes=scratch,
        compiler_params=pltpu.CompilerParams(vmem_limit_bytes=vmem),
        cost_estimate=pl.CostEstimate(flops=cost[0], bytes_accessed=cost[1], transcendentals=0),
    )(*operands)


def shards(axes, order, spectra):
    _, chans, windows, width = spectra.shape
    bins = width // 2
    n_chan, n_day = order.shape
    groups = n_chan * n_day
    per_dev = bins // groups
    total = n_chan * chans
    far = total // n_day
    late = per_dev // 2
    early = per_dev - late

    first, second = call(
        functools.partial(pack_kernel, groups, per_dev),
        [
            jax.ShapeDtypeStruct((groups, early + 1, chans, bins), jnp.bfloat16),
            jax.ShapeDtypeStruct((groups, late, chans, bins), jnp.bfloat16),
        ],
        [
            pltpu.VMEM((chans, windows, width), jnp.bfloat16),
            pltpu.VMEM((groups * ((per_dev + 1) * chans + 1), bins), jnp.float32),
            pltpu.SemaphoreType.DMA((FETCHES,)),
        ],
        [pltpu.HBM],
        pltpu.VMEM,
        (0, 6 * chans * windows * width),
        spectra[0],
        vmem=PACK_VMEM_LIMIT,
    )

    def exchange(part):
        return lax.all_to_all(part, axes, 0, 0, tiled=True)

    def cross(main, tail, slots):
        size = groups * 2 * len(slots) * chans * far
        out = call(
            functools.partial(cross_kernel, order.tolist(), n_day, per_dev, slots),
            jax.ShapeDtypeStruct((groups, 2 * len(slots), chans, far), jnp.bfloat16),
            [],
            [pltpu.VMEM] * 2,
            pltpu.VMEM,
            (2 * size * 512, 2 * size),
            main,
            tail,
        )
        return exchange(out).reshape(-1, far)

    early_slots, late_slots = tuple(range(late, per_dev)), tuple(range(late))
    first, second = exchange(first), exchange(second)
    parts = [cross(first, first, early_slots), cross(second, first, late_slots)]
    tables = lag_table(bins, per_dev, groups, 1.0 / (windows * n_day))
    tables = [table.reshape(groups, per_dev, 2, width) for table in tables]
    tables = [
        [jnp.asarray(table[:, slots].reshape(-1, width)) for table in tables] for slots in (early_slots, late_slots)
    ]

    def rows(part):
        return pltpu.VMEM((part.shape[0] // chans * (chans + 1), far), jnp.float32)

    sums = call(
        first_lags_kernel,
        jax.ShapeDtypeStruct((chans, far, width), jnp.float32),
        [rows(parts[0])],
        [pltpu.VMEM] * 3,
        pltpu.VMEM,
        (4 * parts[0].size * width, 4 * chans * far * width),
        parts[0],
        *tables[0],
    )
    return call(
        lags_kernel,
        jax.ShapeDtypeStruct((far, chans, width), jnp.float32),
        [
            rows(parts[1]),
            pltpu.VMEM((far, chans, width), jnp.float32),
            pltpu.SemaphoreType.DMA((SENDS,)),
        ],
        [pltpu.VMEM] * 4,
        pltpu.HBM,
        (4 * parts[1].size * width, 8 * chans * far * width),
        parts[1],
        sums,
        *tables[1],
    )


def solution(mesh):
    n_chan, n_day = mesh.shape["chan"], mesh.shape["day"]
    outer = 4 if n_chan % 4 == 0 else 1
    inner = n_chan // outer
    split_mesh = jax.sharding.Mesh(mesh.devices.reshape(outer, inner, n_day), ("outer", "inner", "day"))
    order = np.arange(n_chan * n_day).reshape(n_day, inner, outer).transpose(2, 1, 0).reshape(n_chan, n_day)

    def run(spectra):
        bins = spectra.shape[-1] // 2
        if bins % (n_chan * n_day):
            return jax.shard_map(
                gathered_shards,
                mesh=mesh,
                in_specs=(P("day", "chan", None, None),),
                out_specs=P("day", "chan", None),
                check_vma=False,
            )(spectra)
        return jax.shard_map(
            functools.partial(shards, ("day", "inner", "outer"), order),
            mesh=split_mesh,
            in_specs=(P("day", ("outer", "inner"), None, None),),
            out_specs=P("day", ("outer", "inner"), None),
            check_vma=False,
        )(spectra)

    return run
```

```python
import functools

import jax
import jax.numpy as jnp
import numpy as np
from jax import lax
from jax.experimental import pallas as pl
from jax.experimental.pallas import tpu as pltpu
from jax.sharding import PartitionSpec as P

VMEM_LIMIT = 48 * 1024 * 1024
PACK_VMEM_LIMIT = 53 * 1024 * 1024
FETCHES = 4
SENDS = (2, 2)


def freq_taper(bins):
    freq_index = jnp.arange(bins, dtype=jnp.float32)
    half_taper = 0.54 - 0.46 * jnp.cos(2.0 * jnp.pi * (freq_index + 0.5) / bins)
    return jnp.concatenate([half_taper, half_taper])


def whiten(spectra):
    values = spectra.astype(jnp.float32)
    bins = values.shape[-1] // 2
    band_power = jnp.sum(values * values, axis=-1, keepdims=True) / bins + 1e-06
    return (values * freq_taper(bins) / jnp.sqrt(band_power)).astype(jnp.bfloat16)


def lag_matrix(bins):
    lag_count = 2 * bins
    freq_index = jnp.arange(bins, dtype=jnp.int32)
    lag_index = jnp.arange(lag_count, dtype=jnp.int32) - bins
    wound = jnp.mod(freq_index[:, None] * lag_index[None, :], lag_count)
    phase_angle = 2.0 * jnp.pi / lag_count * wound.astype(jnp.float32)
    return jnp.concatenate([jnp.cos(phase_angle), -jnp.sin(phase_angle)], axis=0)


def cross_spectra(far_rows, near_rows):
    bins = far_rows.shape[-1] // 2
    windows = far_rows.shape[-2]
    far_re, far_im = (far_rows[..., :bins], far_rows[..., bins:])
    near_re, near_im = (near_rows[..., :bins], near_rows[..., bins:])
    real_part = jnp.einsum("jwf,iwf->jif", far_re, near_re, preferred_element_type=jnp.float32)
    real_part = real_part + jnp.einsum(
        "jwf,iwf->jif", far_im, near_im, preferred_element_type=jnp.float32
    )
    imag_part = jnp.einsum("jwf,iwf->jif", far_re, near_im, preferred_element_type=jnp.float32)
    imag_part = imag_part - jnp.einsum(
        "jwf,iwf->jif", far_im, near_re, preferred_element_type=jnp.float32
    )
    return jnp.concatenate([real_part, imag_part], axis=-1) / windows


def to_lags(cross, table):
    flat = cross.reshape(-1, cross.shape[-1])
    lagged = jnp.dot(
        flat, table, precision=lax.Precision.HIGHEST, preferred_element_type=jnp.float32
    )
    return lagged.reshape(cross.shape[:-1] + (table.shape[1],))


def gathered_shards(spectra):
    local_white = whiten(spectra)[0]
    gathered = lax.all_gather(local_white, "chan", axis=0, tiled=True)
    table = lag_matrix(local_white.shape[-1] // 2)
    day_count = lax.axis_size("day")
    return lax.psum_scatter(
        to_lags(cross_spectra(gathered, local_white), table) / day_count,
        "day",
        scatter_dimension=0,
        tiled=True,
    )


def lag_table(bins, per_dev, groups, scale):
    lags = 2 * bins
    freq = (np.arange(per_dev)[None, :] * groups + np.arange(groups)[:, None]).reshape(-1)
    wound = (freq[:, None] * (np.arange(lags)[None, :] - bins)) % lags
    angle = 2.0 * np.pi / lags * wound
    table = (np.stack([np.cos(angle), -np.sin(angle)], axis=1) * scale).reshape(2 * bins, lags)
    table = table.astype(np.float32)
    high = table.astype(jnp.bfloat16)
    low = (table - high.astype(np.float32)).astype(jnp.bfloat16)
    return high, low


def pack_kernel(groups, per_dev, spectra_ref, out_ref, held_ref, rows_ref, arrived):
    chans, windows, width = held_ref.shape
    bins = width // 2
    head = bins // 2
    size = (per_dev + 1) * chans
    stride = size + 1
    fetches = arrived.shape[0]
    batch = chans // fetches
    copies = []
    for step in range(fetches):
        part = pl.ds(step * batch, batch)
        copies.append(pltpu.make_async_copy(spectra_ref.at[part], held_ref.at[part], arrived.at[step]))
        copies[-1].start()
    freq = (lax.broadcasted_iota(jnp.int32, (1, width), 1) % bins).astype(jnp.float32)
    taper = 0.54 - 0.46 * jnp.cos(2.0 * jnp.pi * (freq + 0.5) / bins)
    lane = lax.broadcasted_iota(jnp.int32, (windows - head, bins), 1)
    pick = lax.broadcasted_iota(jnp.int32, (groups, bins), 1) % groups
    pick = (pick == lax.broadcasted_iota(jnp.int32, (groups, bins), 0)).astype(jnp.float32).astype(jnp.bfloat16)
    for ch in range(chans):
        if ch % batch == 0:
            copies[ch // batch].wait()
        values = held_ref[ch].astype(jnp.float32)
        power = jnp.sum(values * values, axis=-1, keepdims=True) / bins + 1e-06
        white = (values * taper * lax.rsqrt(power)).astype(jnp.bfloat16)
        real, imag = white[:, :bins], white[:, bins:]
        main = jnp.concatenate([real[:head], imag[:head]], axis=0).astype(jnp.float32).T
        spread = []
        for slot in range(per_dev):
            chosen = lane // groups == slot
            spread += [jnp.where(chosen, part[head:], jnp.zeros_like(part[head:])) for part in (real, imag)]
        tail = lax.dot_general(
            pick, jnp.concatenate(spread, axis=0), (((1,), (1,)), ((), ())), preferred_element_type=jnp.float32
        )
        for slot in range(per_dev):
            part = main[slot * groups:(slot + 1) * groups]
            rows_ref[pl.ds(slot * chans + ch, groups, stride=stride), :] = part
        rows_ref[pl.ds(per_dev * chans + ch, groups, stride=stride), :] = tail
    for group in range(groups):
        rows = rows_ref[pl.ds(group * stride, size), :]
        out_ref[group] = rows.astype(jnp.bfloat16).reshape(out_ref.shape[1:])


def swap_parts(rows, half):
    lanes = rows.shape[-1]
    values = rows.astype(jnp.float32)
    lane = lax.broadcasted_iota(jnp.int32, values.shape, 1)
    first = (lane % (2 * half)) < half
    ahead = pltpu.roll(values, lanes - half, 1)
    behind = pltpu.roll(values, half, 1)
    return jnp.where(first, ahead, -behind).astype(jnp.bfloat16)


def cross_kernel(order, days, in_ref, out_ref):
    groups, parts, chans, lanes = in_ref.shape
    blocks = groups // days
    per_dev = parts - 1
    total = blocks * chans
    far = out_ref.shape[-1]
    narrow = lanes // per_dev // 2

    def rows(day, part):
        return jnp.concatenate([in_ref[order[block][day], part] for block in range(blocks)], axis=0)

    tails = [rows(day, per_dev) for day in range(days)]
    tails_swapped = [swap_parts(tail, narrow) for tail in tails]
    far_tail = jnp.concatenate(tails, axis=1)
    lane = lax.broadcasted_iota(jnp.int32, (total, lanes), 1) // (2 * narrow)
    dims = (((1,), (1,)), ((), ()))
    for slot in range(per_dev):
        mains = [rows(day, slot) for day in range(days)]
        far_main = jnp.concatenate(mains, axis=1)
        for kind in range(2):
            if kind == 0:
                near_main, near_tail = mains, tails
            else:
                near_main, near_tail = [swap_parts(m, lanes // 2) for m in mains], tails_swapped
            near_tail = [jnp.where(lane == slot, t, jnp.zeros_like(t)) for t in near_tail]
            cross = lax.dot_general(
                jnp.concatenate(near_main, axis=1), far_main, dims, preferred_element_type=jnp.float32
            ) + lax.dot_general(
                jnp.concatenate(near_tail, axis=1), far_tail, dims, preferred_element_type=jnp.float32
            )
            cross = cross.astype(out_ref.dtype)
            for block in range(blocks):
                for half in range(days):
                    piece = cross[block * chans:(block + 1) * chans, half * far:(half + 1) * far]
                    out_ref[order[block][half], 2 * slot + kind] = piece


def lags_kernel(cross_ref, high_ref, low_ref, out_ref, rows_ref, flip_ref, lag_ref, sent):
    far, chans, _ = out_ref.shape
    depth = high_ref.shape[0]
    stride = chans + 1
    for row in range(depth):
        rows_ref[pl.ds(row * stride, chans), :] = cross_ref[pl.ds(row * chans, chans), :].astype(jnp.float32)
    high, low = high_ref[...], low_ref[...]
    parts, blocks = sent.shape
    batch, run = chans // parts, far // blocks
    copies = []
    for step in range(parts):
        group = range(step * batch, (step + 1) * batch)
        for ch in group:
            flip_ref[ch] = rows_ref[pl.ds(ch, depth, stride=stride), :].astype(jnp.bfloat16).T
        for block in range(blocks):
            done = pl.ds(block * run, run)
            for ch in group:
                part = flip_ref[ch, done]
                lag = jnp.dot(part, high, preferred_element_type=jnp.float32)
                lag_ref[done, ch, :] = lag + jnp.dot(part, low, preferred_element_type=jnp.float32)
            place = (done, pl.ds(step * batch, batch))
            copies.append(pltpu.make_async_copy(lag_ref.at[place], out_ref.at[place], sent.at[step, block]))
            copies[-1].start()
    for copy in copies:
        copy.wait()


def call(kernel, out_shape, scratch, in_spaces, out_space, *operands, vmem=VMEM_LIMIT):
    return pl.pallas_call(
        kernel,
        out_shape=out_shape,
        in_specs=[pl.BlockSpec(memory_space=space) for space in in_spaces],
        out_specs=pl.BlockSpec(memory_space=out_space),
        scratch_shapes=scratch,
        compiler_params=pltpu.CompilerParams(vmem_limit_bytes=vmem),
    )(*operands)


def shards(axes, order, spectra):
    _, chans, windows, width = spectra.shape
    bins = width // 2
    n_chan, n_day = order.shape
    groups = n_chan * n_day
    per_dev = bins // groups
    far = n_chan * chans // n_day

    packed = call(
        functools.partial(pack_kernel, groups, per_dev),
        jax.ShapeDtypeStruct((groups, per_dev + 1, chans, bins), jnp.bfloat16),
        [
            pltpu.VMEM((chans, windows, width), jnp.bfloat16),
            pltpu.VMEM((groups * ((per_dev + 1) * chans + 1), bins), jnp.float32),
            pltpu.SemaphoreType.DMA((FETCHES,)),
        ],
        [pltpu.HBM],
        pltpu.VMEM,
        spectra[0],
        vmem=PACK_VMEM_LIMIT,
    )
    mine = lax.all_to_all(packed, axes, 0, 0, tiled=True)
    cross = call(
        functools.partial(cross_kernel, order.tolist(), n_day),
        jax.ShapeDtypeStruct((groups, 2 * per_dev, chans, far), jnp.bfloat16),
        [],
        [pltpu.VMEM],
        pltpu.VMEM,
        mine,
    )
    cross = lax.all_to_all(cross, axes, 0, 0, tiled=True)
    high, low = lag_table(bins, per_dev, groups, 1.0 / (windows * n_day))
    return call(
        lags_kernel,
        jax.ShapeDtypeStruct((far, chans, width), jnp.float32),
        [
            pltpu.VMEM((width * (chans + 1), far), jnp.float32),
            pltpu.VMEM((chans, far, width), jnp.bfloat16),
            pltpu.VMEM((far, chans, width), jnp.float32),
            pltpu.SemaphoreType.DMA(SENDS),
        ],
        [pltpu.VMEM] * 3,
        pltpu.HBM,
        cross.reshape(width * chans, far),
        jnp.asarray(high),
        jnp.asarray(low),
    )


def solution(mesh):
    n_chan, n_day = mesh.shape["chan"], mesh.shape["day"]
    outer = 4 if n_chan % 4 == 0 else 1
    inner = n_chan // outer
    split_mesh = jax.sharding.Mesh(mesh.devices.reshape(outer, inner, n_day), ("outer", "inner", "day"))
    order = np.arange(n_chan * n_day).reshape(n_day, inner, outer).transpose(2, 1, 0).reshape(n_chan, n_day)

    def run(spectra):
        bins = spectra.shape[-1] // 2
        if bins % (n_chan * n_day):
            return jax.shard_map(
                gathered_shards,
                mesh=mesh,
                in_specs=(P("day", "chan", None, None),),
                out_specs=P("day", "chan", None),
                check_vma=False,
            )(spectra)
        return jax.shard_map(
            functools.partial(shards, ("day", "inner", "outer"), order),
            mesh=split_mesh,
            in_specs=(P("day", ("outer", "inner"), None, None),),
            out_specs=P("day", ("outer", "inner"), None),
            check_vma=False,
        )(spectra)

    return run
```

```python
import functools

import jax
import jax.numpy as jnp
import numpy as np
from jax import lax
from jax.experimental import pallas as pl
from jax.experimental.pallas import tpu as pltpu
from jax.sharding import PartitionSpec as P

VMEM_LIMIT = 48 * 1024 * 1024
PACK_VMEM_LIMIT = 53 * 1024 * 1024
FETCHES = 4
SENDS = 2


def freq_taper(bins):
    freq_index = jnp.arange(bins, dtype=jnp.float32)
    half_taper = 0.54 - 0.46 * jnp.cos(2.0 * jnp.pi * (freq_index + 0.5) / bins)
    return jnp.concatenate([half_taper, half_taper])


def whiten(spectra):
    values = spectra.astype(jnp.float32)
    bins = values.shape[-1] // 2
    band_power = jnp.sum(values * values, axis=-1, keepdims=True) / bins + 1e-06
    return (values * freq_taper(bins) / jnp.sqrt(band_power)).astype(jnp.bfloat16)


def lag_matrix(bins):
    lag_count = 2 * bins
    freq_index = jnp.arange(bins, dtype=jnp.int32)
    lag_index = jnp.arange(lag_count, dtype=jnp.int32) - bins
    wound = jnp.mod(freq_index[:, None] * lag_index[None, :], lag_count)
    phase_angle = 2.0 * jnp.pi / lag_count * wound.astype(jnp.float32)
    return jnp.concatenate([jnp.cos(phase_angle), -jnp.sin(phase_angle)], axis=0)


def cross_spectra(far_rows, near_rows):
    bins = far_rows.shape[-1] // 2
    windows = far_rows.shape[-2]
    far_re, far_im = (far_rows[..., :bins], far_rows[..., bins:])
    near_re, near_im = (near_rows[..., :bins], near_rows[..., bins:])
    real_part = jnp.einsum("jwf,iwf->jif", far_re, near_re, preferred_element_type=jnp.float32)
    real_part = real_part + jnp.einsum(
        "jwf,iwf->jif", far_im, near_im, preferred_element_type=jnp.float32
    )
    imag_part = jnp.einsum("jwf,iwf->jif", far_re, near_im, preferred_element_type=jnp.float32)
    imag_part = imag_part - jnp.einsum(
        "jwf,iwf->jif", far_im, near_re, preferred_element_type=jnp.float32
    )
    return jnp.concatenate([real_part, imag_part], axis=-1) / windows


def to_lags(cross, table):
    flat = cross.reshape(-1, cross.shape[-1])
    lagged = jnp.dot(
        flat, table, precision=lax.Precision.HIGHEST, preferred_element_type=jnp.float32
    )
    return lagged.reshape(cross.shape[:-1] + (table.shape[1],))


def gathered_shards(spectra):
    local_white = whiten(spectra)[0]
    gathered = lax.all_gather(local_white, "chan", axis=0, tiled=True)
    table = lag_matrix(local_white.shape[-1] // 2)
    day_count = lax.axis_size("day")
    return lax.psum_scatter(
        to_lags(cross_spectra(gathered, local_white), table) / day_count,
        "day",
        scatter_dimension=0,
        tiled=True,
    )


def lag_table(bins, per_dev, groups, scale):
    lags = 2 * bins
    freq = (np.arange(per_dev)[None, :] * groups + np.arange(groups)[:, None]).reshape(-1)
    wound = (freq[:, None] * (np.arange(lags)[None, :] - bins)) % lags
    angle = 2.0 * np.pi / lags * wound
    table = (np.stack([np.cos(angle), -np.sin(angle)], axis=1) * scale).reshape(2 * bins, lags)
    table = table.astype(np.float32)
    high = table.astype(jnp.bfloat16)
    low = (table - high.astype(np.float32)).astype(jnp.bfloat16)
    return high, low


def pack_kernel(groups, per_dev, spectra_ref, out_ref, held_ref, rows_ref, arrived):
    chans, windows, width = held_ref.shape
    bins = width // 2
    head = bins // 2
    size = (per_dev + 1) * chans
    stride = size + 1
    fetches = arrived.shape[0]
    batch = chans // fetches
    copies = []
    for step in range(fetches):
        part = pl.ds(step * batch, batch)
        copies.append(pltpu.make_async_copy(spectra_ref.at[part], held_ref.at[part], arrived.at[step]))
        copies[-1].start()
    freq = (lax.broadcasted_iota(jnp.int32, (1, width), 1) % bins).astype(jnp.float32)
    taper = 0.54 - 0.46 * jnp.cos(2.0 * jnp.pi * (freq + 0.5) / bins)
    lane = lax.broadcasted_iota(jnp.int32, (windows - head, bins), 1)
    pick = lax.broadcasted_iota(jnp.int32, (groups, bins), 1) % groups
    pick = (pick == lax.broadcasted_iota(jnp.int32, (groups, bins), 0)).astype(jnp.float32).astype(jnp.bfloat16)
    ones = jnp.ones((2 * width, bins), jnp.bfloat16)
    for ch in range(chans):
        if ch % batch == 0:
            copies[ch // batch].wait()
            values = held_ref[pl.ds(ch, batch)].astype(jnp.float32).reshape(batch * windows, width)
            square = values * values
            high = square.astype(jnp.bfloat16)
            low = (square - high.astype(jnp.float32)).astype(jnp.bfloat16)
            power = jnp.dot(jnp.concatenate([high, low], axis=1), ones, preferred_element_type=jnp.float32)
            scale = lax.rsqrt(power / bins + 1e-06)
            batch_white = (values * taper * jnp.concatenate([scale, scale], axis=1)).astype(jnp.bfloat16)
        white = batch_white[ch % batch * windows:(ch % batch + 1) * windows]
        real, imag = white[:, :bins], white[:, bins:]
        main = jnp.concatenate([real[:head], imag[:head]], axis=0).astype(jnp.float32).T
        spread = []
        for slot in range(per_dev):
            chosen = lane // groups == slot
            spread += [jnp.where(chosen, part[head:], jnp.zeros_like(part[head:])) for part in (real, imag)]
        tail = lax.dot_general(
            pick, jnp.concatenate(spread, axis=0), (((1,), (1,)), ((), ())), preferred_element_type=jnp.float32
        )
        for slot in range(per_dev):
            part = main[slot * groups:(slot + 1) * groups]
            rows_ref[pl.ds(slot * chans + ch, groups, stride=stride), :] = part
        rows_ref[pl.ds(per_dev * chans + ch, groups, stride=stride), :] = tail
    for group in range(groups):
        rows = rows_ref[pl.ds(group * stride, size), :]
        out_ref[group] = rows.astype(jnp.bfloat16).reshape(out_ref.shape[1:])


def swap_parts(rows, half):
    lanes = rows.shape[-1]
    values = rows.astype(jnp.float32)
    lane = lax.broadcasted_iota(jnp.int32, values.shape, 1)
    first = (lane % (2 * half)) < half
    ahead = pltpu.roll(values, lanes - half, 1)
    behind = pltpu.roll(values, half, 1)
    return jnp.where(first, ahead, -behind).astype(jnp.bfloat16)


def cross_kernel(order, days, in_ref, out_ref):
    groups, parts, chans, lanes = in_ref.shape
    blocks = groups // days
    per_dev = parts - 1
    total = blocks * chans
    far = out_ref.shape[-1]
    narrow = lanes // per_dev // 2

    def rows(day, part):
        return jnp.concatenate([in_ref[order[block][day], part] for block in range(blocks)], axis=0)

    tails = [rows(day, per_dev) for day in range(days)]
    tails_swapped = [swap_parts(tail, narrow) for tail in tails]
    far_tail = jnp.concatenate(tails, axis=1)
    lane = lax.broadcasted_iota(jnp.int32, (2 * total, lanes), 1) // (2 * narrow)
    dims = (((1,), (1,)), ((), ()))
    for slot in range(per_dev):
        mains = [rows(day, slot) for day in range(days)]
        far_main = jnp.concatenate(mains, axis=1)
        turned = [swap_parts(m, lanes // 2) for m in mains]
        near_main = [jnp.concatenate(pair, axis=0) for pair in zip(mains, turned)]
        near_tail = [jnp.concatenate(pair, axis=0) for pair in zip(tails, tails_swapped)]
        near_tail = [jnp.where(lane == slot, t, jnp.zeros_like(t)) for t in near_tail]
        cross = lax.dot_general(
            jnp.concatenate(near_main, axis=1), far_main, dims, preferred_element_type=jnp.float32
        ) + lax.dot_general(
            jnp.concatenate(near_tail, axis=1), far_tail, dims, preferred_element_type=jnp.float32
        )
        cross = cross.astype(out_ref.dtype)
        for kind in range(2):
            for block in range(blocks):
                start = kind * total + block * chans
                for half in range(days):
                    piece = cross[start:start + chans, half * far:(half + 1) * far]
                    out_ref[order[block][half], 2 * slot + kind] = piece


def lags_kernel(cross_ref, high_ref, low_ref, out_ref, rows_ref, flip_ref, lag_ref, sent):
    far, chans, _ = out_ref.shape
    depth = high_ref.shape[0]
    stride = chans + 1
    for row in range(depth):
        rows_ref[pl.ds(row * stride, chans), :] = cross_ref[pl.ds(row * chans, chans), :].astype(jnp.float32)
    table = jnp.concatenate([high_ref[...], low_ref[...]], axis=0)
    parts = sent.shape[0]
    batch = chans // parts
    copies = []
    for step in range(parts):
        group = range(step * batch, (step + 1) * batch)
        for ch in group:
            flip_ref[ch] = rows_ref[pl.ds(ch, depth, stride=stride), :].astype(jnp.bfloat16).T
        rows = flip_ref[pl.ds(step * batch, batch)].reshape(batch * far, depth)
        lag = jnp.dot(jnp.concatenate([rows, rows], axis=1), table, preferred_element_type=jnp.float32)
        for place, ch in enumerate(group):
            lag_ref[:, ch, :] = lag[place * far:(place + 1) * far]
        place = (slice(None), pl.ds(step * batch, batch))
        copies.append(pltpu.make_async_copy(lag_ref.at[place], out_ref.at[place], sent.at[step]))
        copies[-1].start()
    for copy in copies:
        copy.wait()


def call(kernel, out_shape, scratch, in_spaces, out_space, *operands, vmem=VMEM_LIMIT):
    return pl.pallas_call(
        kernel,
        out_shape=out_shape,
        in_specs=[pl.BlockSpec(memory_space=space) for space in in_spaces],
        out_specs=pl.BlockSpec(memory_space=out_space),
        scratch_shapes=scratch,
        compiler_params=pltpu.CompilerParams(vmem_limit_bytes=vmem),
    )(*operands)


def shards(axes, order, spectra):
    _, chans, windows, width = spectra.shape
    bins = width // 2
    n_chan, n_day = order.shape
    groups = n_chan * n_day
    per_dev = bins // groups
    far = n_chan * chans // n_day

    packed = call(
        functools.partial(pack_kernel, groups, per_dev),
        jax.ShapeDtypeStruct((groups, per_dev + 1, chans, bins), jnp.bfloat16),
        [
            pltpu.VMEM((chans, windows, width), jnp.bfloat16),
            pltpu.VMEM((groups * ((per_dev + 1) * chans + 1), bins), jnp.float32),
            pltpu.SemaphoreType.DMA((FETCHES,)),
        ],
        [pltpu.HBM],
        pltpu.VMEM,
        spectra[0],
        vmem=PACK_VMEM_LIMIT,
    )
    mine = lax.all_to_all(packed, axes, 0, 0, tiled=True)
    cross = call(
        functools.partial(cross_kernel, order.tolist(), n_day),
        jax.ShapeDtypeStruct((groups, 2 * per_dev, chans, far), jnp.bfloat16),
        [],
        [pltpu.VMEM],
        pltpu.VMEM,
        mine,
    )
    cross = lax.all_to_all(cross, axes, 0, 0, tiled=True)
    high, low = lag_table(bins, per_dev, groups, 1.0 / (windows * n_day))
    return call(
        lags_kernel,
        jax.ShapeDtypeStruct((far, chans, width), jnp.float32),
        [
            pltpu.VMEM((width * (chans + 1), far), jnp.float32),
            pltpu.VMEM((chans, far, width), jnp.bfloat16),
            pltpu.VMEM((far, chans, width), jnp.float32),
            pltpu.SemaphoreType.DMA((SENDS,)),
        ],
        [pltpu.VMEM] * 3,
        pltpu.HBM,
        cross.reshape(width * chans, far),
        jnp.asarray(high),
        jnp.asarray(low),
    )


def solution(mesh):
    n_chan, n_day = mesh.shape["chan"], mesh.shape["day"]
    outer = 4 if n_chan % 4 == 0 else 1
    inner = n_chan // outer
    split_mesh = jax.sharding.Mesh(mesh.devices.reshape(outer, inner, n_day), ("outer", "inner", "day"))
    order = np.arange(n_chan * n_day).reshape(n_day, inner, outer).transpose(2, 1, 0).reshape(n_chan, n_day)

    def run(spectra):
        bins = spectra.shape[-1] // 2
        if bins % (n_chan * n_day):
            return jax.shard_map(
                gathered_shards,
                mesh=mesh,
                in_specs=(P("day", "chan", None, None),),
                out_specs=P("day", "chan", None),
                check_vma=False,
            )(spectra)
        return jax.shard_map(
            functools.partial(shards, ("day", "inner", "outer"), order),
            mesh=split_mesh,
            in_specs=(P("day", ("outer", "inner"), None, None),),
            out_specs=P("day", ("outer", "inner"), None),
            check_vma=False,
        )(spectra)

    return run
```

```python
import functools

import jax
import jax.numpy as jnp
import numpy as np
from jax import lax
from jax.experimental import pallas as pl
from jax.experimental.pallas import tpu as pltpu
from jax.sharding import PartitionSpec as P

VMEM_LIMIT = 48 * 1024 * 1024
PACK_VMEM_LIMIT = 53 * 1024 * 1024
FETCHES = 4
SENDS = 2
TALL = 2


def freq_taper(bins):
    freq_index = jnp.arange(bins, dtype=jnp.float32)
    half_taper = 0.54 - 0.46 * jnp.cos(2.0 * jnp.pi * (freq_index + 0.5) / bins)
    return jnp.concatenate([half_taper, half_taper])


def whiten(spectra):
    values = spectra.astype(jnp.float32)
    bins = values.shape[-1] // 2
    band_power = jnp.sum(values * values, axis=-1, keepdims=True) / bins + 1e-06
    return (values * freq_taper(bins) / jnp.sqrt(band_power)).astype(jnp.bfloat16)


def lag_matrix(bins):
    lag_count = 2 * bins
    freq_index = jnp.arange(bins, dtype=jnp.int32)
    lag_index = jnp.arange(lag_count, dtype=jnp.int32) - bins
    wound = jnp.mod(freq_index[:, None] * lag_index[None, :], lag_count)
    phase_angle = 2.0 * jnp.pi / lag_count * wound.astype(jnp.float32)
    return jnp.concatenate([jnp.cos(phase_angle), -jnp.sin(phase_angle)], axis=0)


def cross_spectra(far_rows, near_rows):
    bins = far_rows.shape[-1] // 2
    windows = far_rows.shape[-2]
    far_re, far_im = (far_rows[..., :bins], far_rows[..., bins:])
    near_re, near_im = (near_rows[..., :bins], near_rows[..., bins:])
    real_part = jnp.einsum("jwf,iwf->jif", far_re, near_re, preferred_element_type=jnp.float32)
    real_part = real_part + jnp.einsum(
        "jwf,iwf->jif", far_im, near_im, preferred_element_type=jnp.float32
    )
    imag_part = jnp.einsum("jwf,iwf->jif", far_re, near_im, preferred_element_type=jnp.float32)
    imag_part = imag_part - jnp.einsum(
        "jwf,iwf->jif", far_im, near_re, preferred_element_type=jnp.float32
    )
    return jnp.concatenate([real_part, imag_part], axis=-1) / windows


def to_lags(cross, table):
    flat = cross.reshape(-1, cross.shape[-1])
    lagged = jnp.dot(
        flat, table, precision=lax.Precision.HIGHEST, preferred_element_type=jnp.float32
    )
    return lagged.reshape(cross.shape[:-1] + (table.shape[1],))


def gathered_shards(spectra):
    local_white = whiten(spectra)[0]
    gathered = lax.all_gather(local_white, "chan", axis=0, tiled=True)
    table = lag_matrix(local_white.shape[-1] // 2)
    day_count = lax.axis_size("day")
    return lax.psum_scatter(
        to_lags(cross_spectra(gathered, local_white), table) / day_count,
        "day",
        scatter_dimension=0,
        tiled=True,
    )


def lag_table(bins, per_dev, groups, scale):
    lags = 2 * bins
    freq = (np.arange(per_dev)[None, :] * groups + np.arange(groups)[:, None]).reshape(-1)
    wound = (freq[:, None] * (np.arange(lags)[None, :] - bins)) % lags
    angle = 2.0 * np.pi / lags * wound
    table = (np.stack([np.cos(angle), -np.sin(angle)], axis=1) * scale).reshape(2 * bins, lags)
    table = table.astype(np.float32)
    high = table.astype(jnp.bfloat16)
    low = (table - high.astype(np.float32)).astype(jnp.bfloat16)
    return high, low


def pack_kernel(groups, per_dev, spectra_ref, out_ref, held_ref, rows_ref, arrived):
    chans, windows, width = held_ref.shape
    bins = width // 2
    head = bins // 2
    size = (per_dev + 1) * chans
    stride = size + 1
    fetches = arrived.shape[0]
    batch = chans // fetches
    copies = []
    for step in range(fetches):
        part = pl.ds(step * batch, batch)
        copies.append(pltpu.make_async_copy(spectra_ref.at[part], held_ref.at[part], arrived.at[step]))
        copies[-1].start()
    freq = (lax.broadcasted_iota(jnp.int32, (1, width), 1) % bins).astype(jnp.float32)
    taper = 0.54 - 0.46 * jnp.cos(2.0 * jnp.pi * (freq + 0.5) / bins)
    lane = lax.broadcasted_iota(jnp.int32, (windows - head, bins), 1)
    pick = lax.broadcasted_iota(jnp.int32, (groups, bins), 1) % groups
    pick = (pick == lax.broadcasted_iota(jnp.int32, (groups, bins), 0)).astype(jnp.float32).astype(jnp.bfloat16)

    def whiten_channel(ch):
        values = held_ref[ch].astype(jnp.float32)
        power = jnp.sum(values * values, axis=-1, keepdims=True) / bins + 1e-06
        return (values * taper * lax.rsqrt(power)).astype(jnp.bfloat16)

    def place_channel(ch, white):
        real, imag = white[:, :bins], white[:, bins:]
        main = jnp.concatenate([real[:head], imag[:head]], axis=0).astype(jnp.float32).T
        spread = []
        for slot in range(per_dev):
            chosen = lane // groups == slot
            spread += [jnp.where(chosen, part[head:], jnp.zeros_like(part[head:])) for part in (real, imag)]
        tail = lax.dot_general(
            pick, jnp.concatenate(spread, axis=0), (((1,), (1,)), ((), ())), preferred_element_type=jnp.float32
        )
        for slot in range(per_dev):
            part = main[slot * groups:(slot + 1) * groups]
            rows_ref[pl.ds(slot * chans + ch, groups, stride=stride), :] = part
        rows_ref[pl.ds(per_dev * chans + ch, groups, stride=stride), :] = tail

    ready = []
    for step in range(fetches):
        copies[step].wait()
        fresh = [(ch, whiten_channel(ch)) for ch in range(step * batch, (step + 1) * batch)]
        for ch, white in ready:
            place_channel(ch, white)
        ready = fresh
    for ch, white in ready:
        place_channel(ch, white)
    for group in range(groups):
        rows = rows_ref[pl.ds(group * stride, size), :]
        out_ref[group] = rows.astype(jnp.bfloat16).reshape(out_ref.shape[1:])


def swap_parts(rows, half):
    lanes = rows.shape[-1]
    values = rows.astype(jnp.float32)
    lane = lax.broadcasted_iota(jnp.int32, values.shape, 1)
    first = (lane % (2 * half)) < half
    ahead = pltpu.roll(values, lanes - half, 1)
    behind = pltpu.roll(values, half, 1)
    return jnp.where(first, ahead, -behind).astype(jnp.bfloat16)


def cross_kernel(order, days, in_ref, out_ref):
    groups, parts, chans, lanes = in_ref.shape
    blocks = groups // days
    per_dev = parts - 1
    total = blocks * chans
    far = out_ref.shape[-1]
    narrow = lanes // per_dev // 2

    def rows(day, part):
        return jnp.concatenate([in_ref[order[block][day], part] for block in range(blocks)], axis=0)

    tails = [rows(day, per_dev) for day in range(days)]
    tails_swapped = [swap_parts(tail, narrow) for tail in tails]
    far_tail = jnp.concatenate(tails, axis=1)
    lane = lax.broadcasted_iota(jnp.int32, (2 * total, lanes), 1) // (2 * narrow)
    dims = (((1,), (1,)), ((), ()))
    for slot in range(per_dev):
        mains = [rows(day, slot) for day in range(days)]
        far_main = jnp.concatenate(mains, axis=1)
        turned = [swap_parts(m, lanes // 2) for m in mains]
        near_main = [jnp.concatenate(pair, axis=0) for pair in zip(mains, turned)]
        near_tail = [jnp.concatenate(pair, axis=0) for pair in zip(tails, tails_swapped)]
        near_tail = [jnp.where(lane == slot, t, jnp.zeros_like(t)) for t in near_tail]
        cross = lax.dot_general(
            jnp.concatenate(near_main, axis=1), far_main, dims, preferred_element_type=jnp.float32
        ) + lax.dot_general(
            jnp.concatenate(near_tail, axis=1), far_tail, dims, preferred_element_type=jnp.float32
        )
        cross = cross.astype(out_ref.dtype)
        for kind in range(2):
            for block in range(blocks):
                start = kind * total + block * chans
                for half in range(days):
                    piece = cross[start:start + chans, half * far:(half + 1) * far]
                    out_ref[order[block][half], 2 * slot + kind] = piece


def lags_kernel(cross_ref, high_ref, low_ref, out_ref, rows_ref, lag_ref, sent):
    far, chans, _ = out_ref.shape
    depth = high_ref.shape[0]
    stride = chans + 1
    for row in range(depth):
        rows_ref[pl.ds(row * stride, chans), :] = cross_ref[pl.ds(row * chans, chans), :].astype(jnp.float32)
    high, low = high_ref[...], low_ref[...]
    dims = (((0,), (0,)), ((), ()))
    parts = sent.shape[0]
    batch = chans // parts
    copies = []
    for step in range(parts):
        for first in range(step * batch, (step + 1) * batch, TALL):
            group = range(first, first + TALL)
            part = [rows_ref[pl.ds(ch, depth, stride=stride), :].astype(jnp.bfloat16) for ch in group]
            part = jnp.concatenate(part, axis=1)
            lag = lax.dot_general(part, high, dims, preferred_element_type=jnp.float32)
            lag = lag + lax.dot_general(part, low, dims, preferred_element_type=jnp.float32)
            for place, ch in enumerate(group):
                lag_ref[:, ch, :] = lag[place * far:(place + 1) * far]
        done = pl.ds(step * batch, batch)
        copies.append(pltpu.make_async_copy(lag_ref.at[:, done], out_ref.at[:, done], sent.at[step]))
        copies[-1].start()
    for copy in copies:
        copy.wait()


def call(kernel, out_shape, scratch, in_spaces, out_space, *operands, vmem=VMEM_LIMIT):
    return pl.pallas_call(
        kernel,
        out_shape=out_shape,
        in_specs=[pl.BlockSpec(memory_space=space) for space in in_spaces],
        out_specs=pl.BlockSpec(memory_space=out_space),
        scratch_shapes=scratch,
        compiler_params=pltpu.CompilerParams(vmem_limit_bytes=vmem),
    )(*operands)


def shards(axes, order, spectra):
    _, chans, windows, width = spectra.shape
    bins = width // 2
    n_chan, n_day = order.shape
    groups = n_chan * n_day
    per_dev = bins // groups
    far = n_chan * chans // n_day

    packed = call(
        functools.partial(pack_kernel, groups, per_dev),
        jax.ShapeDtypeStruct((groups, per_dev + 1, chans, bins), jnp.bfloat16),
        [
            pltpu.VMEM((chans, windows, width), jnp.bfloat16),
            pltpu.VMEM((groups * ((per_dev + 1) * chans + 1), bins), jnp.float32),
            pltpu.SemaphoreType.DMA((FETCHES,)),
        ],
        [pltpu.HBM],
        pltpu.VMEM,
        spectra[0],
        vmem=PACK_VMEM_LIMIT,
    )
    mine = lax.all_to_all(packed, axes, 0, 0, tiled=True)
    cross = call(
        functools.partial(cross_kernel, order.tolist(), n_day),
        jax.ShapeDtypeStruct((groups, 2 * per_dev, chans, far), jnp.bfloat16),
        [],
        [pltpu.VMEM],
        pltpu.VMEM,
        mine,
    )
    cross = lax.all_to_all(cross, axes, 0, 0, tiled=True)
    high, low = lag_table(bins, per_dev, groups, 1.0 / (windows * n_day))
    return call(
        lags_kernel,
        jax.ShapeDtypeStruct((far, chans, width), jnp.float32),
        [
            pltpu.VMEM((width * (chans + 1), far), jnp.float32),
            pltpu.VMEM((far, chans, width), jnp.float32),
            pltpu.SemaphoreType.DMA((SENDS,)),
        ],
        [pltpu.VMEM] * 3,
        pltpu.HBM,
        cross.reshape(width * chans, far),
        jnp.asarray(high),
        jnp.asarray(low),
    )


def solution(mesh):
    n_chan, n_day = mesh.shape["chan"], mesh.shape["day"]
    outer = 4 if n_chan % 4 == 0 else 1
    inner = n_chan // outer
    split_mesh = jax.sharding.Mesh(mesh.devices.reshape(outer, inner, n_day), ("outer", "inner", "day"))
    order = np.arange(n_chan * n_day).reshape(n_day, inner, outer).transpose(2, 1, 0).reshape(n_chan, n_day)

    def run(spectra):
        bins = spectra.shape[-1] // 2
        if bins % (n_chan * n_day):
            return jax.shard_map(
                gathered_shards,
                mesh=mesh,
                in_specs=(P("day", "chan", None, None),),
                out_specs=P("day", "chan", None),
                check_vma=False,
            )(spectra)
        return jax.shard_map(
            functools.partial(shards, ("day", "inner", "outer"), order),
            mesh=split_mesh,
            in_specs=(P("day", ("outer", "inner"), None, None),),
            out_specs=P("day", ("outer", "inner"), None),
            check_vma=False,
        )(spectra)

    return run
```

```python
import functools

import jax
import jax.numpy as jnp
import numpy as np
from jax import lax
from jax.experimental import pallas as pl
from jax.experimental.pallas import tpu as pltpu
from jax.sharding import PartitionSpec as P

VMEM_LIMIT = 48 * 1024 * 1024
PACK_VMEM_LIMIT = 53 * 1024 * 1024
FETCHES = 4
SENDS = 2


def freq_taper(bins):
    freq_index = jnp.arange(bins, dtype=jnp.float32)
    half_taper = 0.54 - 0.46 * jnp.cos(2.0 * jnp.pi * (freq_index + 0.5) / bins)
    return jnp.concatenate([half_taper, half_taper])


def whiten(spectra):
    values = spectra.astype(jnp.float32)
    bins = values.shape[-1] // 2
    band_power = jnp.sum(values * values, axis=-1, keepdims=True) / bins + 1e-06
    return (values * freq_taper(bins) / jnp.sqrt(band_power)).astype(jnp.bfloat16)


def lag_matrix(bins):
    lag_count = 2 * bins
    freq_index = jnp.arange(bins, dtype=jnp.int32)
    lag_index = jnp.arange(lag_count, dtype=jnp.int32) - bins
    wound = jnp.mod(freq_index[:, None] * lag_index[None, :], lag_count)
    phase_angle = 2.0 * jnp.pi / lag_count * wound.astype(jnp.float32)
    return jnp.concatenate([jnp.cos(phase_angle), -jnp.sin(phase_angle)], axis=0)


def cross_spectra(far_rows, near_rows):
    bins = far_rows.shape[-1] // 2
    windows = far_rows.shape[-2]
    far_re, far_im = (far_rows[..., :bins], far_rows[..., bins:])
    near_re, near_im = (near_rows[..., :bins], near_rows[..., bins:])
    real_part = jnp.einsum("jwf,iwf->jif", far_re, near_re, preferred_element_type=jnp.float32)
    real_part = real_part + jnp.einsum(
        "jwf,iwf->jif", far_im, near_im, preferred_element_type=jnp.float32
    )
    imag_part = jnp.einsum("jwf,iwf->jif", far_re, near_im, preferred_element_type=jnp.float32)
    imag_part = imag_part - jnp.einsum(
        "jwf,iwf->jif", far_im, near_re, preferred_element_type=jnp.float32
    )
    return jnp.concatenate([real_part, imag_part], axis=-1) / windows


def to_lags(cross, table):
    flat = cross.reshape(-1, cross.shape[-1])
    lagged = jnp.dot(
        flat, table, precision=lax.Precision.HIGHEST, preferred_element_type=jnp.float32
    )
    return lagged.reshape(cross.shape[:-1] + (table.shape[1],))


def gathered_shards(spectra):
    local_white = whiten(spectra)[0]
    gathered = lax.all_gather(local_white, "chan", axis=0, tiled=True)
    table = lag_matrix(local_white.shape[-1] // 2)
    day_count = lax.axis_size("day")
    return lax.psum_scatter(
        to_lags(cross_spectra(gathered, local_white), table) / day_count,
        "day",
        scatter_dimension=0,
        tiled=True,
    )


def lag_table(bins, per_dev, groups, scale):
    lags = 2 * bins
    freq = (np.arange(per_dev)[None, :] * groups + np.arange(groups)[:, None]).reshape(-1)
    wound = (freq[:, None] * (np.arange(lags)[None, :] - bins)) % lags
    angle = 2.0 * np.pi / lags * wound
    table = (np.stack([np.cos(angle), -np.sin(angle)], axis=1) * scale).reshape(2 * bins, lags)
    table = table.astype(np.float32)
    high = table.astype(jnp.bfloat16)
    low = (table - high.astype(np.float32)).astype(jnp.bfloat16)
    return high, low


def pack_kernel(groups, per_dev, spectra_ref, out_ref, held_ref, rows_ref, arrived):
    chans, windows, width = held_ref.shape
    bins = width // 2
    head = bins // 2
    size = (per_dev + 1) * chans
    stride = size + 1
    fetches = arrived.shape[0]
    batch = chans // fetches
    copies = []
    for step in range(fetches):
        part = pl.ds(step * batch, batch)
        copies.append(pltpu.make_async_copy(spectra_ref.at[part], held_ref.at[part], arrived.at[step]))
        copies[-1].start()
    freq = (lax.broadcasted_iota(jnp.int32, (1, width), 1) % bins).astype(jnp.float32)
    taper = 0.54 - 0.46 * jnp.cos(2.0 * jnp.pi * (freq + 0.5) / bins)
    lane = lax.broadcasted_iota(jnp.int32, (windows - head, bins), 1)
    pick = lax.broadcasted_iota(jnp.int32, (groups, bins), 1) % groups
    pick = (pick == lax.broadcasted_iota(jnp.int32, (groups, bins), 0)).astype(jnp.float32).astype(jnp.bfloat16)

    def whiten_channel(ch):
        values = held_ref[ch].astype(jnp.float32)
        power = jnp.sum(values * values, axis=-1, keepdims=True) / bins + 1e-06
        return (values * taper * lax.rsqrt(power)).astype(jnp.bfloat16)

    def place_channel(ch, white):
        real, imag = white[:, :bins], white[:, bins:]
        main = jnp.concatenate([real[:head], imag[:head]], axis=0).astype(jnp.float32).T
        spread = []
        for slot in range(per_dev):
            chosen = lane // groups == slot
            spread += [jnp.where(chosen, part[head:], jnp.zeros_like(part[head:])) for part in (real, imag)]
        tail = lax.dot_general(
            pick, jnp.concatenate(spread, axis=0), (((1,), (1,)), ((), ())), preferred_element_type=jnp.float32
        )
        for slot in range(per_dev):
            part = main[slot * groups:(slot + 1) * groups]
            rows_ref[pl.ds(slot * chans + ch, groups, stride=stride), :] = part
        rows_ref[pl.ds(per_dev * chans + ch, groups, stride=stride), :] = tail

    ready = []
    for step in range(fetches):
        copies[step].wait()
        fresh = [(ch, whiten_channel(ch)) for ch in range(step * batch, (step + 1) * batch)]
        for ch, white in ready:
            place_channel(ch, white)
        ready = fresh
    for ch, white in ready:
        place_channel(ch, white)
    for group in range(groups):
        rows = rows_ref[pl.ds(group * stride, size), :]
        out_ref[group] = rows.astype(jnp.bfloat16).reshape(out_ref.shape[1:])


def swap_parts(rows, half):
    lanes = rows.shape[-1]
    values = rows.astype(jnp.float32)
    lane = lax.broadcasted_iota(jnp.int32, values.shape, 1)
    first = (lane % (2 * half)) < half
    ahead = pltpu.roll(values, lanes - half, 1)
    behind = pltpu.roll(values, half, 1)
    return jnp.where(first, ahead, -behind).astype(jnp.bfloat16)


def cross_kernel(order, days, in_ref, out_ref):
    groups, parts, chans, lanes = in_ref.shape
    blocks = groups // days
    per_dev = parts - 1
    total = blocks * chans
    far = out_ref.shape[-1]
    narrow = lanes // per_dev // 2

    def rows(day, part):
        return jnp.concatenate([in_ref[order[block][day], part] for block in range(blocks)], axis=0)

    tails = [rows(day, per_dev) for day in range(days)]
    tails_swapped = [swap_parts(tail, narrow) for tail in tails]
    far_tail = jnp.concatenate(tails, axis=1)
    lane = lax.broadcasted_iota(jnp.int32, (2 * total, lanes), 1) // (2 * narrow)
    dims = (((1,), (1,)), ((), ()))
    for slot in range(per_dev):
        mains = [rows(day, slot) for day in range(days)]
        far_main = jnp.concatenate(mains, axis=1)
        turned = [swap_parts(m, lanes // 2) for m in mains]
        near_main = [jnp.concatenate(pair, axis=0) for pair in zip(mains, turned)]
        near_tail = [jnp.concatenate(pair, axis=0) for pair in zip(tails, tails_swapped)]
        near_tail = [jnp.where(lane == slot, t, jnp.zeros_like(t)) for t in near_tail]
        cross = lax.dot_general(
            jnp.concatenate(near_main, axis=1), far_main, dims, preferred_element_type=jnp.float32
        ) + lax.dot_general(
            jnp.concatenate(near_tail, axis=1), far_tail, dims, preferred_element_type=jnp.float32
        )
        cross = cross.astype(out_ref.dtype)
        for kind in range(2):
            for block in range(blocks):
                start = kind * total + block * chans
                for half in range(days):
                    piece = cross[start:start + chans, half * far:(half + 1) * far]
                    out_ref[order[block][half], 2 * slot + kind] = piece


def lags_kernel(cross_ref, high_ref, low_ref, out_ref, rows_ref, lag_ref, sent):
    chans = out_ref.shape[1]
    depth = high_ref.shape[0]
    high, low = high_ref[...], low_ref[...]
    dims = (((0,), (0,)), ((), ()))
    parts = sent.shape[0]
    batch = chans // parts
    stride = batch + 1
    share = depth // batch

    def fill(step, rows):
        for row in rows:
            values = cross_ref[pl.ds(row * chans, chans), :].astype(jnp.float32)
            rows_ref[step, pl.ds(row * stride, batch), :] = values[step * batch:(step + 1) * batch]

    fill(0, range(depth))
    copies = []
    for step in range(parts):
        for place in range(batch):
            part = rows_ref[step, pl.ds(place, depth, stride=stride), :].astype(jnp.bfloat16)
            if step + 1 < parts:
                fill(step + 1, range(place * share, (place + 1) * share))
            lag = lax.dot_general(part, high, dims, preferred_element_type=jnp.float32)
            lag = lag + lax.dot_general(part, low, dims, preferred_element_type=jnp.float32)
            lag_ref[:, step * batch + place, :] = lag
        done = pl.ds(step * batch, batch)
        copies.append(pltpu.make_async_copy(lag_ref.at[:, done], out_ref.at[:, done], sent.at[step]))
        copies[-1].start()
    for copy in copies:
        copy.wait()


def call(kernel, out_shape, scratch, in_spaces, out_space, *operands, vmem=VMEM_LIMIT):
    return pl.pallas_call(
        kernel,
        out_shape=out_shape,
        in_specs=[pl.BlockSpec(memory_space=space) for space in in_spaces],
        out_specs=pl.BlockSpec(memory_space=out_space),
        scratch_shapes=scratch,
        compiler_params=pltpu.CompilerParams(vmem_limit_bytes=vmem),
    )(*operands)


def shards(axes, order, spectra):
    _, chans, windows, width = spectra.shape
    bins = width // 2
    n_chan, n_day = order.shape
    groups = n_chan * n_day
    per_dev = bins // groups
    far = n_chan * chans // n_day

    packed = call(
        functools.partial(pack_kernel, groups, per_dev),
        jax.ShapeDtypeStruct((groups, per_dev + 1, chans, bins), jnp.bfloat16),
        [
            pltpu.VMEM((chans, windows, width), jnp.bfloat16),
            pltpu.VMEM((groups * ((per_dev + 1) * chans + 1), bins), jnp.float32),
            pltpu.SemaphoreType.DMA((FETCHES,)),
        ],
        [pltpu.HBM],
        pltpu.VMEM,
        spectra[0],
        vmem=PACK_VMEM_LIMIT,
    )
    mine = lax.all_to_all(packed, axes, 0, 0, tiled=True)
    cross = call(
        functools.partial(cross_kernel, order.tolist(), n_day),
        jax.ShapeDtypeStruct((groups, 2 * per_dev, chans, far), jnp.bfloat16),
        [],
        [pltpu.VMEM],
        pltpu.VMEM,
        mine,
    )
    cross = lax.all_to_all(cross, axes, 0, 0, tiled=True)
    high, low = lag_table(bins, per_dev, groups, 1.0 / (windows * n_day))
    return call(
        lags_kernel,
        jax.ShapeDtypeStruct((far, chans, width), jnp.float32),
        [
            pltpu.VMEM((SENDS, width * (chans // SENDS + 1), far), jnp.float32),
            pltpu.VMEM((far, chans, width), jnp.float32),
            pltpu.SemaphoreType.DMA((SENDS,)),
        ],
        [pltpu.VMEM] * 3,
        pltpu.HBM,
        cross.reshape(width * chans, far),
        jnp.asarray(high),
        jnp.asarray(low),
    )


def solution(mesh):
    n_chan, n_day = mesh.shape["chan"], mesh.shape["day"]
    outer = 4 if n_chan % 4 == 0 else 1
    inner = n_chan // outer
    split_mesh = jax.sharding.Mesh(mesh.devices.reshape(outer, inner, n_day), ("outer", "inner", "day"))
    order = np.arange(n_chan * n_day).reshape(n_day, inner, outer).transpose(2, 1, 0).reshape(n_chan, n_day)

    def run(spectra):
        bins = spectra.shape[-1] // 2
        if bins % (n_chan * n_day):
            return jax.shard_map(
                gathered_shards,
                mesh=mesh,
                in_specs=(P("day", "chan", None, None),),
                out_specs=P("day", "chan", None),
                check_vma=False,
            )(spectra)
        return jax.shard_map(
            functools.partial(shards, ("day", "inner", "outer"), order),
            mesh=split_mesh,
            in_specs=(P("day", ("outer", "inner"), None, None),),
            out_specs=P("day", ("outer", "inner"), None),
            check_vma=False,
        )(spectra)

    return run
```

```python
import functools

import jax
import jax.numpy as jnp
import numpy as np
from jax import lax
from jax.experimental import pallas as pl
from jax.experimental.pallas import tpu as pltpu
from jax.sharding import PartitionSpec as P

VMEM_LIMIT = 48 * 1024 * 1024
PACK_VMEM_LIMIT = 53 * 1024 * 1024
FETCHES = 8
SENDS = 2


def freq_taper(bins):
    freq_index = jnp.arange(bins, dtype=jnp.float32)
    half_taper = 0.54 - 0.46 * jnp.cos(2.0 * jnp.pi * (freq_index + 0.5) / bins)
    return jnp.concatenate([half_taper, half_taper])


def whiten(spectra):
    values = spectra.astype(jnp.float32)
    bins = values.shape[-1] // 2
    band_power = jnp.sum(values * values, axis=-1, keepdims=True) / bins + 1e-06
    return (values * freq_taper(bins) / jnp.sqrt(band_power)).astype(jnp.bfloat16)


def lag_matrix(bins):
    lag_count = 2 * bins
    freq_index = jnp.arange(bins, dtype=jnp.int32)
    lag_index = jnp.arange(lag_count, dtype=jnp.int32) - bins
    wound = jnp.mod(freq_index[:, None] * lag_index[None, :], lag_count)
    phase_angle = 2.0 * jnp.pi / lag_count * wound.astype(jnp.float32)
    return jnp.concatenate([jnp.cos(phase_angle), -jnp.sin(phase_angle)], axis=0)


def cross_spectra(far_rows, near_rows):
    bins = far_rows.shape[-1] // 2
    windows = far_rows.shape[-2]
    far_re, far_im = (far_rows[..., :bins], far_rows[..., bins:])
    near_re, near_im = (near_rows[..., :bins], near_rows[..., bins:])
    real_part = jnp.einsum("jwf,iwf->jif", far_re, near_re, preferred_element_type=jnp.float32)
    real_part = real_part + jnp.einsum(
        "jwf,iwf->jif", far_im, near_im, preferred_element_type=jnp.float32
    )
    imag_part = jnp.einsum("jwf,iwf->jif", far_re, near_im, preferred_element_type=jnp.float32)
    imag_part = imag_part - jnp.einsum(
        "jwf,iwf->jif", far_im, near_re, preferred_element_type=jnp.float32
    )
    return jnp.concatenate([real_part, imag_part], axis=-1) / windows


def to_lags(cross, table):
    flat = cross.reshape(-1, cross.shape[-1])
    lagged = jnp.dot(
        flat, table, precision=lax.Precision.HIGHEST, preferred_element_type=jnp.float32
    )
    return lagged.reshape(cross.shape[:-1] + (table.shape[1],))


def gathered_shards(spectra):
    local_white = whiten(spectra)[0]
    gathered = lax.all_gather(local_white, "chan", axis=0, tiled=True)
    table = lag_matrix(local_white.shape[-1] // 2)
    day_count = lax.axis_size("day")
    return lax.psum_scatter(
        to_lags(cross_spectra(gathered, local_white), table) / day_count,
        "day",
        scatter_dimension=0,
        tiled=True,
    )


def lag_table(bins, per_dev, groups, scale):
    lags = 2 * bins
    freq = (np.arange(per_dev)[None, :] * groups + np.arange(groups)[:, None]).reshape(-1)
    wound = (freq[:, None] * (np.arange(lags)[None, :] - bins)) % lags
    angle = 2.0 * np.pi / lags * wound
    table = (np.stack([np.cos(angle), -np.sin(angle)], axis=1) * scale).reshape(2 * bins, lags)
    table = table.astype(np.float32)
    high = table.astype(jnp.bfloat16)
    low = (table - high.astype(np.float32)).astype(jnp.bfloat16)
    return high, low


def pack_kernel(groups, per_dev, spectra_ref, out_ref, held_ref, rows_ref, arrived):
    chans, windows, width = held_ref.shape
    bins = width // 2
    head = bins // 2
    size = (per_dev + 1) * chans
    stride = size + 1
    fetches = arrived.shape[0]
    batch = chans // fetches
    copies = []
    for step in range(fetches):
        part = pl.ds(step * batch, batch)
        copies.append(pltpu.make_async_copy(spectra_ref.at[part], held_ref.at[part], arrived.at[step]))
        copies[-1].start()
    freq = (lax.broadcasted_iota(jnp.int32, (1, width), 1) % bins).astype(jnp.float32)
    taper = 0.54 - 0.46 * jnp.cos(2.0 * jnp.pi * (freq + 0.5) / bins)
    lane = lax.broadcasted_iota(jnp.int32, (windows - head, bins), 1)
    pick = lax.broadcasted_iota(jnp.int32, (groups, bins), 1) % groups
    pick = (pick == lax.broadcasted_iota(jnp.int32, (groups, bins), 0)).astype(jnp.float32).astype(jnp.bfloat16)

    def whiten_channel(ch):
        values = held_ref[ch].astype(jnp.float32)
        power = jnp.sum(values * values, axis=-1, keepdims=True) / bins + 1e-06
        return (values * taper * lax.rsqrt(power)).astype(jnp.bfloat16)

    def place_channel(ch, white):
        real, imag = white[:, :bins], white[:, bins:]
        main = jnp.concatenate([real[:head], imag[:head]], axis=0).astype(jnp.float32).T
        spread = []
        for slot in range(per_dev):
            chosen = lane // groups == slot
            spread += [jnp.where(chosen, part[head:], jnp.zeros_like(part[head:])) for part in (real, imag)]
        tail = lax.dot_general(
            pick, jnp.concatenate(spread, axis=0), (((1,), (1,)), ((), ())), preferred_element_type=jnp.float32
        )
        for slot in range(per_dev):
            part = main[slot * groups:(slot + 1) * groups]
            rows_ref[pl.ds(slot * chans + ch, groups, stride=stride), :] = part
        rows_ref[pl.ds(per_dev * chans + ch, groups, stride=stride), :] = tail

    ready = []
    for step in range(fetches):
        copies[step].wait()
        fresh = [(ch, whiten_channel(ch)) for ch in range(step * batch, (step + 1) * batch)]
        for ch, white in ready:
            place_channel(ch, white)
        ready = fresh
    for ch, white in ready:
        place_channel(ch, white)
    for group in range(groups):
        rows = rows_ref[pl.ds(group * stride, size), :]
        out_ref[group] = rows.astype(jnp.bfloat16).reshape(out_ref.shape[1:])


def swap_parts(rows, half):
    lanes = rows.shape[-1]
    values = rows.astype(jnp.float32)
    lane = lax.broadcasted_iota(jnp.int32, values.shape, 1)
    first = (lane % (2 * half)) < half
    ahead = pltpu.roll(values, lanes - half, 1)
    behind = pltpu.roll(values, half, 1)
    return jnp.where(first, ahead, -behind).astype(jnp.bfloat16)


def cross_kernel(order, days, in_ref, out_ref):
    groups, parts, chans, lanes = in_ref.shape
    blocks = groups // days
    per_dev = parts - 1
    total = blocks * chans
    far = out_ref.shape[-1]
    narrow = lanes // per_dev // 2

    def rows(day, part):
        return jnp.concatenate([in_ref[order[block][day], part] for block in range(blocks)], axis=0)

    tails = [rows(day, per_dev) for day in range(days)]
    tails_swapped = [swap_parts(tail, narrow) for tail in tails]
    far_tail = jnp.concatenate(tails, axis=1)
    lane = lax.broadcasted_iota(jnp.int32, (2 * total, lanes), 1) // (2 * narrow)
    dims = (((1,), (1,)), ((), ()))
    for slot in range(per_dev):
        mains = [rows(day, slot) for day in range(days)]
        far_main = jnp.concatenate(mains, axis=1)
        turned = [swap_parts(m, lanes // 2) for m in mains]
        near_main = [jnp.concatenate(pair, axis=0) for pair in zip(mains, turned)]
        near_tail = [jnp.concatenate(pair, axis=0) for pair in zip(tails, tails_swapped)]
        near_tail = [jnp.where(lane == slot, t, jnp.zeros_like(t)) for t in near_tail]
        cross = lax.dot_general(
            jnp.concatenate(near_main, axis=1), far_main, dims, preferred_element_type=jnp.float32
        ) + lax.dot_general(
            jnp.concatenate(near_tail, axis=1), far_tail, dims, preferred_element_type=jnp.float32
        )
        cross = cross.astype(out_ref.dtype)
        for kind in range(2):
            for block in range(blocks):
                start = kind * total + block * chans
                for half in range(days):
                    piece = cross[start:start + chans, half * far:(half + 1) * far]
                    out_ref[order[block][half], 2 * slot + kind] = piece


def lags_kernel(cross_ref, high_ref, low_ref, out_ref, rows_ref, lag_ref, sent):
    chans = out_ref.shape[1]
    depth = high_ref.shape[0]
    high, low = high_ref[...], low_ref[...]
    far = cross_ref.shape[-1]
    same = lax.broadcasted_iota(jnp.int32, (far, far), 0) == lax.broadcasted_iota(jnp.int32, (far, far), 1)
    same = same.astype(jnp.float32).astype(jnp.bfloat16)
    dims = (((1,), (1,)), ((), ()))
    parts = sent.shape[0]
    batch = chans // parts
    stride = batch + 1
    share = depth // batch

    def fill(step, rows):
        for row in rows:
            values = cross_ref[pl.ds(row * chans, chans), :].astype(jnp.float32)
            rows_ref[step, pl.ds(row * stride, batch), :] = values[step * batch:(step + 1) * batch]

    fill(0, range(depth))
    copies = []
    for step in range(parts):
        for place in range(batch):
            part = rows_ref[step, pl.ds(place, depth, stride=stride), :].astype(jnp.bfloat16)
            if step + 1 < parts:
                fill(step + 1, range(place * share, (place + 1) * share))
            part = lax.dot_general(same, part, dims, preferred_element_type=jnp.float32).astype(jnp.bfloat16)
            lag = jnp.dot(part, high, preferred_element_type=jnp.float32)
            lag = lag + jnp.dot(part, low, preferred_element_type=jnp.float32)
            lag_ref[:, step * batch + place, :] = lag
        done = pl.ds(step * batch, batch)
        copies.append(pltpu.make_async_copy(lag_ref.at[:, done], out_ref.at[:, done], sent.at[step]))
        copies[-1].start()
    for copy in copies:
        copy.wait()


def call(kernel, out_shape, scratch, in_spaces, out_space, *operands, vmem=VMEM_LIMIT):
    return pl.pallas_call(
        kernel,
        out_shape=out_shape,
        in_specs=[pl.BlockSpec(memory_space=space) for space in in_spaces],
        out_specs=pl.BlockSpec(memory_space=out_space),
        scratch_shapes=scratch,
        compiler_params=pltpu.CompilerParams(vmem_limit_bytes=vmem),
    )(*operands)


def shards(axes, order, spectra):
    _, chans, windows, width = spectra.shape
    bins = width // 2
    n_chan, n_day = order.shape
    groups = n_chan * n_day
    per_dev = bins // groups
    far = n_chan * chans // n_day

    packed = call(
        functools.partial(pack_kernel, groups, per_dev),
        jax.ShapeDtypeStruct((groups, per_dev + 1, chans, bins), jnp.bfloat16),
        [
            pltpu.VMEM((chans, windows, width), jnp.bfloat16),
            pltpu.VMEM((groups * ((per_dev + 1) * chans + 1), bins), jnp.float32),
            pltpu.SemaphoreType.DMA((FETCHES,)),
        ],
        [pltpu.HBM],
        pltpu.VMEM,
        spectra[0],
        vmem=PACK_VMEM_LIMIT,
    )
    mine = lax.all_to_all(packed, axes, 0, 0, tiled=True)
    cross = call(
        functools.partial(cross_kernel, order.tolist(), n_day),
        jax.ShapeDtypeStruct((groups, 2 * per_dev, chans, far), jnp.bfloat16),
        [],
        [pltpu.VMEM],
        pltpu.VMEM,
        mine,
    )
    cross = lax.all_to_all(cross, axes, 0, 0, tiled=True)
    high, low = lag_table(bins, per_dev, groups, 1.0 / (windows * n_day))
    return call(
        lags_kernel,
        jax.ShapeDtypeStruct((far, chans, width), jnp.float32),
        [
            pltpu.VMEM((SENDS, width * (chans // SENDS + 1), far), jnp.float32),
            pltpu.VMEM((far, chans, width), jnp.float32),
            pltpu.SemaphoreType.DMA((SENDS,)),
        ],
        [pltpu.VMEM] * 3,
        pltpu.HBM,
        cross.reshape(width * chans, far),
        jnp.asarray(high),
        jnp.asarray(low),
    )


def solution(mesh):
    n_chan, n_day = mesh.shape["chan"], mesh.shape["day"]
    outer = 4 if n_chan % 4 == 0 else 1
    inner = n_chan // outer
    split_mesh = jax.sharding.Mesh(mesh.devices.reshape(outer, inner, n_day), ("outer", "inner", "day"))
    order = np.arange(n_chan * n_day).reshape(n_day, inner, outer).transpose(2, 1, 0).reshape(n_chan, n_day)

    def run(spectra):
        bins = spectra.shape[-1] // 2
        if bins % (n_chan * n_day):
            return jax.shard_map(
                gathered_shards,
                mesh=mesh,
                in_specs=(P("day", "chan", None, None),),
                out_specs=P("day", "chan", None),
                check_vma=False,
            )(spectra)
        return jax.shard_map(
            functools.partial(shards, ("day", "inner", "outer"), order),
            mesh=split_mesh,
            in_specs=(P("day", ("outer", "inner"), None, None),),
            out_specs=P("day", ("outer", "inner"), None),
            check_vma=False,
        )(spectra)

    return run
```

```python
import functools

import jax
import jax.numpy as jnp
import numpy as np
from jax import lax
from jax.experimental import pallas as pl
from jax.experimental.pallas import tpu as pltpu
from jax.sharding import PartitionSpec as P

VMEM_LIMIT = 48 * 1024 * 1024
PACK_VMEM_LIMIT = 53 * 1024 * 1024
FETCHES = 2
SENDS = 2


def freq_taper(bins):
    freq_index = jnp.arange(bins, dtype=jnp.float32)
    half_taper = 0.54 - 0.46 * jnp.cos(2.0 * jnp.pi * (freq_index + 0.5) / bins)
    return jnp.concatenate([half_taper, half_taper])


def whiten(spectra):
    values = spectra.astype(jnp.float32)
    bins = values.shape[-1] // 2
    band_power = jnp.sum(values * values, axis=-1, keepdims=True) / bins + 1e-06
    return (values * freq_taper(bins) / jnp.sqrt(band_power)).astype(jnp.bfloat16)


def lag_matrix(bins):
    lag_count = 2 * bins
    freq_index = jnp.arange(bins, dtype=jnp.int32)
    lag_index = jnp.arange(lag_count, dtype=jnp.int32) - bins
    wound = jnp.mod(freq_index[:, None] * lag_index[None, :], lag_count)
    phase_angle = 2.0 * jnp.pi / lag_count * wound.astype(jnp.float32)
    return jnp.concatenate([jnp.cos(phase_angle), -jnp.sin(phase_angle)], axis=0)


def cross_spectra(far_rows, near_rows):
    bins = far_rows.shape[-1] // 2
    windows = far_rows.shape[-2]
    far_re, far_im = (far_rows[..., :bins], far_rows[..., bins:])
    near_re, near_im = (near_rows[..., :bins], near_rows[..., bins:])
    real_part = jnp.einsum("jwf,iwf->jif", far_re, near_re, preferred_element_type=jnp.float32)
    real_part = real_part + jnp.einsum(
        "jwf,iwf->jif", far_im, near_im, preferred_element_type=jnp.float32
    )
    imag_part = jnp.einsum("jwf,iwf->jif", far_re, near_im, preferred_element_type=jnp.float32)
    imag_part = imag_part - jnp.einsum(
        "jwf,iwf->jif", far_im, near_re, preferred_element_type=jnp.float32
    )
    return jnp.concatenate([real_part, imag_part], axis=-1) / windows


def to_lags(cross, table):
    flat = cross.reshape(-1, cross.shape[-1])
    lagged = jnp.dot(
        flat, table, precision=lax.Precision.HIGHEST, preferred_element_type=jnp.float32
    )
    return lagged.reshape(cross.shape[:-1] + (table.shape[1],))


def gathered_shards(spectra):
    local_white = whiten(spectra)[0]
    gathered = lax.all_gather(local_white, "chan", axis=0, tiled=True)
    table = lag_matrix(local_white.shape[-1] // 2)
    day_count = lax.axis_size("day")
    return lax.psum_scatter(
        to_lags(cross_spectra(gathered, local_white), table) / day_count,
        "day",
        scatter_dimension=0,
        tiled=True,
    )


def lag_table(bins, per_dev, groups, scale):
    lags = 2 * bins
    freq = (np.arange(per_dev)[None, :] * groups + np.arange(groups)[:, None]).reshape(-1)
    wound = (freq[:, None] * (np.arange(lags)[None, :] - bins)) % lags
    angle = 2.0 * np.pi / lags * wound
    table = (np.stack([np.cos(angle), -np.sin(angle)], axis=1) * scale).reshape(2 * bins, lags)
    table = table.astype(np.float32)
    high = table.astype(jnp.bfloat16)
    low = (table - high.astype(np.float32)).astype(jnp.bfloat16)
    return high, low


def pack_kernel(groups, per_dev, spectra_ref, out_ref, held_ref, rows_ref, arrived):
    chans, windows, width = held_ref.shape
    bins = width // 2
    head = bins // 2
    size = (per_dev + 1) * chans
    stride = size + 1
    fetches = arrived.shape[0]
    batch = chans // fetches
    copies = []
    for step in range(fetches):
        part = pl.ds(step * batch, batch)
        copies.append(pltpu.make_async_copy(spectra_ref.at[part], held_ref.at[part], arrived.at[step]))
        copies[-1].start()
    freq = (lax.broadcasted_iota(jnp.int32, (1, width), 1) % bins).astype(jnp.float32)
    taper = 0.54 - 0.46 * jnp.cos(2.0 * jnp.pi * (freq + 0.5) / bins)
    lane = lax.broadcasted_iota(jnp.int32, (windows - head, bins), 1)
    pick = lax.broadcasted_iota(jnp.int32, (groups, bins), 1) % groups
    pick = (pick == lax.broadcasted_iota(jnp.int32, (groups, bins), 0)).astype(jnp.float32).astype(jnp.bfloat16)

    def whiten_channel(ch):
        values = held_ref[ch].astype(jnp.float32)
        power = jnp.sum(values * values, axis=-1, keepdims=True) / bins + 1e-06
        return (values * taper * lax.rsqrt(power)).astype(jnp.bfloat16)

    def place_channel(ch, white):
        real, imag = white[:, :bins], white[:, bins:]
        main = jnp.concatenate([real[:head], imag[:head]], axis=0).astype(jnp.float32).T
        spread = []
        for slot in range(per_dev):
            chosen = lane // groups == slot
            spread += [jnp.where(chosen, part[head:], jnp.zeros_like(part[head:])) for part in (real, imag)]
        tail = lax.dot_general(
            pick, jnp.concatenate(spread, axis=0), (((1,), (1,)), ((), ())), preferred_element_type=jnp.float32
        )
        for slot in range(per_dev):
            part = main[slot * groups:(slot + 1) * groups]
            rows_ref[pl.ds(slot * chans + ch, groups, stride=stride), :] = part
        rows_ref[pl.ds(per_dev * chans + ch, groups, stride=stride), :] = tail

    ready = []
    for step in range(fetches):
        copies[step].wait()
        fresh = [(ch, whiten_channel(ch)) for ch in range(step * batch, (step + 1) * batch)]
        for ch, white in ready:
            place_channel(ch, white)
        ready = fresh
    for ch, white in ready:
        place_channel(ch, white)
    for first in range(0, groups, 4):
        rows = [rows_ref[pl.ds(group * stride, size), :].astype(jnp.bfloat16) for group in range(first, first + 4)]
        for place, part in enumerate(rows):
            out_ref[first + place] = part.reshape(out_ref.shape[1:])


def swap_parts(rows, half):
    lanes = rows.shape[-1]
    values = rows.astype(jnp.float32)
    lane = lax.broadcasted_iota(jnp.int32, values.shape, 1)
    first = (lane % (2 * half)) < half
    ahead = pltpu.roll(values, lanes - half, 1)
    behind = pltpu.roll(values, half, 1)
    return jnp.where(first, ahead, -behind).astype(jnp.bfloat16)


def cross_kernel(order, days, in_ref, out_ref):
    groups, parts, chans, lanes = in_ref.shape
    blocks = groups // days
    per_dev = parts - 1
    total = blocks * chans
    far = out_ref.shape[-1]
    narrow = lanes // per_dev // 2

    def rows(day, part):
        return jnp.concatenate([in_ref[order[block][day], part] for block in range(blocks)], axis=0)

    tails = [rows(day, per_dev) for day in range(days)]
    tails_swapped = [swap_parts(tail, narrow) for tail in tails]
    far_tail = jnp.concatenate(tails, axis=1)
    lane = lax.broadcasted_iota(jnp.int32, (2 * total, lanes), 1) // (2 * narrow)
    dims = (((1,), (1,)), ((), ()))
    for slot in range(per_dev):
        mains = [rows(day, slot) for day in range(days)]
        far_main = jnp.concatenate(mains, axis=1)
        turned = [swap_parts(m, lanes // 2) for m in mains]
        near_main = [jnp.concatenate(pair, axis=0) for pair in zip(mains, turned)]
        near_tail = [jnp.concatenate(pair, axis=0) for pair in zip(tails, tails_swapped)]
        near_tail = [jnp.where(lane == slot, t, jnp.zeros_like(t)) for t in near_tail]
        cross = lax.dot_general(
            jnp.concatenate(near_main, axis=1), far_main, dims, preferred_element_type=jnp.float32
        ) + lax.dot_general(
            jnp.concatenate(near_tail, axis=1), far_tail, dims, preferred_element_type=jnp.float32
        )
        cross = cross.astype(out_ref.dtype)
        for kind in range(2):
            for block in range(blocks):
                start = kind * total + block * chans
                for half in range(days):
                    piece = cross[start:start + chans, half * far:(half + 1) * far]
                    out_ref[order[block][half], 2 * slot + kind] = piece


def lags_kernel(cross_ref, high_ref, low_ref, out_ref, rows_ref, lag_ref, sent):
    chans = out_ref.shape[1]
    depth = high_ref.shape[0]
    high, low = high_ref[...], low_ref[...]
    dims = (((0,), (0,)), ((), ()))
    parts = sent.shape[0]
    batch = chans // parts
    stride = chans + 1
    for row in range(depth):
        rows_ref[pl.ds(row * stride, chans), :] = cross_ref[pl.ds(row * chans, chans), :].astype(jnp.float32)
    copies = []

    def load(ch):
        return rows_ref[pl.ds(ch, depth, stride=stride), :].astype(jnp.bfloat16)

    def store(ch, lag):
        lag_ref[:, ch, :] = lag
        if (ch + 1) % batch == 0:
            step = ch // batch
            done = pl.ds(step * batch, batch)
            copies.append(pltpu.make_async_copy(lag_ref.at[:, done], out_ref.at[:, done], sent.at[step]))
            copies[-1].start()

    part, lag = load(0), None
    for ch in range(chans):
        following = load(ch + 1) if ch + 1 < chans else None
        fresh = lax.dot_general(part, high, dims, preferred_element_type=jnp.float32)
        fresh = fresh + lax.dot_general(part, low, dims, preferred_element_type=jnp.float32)
        if ch:
            store(ch - 1, lag)
        part, lag = following, fresh
    store(chans - 1, lag)
    for copy in copies:
        copy.wait()


def call(kernel, out_shape, scratch, in_spaces, out_space, *operands, vmem=VMEM_LIMIT):
    return pl.pallas_call(
        kernel,
        out_shape=out_shape,
        in_specs=[pl.BlockSpec(memory_space=space) for space in in_spaces],
        out_specs=pl.BlockSpec(memory_space=out_space),
        scratch_shapes=scratch,
        compiler_params=pltpu.CompilerParams(vmem_limit_bytes=vmem),
    )(*operands)


def shards(axes, order, spectra):
    _, chans, windows, width = spectra.shape
    bins = width // 2
    n_chan, n_day = order.shape
    groups = n_chan * n_day
    per_dev = bins // groups
    far = n_chan * chans // n_day

    packed = call(
        functools.partial(pack_kernel, groups, per_dev),
        jax.ShapeDtypeStruct((groups, per_dev + 1, chans, bins), jnp.bfloat16),
        [
            pltpu.VMEM((chans, windows, width), jnp.bfloat16),
            pltpu.VMEM((groups * ((per_dev + 1) * chans + 1), bins), jnp.float32),
            pltpu.SemaphoreType.DMA((FETCHES,)),
        ],
        [pltpu.HBM],
        pltpu.VMEM,
        spectra[0],
        vmem=PACK_VMEM_LIMIT,
    )
    mine = lax.all_to_all(packed, axes, 0, 0, tiled=True)
    cross = call(
        functools.partial(cross_kernel, order.tolist(), n_day),
        jax.ShapeDtypeStruct((groups, 2 * per_dev, chans, far), jnp.bfloat16),
        [],
        [pltpu.VMEM],
        pltpu.VMEM,
        mine,
    )
    cross = lax.all_to_all(cross, axes, 0, 0, tiled=True)
    high, low = lag_table(bins, per_dev, groups, 1.0 / (windows * n_day))
    return call(
        lags_kernel,
        jax.ShapeDtypeStruct((far, chans, width), jnp.float32),
        [
            pltpu.VMEM((width * (chans + 1), far), jnp.float32),
            pltpu.VMEM((far, chans, width), jnp.float32),
            pltpu.SemaphoreType.DMA((SENDS,)),
        ],
        [pltpu.VMEM] * 3,
        pltpu.HBM,
        cross.reshape(width * chans, far),
        jnp.asarray(high),
        jnp.asarray(low),
    )


def solution(mesh):
    n_chan, n_day = mesh.shape["chan"], mesh.shape["day"]
    outer = 4 if n_chan % 4 == 0 else 1
    inner = n_chan // outer
    split_mesh = jax.sharding.Mesh(mesh.devices.reshape(outer, inner, n_day), ("outer", "inner", "day"))
    order = np.arange(n_chan * n_day).reshape(n_day, inner, outer).transpose(2, 1, 0).reshape(n_chan, n_day)

    def run(spectra):
        bins = spectra.shape[-1] // 2
        if bins % (n_chan * n_day):
            return jax.shard_map(
                gathered_shards,
                mesh=mesh,
                in_specs=(P("day", "chan", None, None),),
                out_specs=P("day", "chan", None),
                check_vma=False,
            )(spectra)
        return jax.shard_map(
            functools.partial(shards, ("day", "inner", "outer"), order),
            mesh=split_mesh,
            in_specs=(P("day", ("outer", "inner"), None, None),),
            out_specs=P("day", ("outer", "inner"), None),
            check_vma=False,
        )(spectra)

    return run
```

```python
import functools

import jax
import jax.numpy as jnp
import numpy as np
from jax import lax
from jax.experimental import pallas as pl
from jax.experimental.pallas import tpu as pltpu
from jax.sharding import PartitionSpec as P

VMEM_LIMIT = 48 * 1024 * 1024
PACK_VMEM_LIMIT = 53 * 1024 * 1024
FETCHES = (2, 4)
SENDS = (2, 4)


def freq_taper(bins):
    freq_index = jnp.arange(bins, dtype=jnp.float32)
    half_taper = 0.54 - 0.46 * jnp.cos(2.0 * jnp.pi * (freq_index + 0.5) / bins)
    return jnp.concatenate([half_taper, half_taper])


def whiten(spectra):
    values = spectra.astype(jnp.float32)
    bins = values.shape[-1] // 2
    band_power = jnp.sum(values * values, axis=-1, keepdims=True) / bins + 1e-06
    return (values * freq_taper(bins) / jnp.sqrt(band_power)).astype(jnp.bfloat16)


def lag_matrix(bins):
    lag_count = 2 * bins
    freq_index = jnp.arange(bins, dtype=jnp.int32)
    lag_index = jnp.arange(lag_count, dtype=jnp.int32) - bins
    wound = jnp.mod(freq_index[:, None] * lag_index[None, :], lag_count)
    phase_angle = 2.0 * jnp.pi / lag_count * wound.astype(jnp.float32)
    return jnp.concatenate([jnp.cos(phase_angle), -jnp.sin(phase_angle)], axis=0)


def cross_spectra(far_rows, near_rows):
    bins = far_rows.shape[-1] // 2
    windows = far_rows.shape[-2]
    far_re, far_im = (far_rows[..., :bins], far_rows[..., bins:])
    near_re, near_im = (near_rows[..., :bins], near_rows[..., bins:])
    real_part = jnp.einsum("jwf,iwf->jif", far_re, near_re, preferred_element_type=jnp.float32)
    real_part = real_part + jnp.einsum(
        "jwf,iwf->jif", far_im, near_im, preferred_element_type=jnp.float32
    )
    imag_part = jnp.einsum("jwf,iwf->jif", far_re, near_im, preferred_element_type=jnp.float32)
    imag_part = imag_part - jnp.einsum(
        "jwf,iwf->jif", far_im, near_re, preferred_element_type=jnp.float32
    )
    return jnp.concatenate([real_part, imag_part], axis=-1) / windows


def to_lags(cross, table):
    flat = cross.reshape(-1, cross.shape[-1])
    lagged = jnp.dot(
        flat, table, precision=lax.Precision.HIGHEST, preferred_element_type=jnp.float32
    )
    return lagged.reshape(cross.shape[:-1] + (table.shape[1],))


def gathered_shards(spectra):
    local_white = whiten(spectra)[0]
    gathered = lax.all_gather(local_white, "chan", axis=0, tiled=True)
    table = lag_matrix(local_white.shape[-1] // 2)
    day_count = lax.axis_size("day")
    return lax.psum_scatter(
        to_lags(cross_spectra(gathered, local_white), table) / day_count,
        "day",
        scatter_dimension=0,
        tiled=True,
    )


def lag_table(bins, per_dev, groups, scale):
    lags = 2 * bins
    freq = (np.arange(per_dev)[None, :] * groups + np.arange(groups)[:, None]).reshape(-1)
    wound = (freq[:, None] * (np.arange(lags)[None, :] - bins)) % lags
    angle = 2.0 * np.pi / lags * wound
    table = (np.stack([np.cos(angle), -np.sin(angle)], axis=1) * scale).reshape(2 * bins, lags)
    table = table.astype(np.float32)
    high = table.astype(jnp.bfloat16)
    low = (table - high.astype(np.float32)).astype(jnp.bfloat16)
    return high, low


def pack_kernel(groups, per_dev, spectra_ref, out_ref, held_ref, rows_ref, arrived):
    chans, windows, width = held_ref.shape
    bins = width // 2
    head = bins // 2
    size = (per_dev + 1) * chans
    stride = size + 1
    fetches, pieces = arrived.shape
    batch = chans // fetches
    copies = []
    for piece in range(fetches * pieces):
        part = pl.ds(piece * (batch // pieces), batch // pieces)
        place = divmod(piece, pieces)
        copies.append(pltpu.make_async_copy(spectra_ref.at[part], held_ref.at[part], arrived.at[place]))
        copies[-1].start()
    freq = (lax.broadcasted_iota(jnp.int32, (1, width), 1) % bins).astype(jnp.float32)
    taper = 0.54 - 0.46 * jnp.cos(2.0 * jnp.pi * (freq + 0.5) / bins)
    lane = lax.broadcasted_iota(jnp.int32, (windows - head, bins), 1)
    pick = lax.broadcasted_iota(jnp.int32, (groups, bins), 1) % groups
    pick = (pick == lax.broadcasted_iota(jnp.int32, (groups, bins), 0)).astype(jnp.float32).astype(jnp.bfloat16)

    def whiten_channel(ch):
        values = held_ref[ch].astype(jnp.float32)
        power = jnp.sum(values * values, axis=-1, keepdims=True) / bins + 1e-06
        return (values * taper * lax.rsqrt(power)).astype(jnp.bfloat16)

    def place_channel(ch, white):
        real, imag = white[:, :bins], white[:, bins:]
        main = jnp.concatenate([real[:head], imag[:head]], axis=0).astype(jnp.float32).T
        spread = []
        for slot in range(per_dev):
            chosen = lane // groups == slot
            spread += [jnp.where(chosen, part[head:], jnp.zeros_like(part[head:])) for part in (real, imag)]
        tail = lax.dot_general(
            pick, jnp.concatenate(spread, axis=0), (((1,), (1,)), ((), ())), preferred_element_type=jnp.float32
        )
        for slot in range(per_dev):
            part = main[slot * groups:(slot + 1) * groups]
            rows_ref[pl.ds(slot * chans + ch, groups, stride=stride), :] = part
        rows_ref[pl.ds(per_dev * chans + ch, groups, stride=stride), :] = tail

    ready = []
    for step in range(fetches):
        for copy in copies[step * pieces:(step + 1) * pieces]:
            copy.wait()
        fresh = [(ch, whiten_channel(ch)) for ch in range(step * batch, (step + 1) * batch)]
        for ch, white in ready:
            place_channel(ch, white)
        ready = fresh
    for ch, white in ready:
        place_channel(ch, white)
    for first in range(0, groups, 4):
        rows = [rows_ref[pl.ds(group * stride, size), :].astype(jnp.bfloat16) for group in range(first, first + 4)]
        for place, part in enumerate(rows):
            out_ref[first + place] = part.reshape(out_ref.shape[1:])


def swap_parts(rows, half):
    lanes = rows.shape[-1]
    values = rows.astype(jnp.float32)
    lane = lax.broadcasted_iota(jnp.int32, values.shape, 1)
    first = (lane % (2 * half)) < half
    ahead = pltpu.roll(values, lanes - half, 1)
    behind = pltpu.roll(values, half, 1)
    return jnp.where(first, ahead, -behind).astype(jnp.bfloat16)


def cross_kernel(order, days, in_ref, out_ref):
    groups, parts, chans, lanes = in_ref.shape
    blocks = groups // days
    per_dev = parts - 1
    total = blocks * chans
    far = out_ref.shape[-1]
    narrow = lanes // per_dev // 2

    def rows(day, part):
        return jnp.concatenate([in_ref[order[block][day], part] for block in range(blocks)], axis=0)

    tails = [rows(day, per_dev) for day in range(days)]
    tails_swapped = [swap_parts(tail, narrow) for tail in tails]
    far_tail = jnp.concatenate(tails, axis=1)
    lane = lax.broadcasted_iota(jnp.int32, (2 * total, lanes), 1) // (2 * narrow)
    dims = (((1,), (1,)), ((), ()))
    for slot in range(per_dev):
        mains = [rows(day, slot) for day in range(days)]
        far_main = jnp.concatenate(mains, axis=1)
        turned = [swap_parts(m, lanes // 2) for m in mains]
        near_main = [jnp.concatenate(pair, axis=0) for pair in zip(mains, turned)]
        near_tail = [jnp.concatenate(pair, axis=0) for pair in zip(tails, tails_swapped)]
        near_tail = [jnp.where(lane == slot, t, jnp.zeros_like(t)) for t in near_tail]
        cross = lax.dot_general(
            jnp.concatenate(near_main, axis=1), far_main, dims, preferred_element_type=jnp.float32
        ) + lax.dot_general(
            jnp.concatenate(near_tail, axis=1), far_tail, dims, preferred_element_type=jnp.float32
        )
        cross = cross.astype(out_ref.dtype)
        for kind in range(2):
            for block in range(blocks):
                start = kind * total + block * chans
                for half in range(days):
                    piece = cross[start:start + chans, half * far:(half + 1) * far]
                    out_ref[order[block][half], 2 * slot + kind] = piece


def lags_kernel(cross_ref, high_ref, low_ref, out_ref, rows_ref, lag_ref, sent):
    chans = out_ref.shape[1]
    depth = high_ref.shape[0]
    high, low = high_ref[...], low_ref[...]
    dims = (((0,), (0,)), ((), ()))
    parts, pieces = sent.shape
    batch = chans // parts
    run = out_ref.shape[0] // pieces
    stride = chans + 1
    for row in range(depth):
        rows_ref[pl.ds(row * stride, chans), :] = cross_ref[pl.ds(row * chans, chans), :].astype(jnp.float32)
    copies = []

    def load(ch):
        return rows_ref[pl.ds(ch, depth, stride=stride), :].astype(jnp.bfloat16)

    def store(ch, lag):
        lag_ref[:, ch, :] = lag
        if (ch + 1) % batch == 0:
            step = ch // batch
            for piece in range(pieces):
                place = (pl.ds(piece * run, run), pl.ds(step * batch, batch))
                copies.append(pltpu.make_async_copy(lag_ref.at[place], out_ref.at[place], sent.at[step, piece]))
                copies[-1].start()

    part, lag = load(0), None
    for ch in range(chans):
        following = load(ch + 1) if ch + 1 < chans else None
        fresh = lax.dot_general(part, high, dims, preferred_element_type=jnp.float32)
        fresh = fresh + lax.dot_general(part, low, dims, preferred_element_type=jnp.float32)
        if ch:
            store(ch - 1, lag)
        part, lag = following, fresh
    store(chans - 1, lag)
    for copy in copies:
        copy.wait()


def call(kernel, out_shape, scratch, in_spaces, out_space, *operands, vmem=VMEM_LIMIT):
    return pl.pallas_call(
        kernel,
        out_shape=out_shape,
        in_specs=[pl.BlockSpec(memory_space=space) for space in in_spaces],
        out_specs=pl.BlockSpec(memory_space=out_space),
        scratch_shapes=scratch,
        compiler_params=pltpu.CompilerParams(vmem_limit_bytes=vmem),
    )(*operands)


def shards(axes, order, spectra):
    _, chans, windows, width = spectra.shape
    bins = width // 2
    n_chan, n_day = order.shape
    groups = n_chan * n_day
    per_dev = bins // groups
    far = n_chan * chans // n_day

    packed = call(
        functools.partial(pack_kernel, groups, per_dev),
        jax.ShapeDtypeStruct((groups, per_dev + 1, chans, bins), jnp.bfloat16),
        [
            pltpu.VMEM((chans, windows, width), jnp.bfloat16),
            pltpu.VMEM((groups * ((per_dev + 1) * chans + 1), bins), jnp.float32),
            pltpu.SemaphoreType.DMA(FETCHES),
        ],
        [pltpu.HBM],
        pltpu.VMEM,
        spectra[0],
        vmem=PACK_VMEM_LIMIT,
    )
    mine = lax.all_to_all(packed, axes, 0, 0, tiled=True)
    cross = call(
        functools.partial(cross_kernel, order.tolist(), n_day),
        jax.ShapeDtypeStruct((groups, 2 * per_dev, chans, far), jnp.bfloat16),
        [],
        [pltpu.VMEM],
        pltpu.VMEM,
        mine,
    )
    cross = lax.all_to_all(cross, axes, 0, 0, tiled=True)
    high, low = lag_table(bins, per_dev, groups, 1.0 / (windows * n_day))
    return call(
        lags_kernel,
        jax.ShapeDtypeStruct((far, chans, width), jnp.float32),
        [
            pltpu.VMEM((width * (chans + 1), far), jnp.float32),
            pltpu.VMEM((far, chans, width), jnp.float32),
            pltpu.SemaphoreType.DMA(SENDS),
        ],
        [pltpu.VMEM] * 3,
        pltpu.HBM,
        cross.reshape(width * chans, far),
        jnp.asarray(high),
        jnp.asarray(low),
    )


def solution(mesh):
    n_chan, n_day = mesh.shape["chan"], mesh.shape["day"]
    outer = 4 if n_chan % 4 == 0 else 1
    inner = n_chan // outer
    split_mesh = jax.sharding.Mesh(mesh.devices.reshape(outer, inner, n_day), ("outer", "inner", "day"))
    order = np.arange(n_chan * n_day).reshape(n_day, inner, outer).transpose(2, 1, 0).reshape(n_chan, n_day)

    def run(spectra):
        bins = spectra.shape[-1] // 2
        if bins % (n_chan * n_day):
            return jax.shard_map(
                gathered_shards,
                mesh=mesh,
                in_specs=(P("day", "chan", None, None),),
                out_specs=P("day", "chan", None),
                check_vma=False,
            )(spectra)
        return jax.shard_map(
            functools.partial(shards, ("day", "inner", "outer"), order),
            mesh=split_mesh,
            in_specs=(P("day", ("outer", "inner"), None, None),),
            out_specs=P("day", ("outer", "inner"), None),
            check_vma=False,
        )(spectra)

    return run
```

```python
import functools

import jax
import jax.numpy as jnp
import numpy as np
from jax import lax
from jax.experimental import pallas as pl
from jax.experimental.pallas import tpu as pltpu
from jax.sharding import PartitionSpec as P

VMEM_LIMIT = 48 * 1024 * 1024
PACK_VMEM_LIMIT = 53 * 1024 * 1024
FETCHES = 2
SENDS = 2


def freq_taper(bins):
    freq_index = jnp.arange(bins, dtype=jnp.float32)
    half_taper = 0.54 - 0.46 * jnp.cos(2.0 * jnp.pi * (freq_index + 0.5) / bins)
    return jnp.concatenate([half_taper, half_taper])


def whiten(spectra):
    values = spectra.astype(jnp.float32)
    bins = values.shape[-1] // 2
    band_power = jnp.sum(values * values, axis=-1, keepdims=True) / bins + 1e-06
    return (values * freq_taper(bins) / jnp.sqrt(band_power)).astype(jnp.bfloat16)


def lag_matrix(bins):
    lag_count = 2 * bins
    freq_index = jnp.arange(bins, dtype=jnp.int32)
    lag_index = jnp.arange(lag_count, dtype=jnp.int32) - bins
    wound = jnp.mod(freq_index[:, None] * lag_index[None, :], lag_count)
    phase_angle = 2.0 * jnp.pi / lag_count * wound.astype(jnp.float32)
    return jnp.concatenate([jnp.cos(phase_angle), -jnp.sin(phase_angle)], axis=0)


def cross_spectra(far_rows, near_rows):
    bins = far_rows.shape[-1] // 2
    windows = far_rows.shape[-2]
    far_re, far_im = (far_rows[..., :bins], far_rows[..., bins:])
    near_re, near_im = (near_rows[..., :bins], near_rows[..., bins:])
    real_part = jnp.einsum("jwf,iwf->jif", far_re, near_re, preferred_element_type=jnp.float32)
    real_part = real_part + jnp.einsum(
        "jwf,iwf->jif", far_im, near_im, preferred_element_type=jnp.float32
    )
    imag_part = jnp.einsum("jwf,iwf->jif", far_re, near_im, preferred_element_type=jnp.float32)
    imag_part = imag_part - jnp.einsum(
        "jwf,iwf->jif", far_im, near_re, preferred_element_type=jnp.float32
    )
    return jnp.concatenate([real_part, imag_part], axis=-1) / windows


def to_lags(cross, table):
    flat = cross.reshape(-1, cross.shape[-1])
    lagged = jnp.dot(
        flat, table, precision=lax.Precision.HIGHEST, preferred_element_type=jnp.float32
    )
    return lagged.reshape(cross.shape[:-1] + (table.shape[1],))


def gathered_shards(spectra):
    local_white = whiten(spectra)[0]
    gathered = lax.all_gather(local_white, "chan", axis=0, tiled=True)
    table = lag_matrix(local_white.shape[-1] // 2)
    day_count = lax.axis_size("day")
    return lax.psum_scatter(
        to_lags(cross_spectra(gathered, local_white), table) / day_count,
        "day",
        scatter_dimension=0,
        tiled=True,
    )


def lag_table(bins, per_dev, groups, scale):
    lags = 2 * bins
    freq = (np.arange(per_dev)[None, :] * groups + np.arange(groups)[:, None]).reshape(-1)
    wound = (freq[:, None] * (np.arange(lags)[None, :] - bins)) % lags
    angle = 2.0 * np.pi / lags * wound
    table = (np.stack([np.cos(angle), -np.sin(angle)], axis=1) * scale).reshape(2 * bins, lags)
    table = table.astype(np.float32)
    high = table.astype(jnp.bfloat16)
    low = (table - high.astype(np.float32)).astype(jnp.bfloat16)
    return high, low


def pack_kernel(groups, per_dev, spectra_ref, out_ref, held_ref, rows_ref, arrived):
    chans, windows, width = held_ref.shape
    bins = width // 2
    head = bins // 2
    size = (per_dev + 1) * chans
    stride = size + 1
    fetches = arrived.shape[0]
    batch = chans // fetches
    copies = []
    for step in range(fetches):
        part = pl.ds(step * batch, batch)
        copies.append(pltpu.make_async_copy(spectra_ref.at[part], held_ref.at[part], arrived.at[step]))
        copies[-1].start()
    freq = (lax.broadcasted_iota(jnp.int32, (1, width), 1) % bins).astype(jnp.float32)
    taper = 0.54 - 0.46 * jnp.cos(2.0 * jnp.pi * (freq + 0.5) / bins)
    lane = lax.broadcasted_iota(jnp.int32, (windows - head, bins), 1)
    pick = lax.broadcasted_iota(jnp.int32, (groups, bins), 1) % groups
    pick = (pick == lax.broadcasted_iota(jnp.int32, (groups, bins), 0)).astype(jnp.float32).astype(jnp.bfloat16)

    def whiten_channel(ch):
        values = held_ref[ch].astype(jnp.float32)
        power = jnp.sum(values * values, axis=-1, keepdims=True) / bins + 1e-06
        return (values * taper * lax.rsqrt(power)).astype(jnp.bfloat16)

    def place_channel(ch, white):
        real, imag = white[:, :bins], white[:, bins:]
        main = jnp.concatenate([real[:head], imag[:head]], axis=0).astype(jnp.float32).T
        spread = []
        for slot in range(per_dev):
            chosen = lane // groups == slot
            spread += [jnp.where(chosen, part[head:], jnp.zeros_like(part[head:])) for part in (real, imag)]
        tail = lax.dot_general(
            pick, jnp.concatenate(spread, axis=0), (((1,), (1,)), ((), ())), preferred_element_type=jnp.float32
        )
        for slot in range(per_dev):
            part = main[slot * groups:(slot + 1) * groups]
            rows_ref[pl.ds(slot * chans + ch, groups, stride=stride), :] = part
        rows_ref[pl.ds(per_dev * chans + ch, groups, stride=stride), :] = tail

    ready = []
    for step in range(fetches):
        copies[step].wait()
        fresh = [(ch, whiten_channel(ch)) for ch in range(step * batch, (step + 1) * batch)]
        for ch, white in ready:
            place_channel(ch, white)
        ready = fresh
    for ch, white in ready:
        place_channel(ch, white)
    for first in range(0, groups, 4):
        rows = [rows_ref[pl.ds(group * stride, size), :].astype(jnp.bfloat16) for group in range(first, first + 4)]
        for place, part in enumerate(rows):
            out_ref[first + place] = part.reshape(out_ref.shape[1:])


def swap_parts(rows, half):
    lanes = rows.shape[-1]
    values = rows.astype(jnp.float32)
    lane = lax.broadcasted_iota(jnp.int32, values.shape, 1)
    first = (lane % (2 * half)) < half
    ahead = pltpu.roll(values, lanes - half, 1)
    behind = pltpu.roll(values, half, 1)
    return jnp.where(first, ahead, -behind).astype(jnp.bfloat16)


def cross_kernel(order, days, in_ref, out_ref):
    groups, parts, chans, lanes = in_ref.shape
    blocks = groups // days
    per_dev = parts - 1
    total = blocks * chans
    far = out_ref.shape[-1]
    narrow = lanes // per_dev // 2

    def rows(day, part):
        return jnp.concatenate([in_ref[order[block][day], part] for block in range(blocks)], axis=0)

    tails = [rows(day, per_dev) for day in range(days)]
    tails_swapped = [swap_parts(tail, narrow) for tail in tails]
    far_tail = jnp.concatenate(tails, axis=1)
    lane = lax.broadcasted_iota(jnp.int32, (2 * total, lanes), 1) // (2 * narrow)
    dims = (((1,), (1,)), ((), ()))
    for slot in range(per_dev):
        mains = [rows(day, slot) for day in range(days)]
        far_main = jnp.concatenate(mains, axis=1)
        turned = [swap_parts(m, lanes // 2) for m in mains]
        near_main = [jnp.concatenate(pair, axis=0) for pair in zip(mains, turned)]
        near_tail = [jnp.concatenate(pair, axis=0) for pair in zip(tails, tails_swapped)]
        near_tail = [jnp.where(lane == slot, t, jnp.zeros_like(t)) for t in near_tail]
        cross = lax.dot_general(
            jnp.concatenate(near_main, axis=1), far_main, dims, preferred_element_type=jnp.float32
        ) + lax.dot_general(
            jnp.concatenate(near_tail, axis=1), far_tail, dims, preferred_element_type=jnp.float32
        )
        cross = cross.astype(out_ref.dtype)
        for kind in range(2):
            for block in range(blocks):
                start = kind * total + block * chans
                for half in range(days):
                    piece = cross[start:start + chans, half * far:(half + 1) * far]
                    out_ref[order[block][half], 2 * slot + kind] = piece


def lags_kernel(cross_ref, high_ref, low_ref, out_ref, rows_ref, lag_ref, sent):
    chans = out_ref.shape[1]
    depth = high_ref.shape[0]
    table = jnp.concatenate([high_ref[...], low_ref[...]], axis=0)
    parts = sent.shape[0]
    batch = chans // parts
    stride = chans + 1
    for row in range(depth):
        rows_ref[pl.ds(row * stride, chans), :] = cross_ref[pl.ds(row * chans, chans), :].astype(jnp.float32)
    copies = []

    def load(ch):
        part = rows_ref[pl.ds(ch, depth, stride=stride), :].astype(jnp.bfloat16).T
        return jnp.concatenate([part, part], axis=1)

    def store(ch, lag):
        lag_ref[:, ch, :] = lag
        if (ch + 1) % batch == 0:
            step = ch // batch
            done = pl.ds(step * batch, batch)
            copies.append(pltpu.make_async_copy(lag_ref.at[:, done], out_ref.at[:, done], sent.at[step]))
            copies[-1].start()

    part, lag = load(0), None
    for ch in range(chans):
        following = load(ch + 1) if ch + 1 < chans else None
        fresh = jnp.dot(part, table, preferred_element_type=jnp.float32)
        if ch:
            store(ch - 1, lag)
        part, lag = following, fresh
    store(chans - 1, lag)
    for copy in copies:
        copy.wait()


def call(kernel, out_shape, scratch, in_spaces, out_space, *operands, vmem=VMEM_LIMIT):
    return pl.pallas_call(
        kernel,
        out_shape=out_shape,
        in_specs=[pl.BlockSpec(memory_space=space) for space in in_spaces],
        out_specs=pl.BlockSpec(memory_space=out_space),
        scratch_shapes=scratch,
        compiler_params=pltpu.CompilerParams(vmem_limit_bytes=vmem),
    )(*operands)


def shards(axes, order, spectra):
    _, chans, windows, width = spectra.shape
    bins = width // 2
    n_chan, n_day = order.shape
    groups = n_chan * n_day
    per_dev = bins // groups
    far = n_chan * chans // n_day

    packed = call(
        functools.partial(pack_kernel, groups, per_dev),
        jax.ShapeDtypeStruct((groups, per_dev + 1, chans, bins), jnp.bfloat16),
        [
            pltpu.VMEM((chans, windows, width), jnp.bfloat16),
            pltpu.VMEM((groups * ((per_dev + 1) * chans + 1), bins), jnp.float32),
            pltpu.SemaphoreType.DMA((FETCHES,)),
        ],
        [pltpu.HBM],
        pltpu.VMEM,
        spectra[0],
        vmem=PACK_VMEM_LIMIT,
    )
    mine = lax.all_to_all(packed, axes, 0, 0, tiled=True)
    cross = call(
        functools.partial(cross_kernel, order.tolist(), n_day),
        jax.ShapeDtypeStruct((groups, 2 * per_dev, chans, far), jnp.bfloat16),
        [],
        [pltpu.VMEM],
        pltpu.VMEM,
        mine,
    )
    cross = lax.all_to_all(cross, axes, 0, 0, tiled=True)
    high, low = lag_table(bins, per_dev, groups, 1.0 / (windows * n_day))
    return call(
        lags_kernel,
        jax.ShapeDtypeStruct((far, chans, width), jnp.float32),
        [
            pltpu.VMEM((width * (chans + 1), far), jnp.float32),
            pltpu.VMEM((far, chans, width), jnp.float32),
            pltpu.SemaphoreType.DMA((SENDS,)),
        ],
        [pltpu.VMEM] * 3,
        pltpu.HBM,
        cross.reshape(width * chans, far),
        jnp.asarray(high),
        jnp.asarray(low),
    )


def solution(mesh):
    n_chan, n_day = mesh.shape["chan"], mesh.shape["day"]
    outer = 4 if n_chan % 4 == 0 else 1
    inner = n_chan // outer
    split_mesh = jax.sharding.Mesh(mesh.devices.reshape(outer, inner, n_day), ("outer", "inner", "day"))
    order = np.arange(n_chan * n_day).reshape(n_day, inner, outer).transpose(2, 1, 0).reshape(n_chan, n_day)

    def run(spectra):
        bins = spectra.shape[-1] // 2
        if bins % (n_chan * n_day):
            return jax.shard_map(
                gathered_shards,
                mesh=mesh,
                in_specs=(P("day", "chan", None, None),),
                out_specs=P("day", "chan", None),
                check_vma=False,
            )(spectra)
        return jax.shard_map(
            functools.partial(shards, ("day", "inner", "outer"), order),
            mesh=split_mesh,
            in_specs=(P("day", ("outer", "inner"), None, None),),
            out_specs=P("day", ("outer", "inner"), None),
            check_vma=False,
        )(spectra)

    return run
```

```python
import functools

import jax
import jax.numpy as jnp
import numpy as np
from jax import lax
from jax.experimental import pallas as pl
from jax.experimental.pallas import tpu as pltpu
from jax.sharding import PartitionSpec as P

VMEM_LIMIT = 48 * 1024 * 1024
PACK_VMEM_LIMIT = 53 * 1024 * 1024
FETCHES = 2
SENDS = (2, 2)


def freq_taper(bins):
    freq_index = jnp.arange(bins, dtype=jnp.float32)
    half_taper = 0.54 - 0.46 * jnp.cos(2.0 * jnp.pi * (freq_index + 0.5) / bins)
    return jnp.concatenate([half_taper, half_taper])


def whiten(spectra):
    values = spectra.astype(jnp.float32)
    bins = values.shape[-1] // 2
    band_power = jnp.sum(values * values, axis=-1, keepdims=True) / bins + 1e-06
    return (values * freq_taper(bins) / jnp.sqrt(band_power)).astype(jnp.bfloat16)


def lag_matrix(bins):
    lag_count = 2 * bins
    freq_index = jnp.arange(bins, dtype=jnp.int32)
    lag_index = jnp.arange(lag_count, dtype=jnp.int32) - bins
    wound = jnp.mod(freq_index[:, None] * lag_index[None, :], lag_count)
    phase_angle = 2.0 * jnp.pi / lag_count * wound.astype(jnp.float32)
    return jnp.concatenate([jnp.cos(phase_angle), -jnp.sin(phase_angle)], axis=0)


def cross_spectra(far_rows, near_rows):
    bins = far_rows.shape[-1] // 2
    windows = far_rows.shape[-2]
    far_re, far_im = (far_rows[..., :bins], far_rows[..., bins:])
    near_re, near_im = (near_rows[..., :bins], near_rows[..., bins:])
    real_part = jnp.einsum("jwf,iwf->jif", far_re, near_re, preferred_element_type=jnp.float32)
    real_part = real_part + jnp.einsum(
        "jwf,iwf->jif", far_im, near_im, preferred_element_type=jnp.float32
    )
    imag_part = jnp.einsum("jwf,iwf->jif", far_re, near_im, preferred_element_type=jnp.float32)
    imag_part = imag_part - jnp.einsum(
        "jwf,iwf->jif", far_im, near_re, preferred_element_type=jnp.float32
    )
    return jnp.concatenate([real_part, imag_part], axis=-1) / windows


def to_lags(cross, table):
    flat = cross.reshape(-1, cross.shape[-1])
    lagged = jnp.dot(
        flat, table, precision=lax.Precision.HIGHEST, preferred_element_type=jnp.float32
    )
    return lagged.reshape(cross.shape[:-1] + (table.shape[1],))


def gathered_shards(spectra):
    local_white = whiten(spectra)[0]
    gathered = lax.all_gather(local_white, "chan", axis=0, tiled=True)
    table = lag_matrix(local_white.shape[-1] // 2)
    day_count = lax.axis_size("day")
    return lax.psum_scatter(
        to_lags(cross_spectra(gathered, local_white), table) / day_count,
        "day",
        scatter_dimension=0,
        tiled=True,
    )


def lag_table(bins, per_dev, groups, scale):
    lags = 2 * bins
    freq = (np.arange(per_dev)[None, :] * groups + np.arange(groups)[:, None]).reshape(-1)
    wound = (freq[:, None] * (np.arange(lags)[None, :] - bins)) % lags
    angle = 2.0 * np.pi / lags * wound
    table = (np.stack([np.cos(angle), -np.sin(angle)], axis=1) * scale).reshape(2 * bins, lags)
    table = table.astype(np.float32)
    high = table.astype(jnp.bfloat16)
    low = (table - high.astype(np.float32)).astype(jnp.bfloat16)
    return high, low


def pack_kernel(groups, per_dev, spectra_ref, out_ref, held_ref, rows_ref, arrived):
    chans, windows, width = held_ref.shape
    bins = width // 2
    head = bins // 2
    size = (per_dev + 1) * chans
    stride = size + 1
    fetches = arrived.shape[0]
    batch = chans // fetches
    copies = []
    for step in range(fetches):
        part = pl.ds(step * batch, batch)
        copies.append(pltpu.make_async_copy(spectra_ref.at[part], held_ref.at[part], arrived.at[step]))
        copies[-1].start()
    freq = (lax.broadcasted_iota(jnp.int32, (1, width), 1) % bins).astype(jnp.float32)
    taper = 0.54 - 0.46 * jnp.cos(2.0 * jnp.pi * (freq + 0.5) / bins)
    lane = lax.broadcasted_iota(jnp.int32, (windows - head, bins), 1)
    pick = lax.broadcasted_iota(jnp.int32, (groups, bins), 1) % groups
    pick = (pick == lax.broadcasted_iota(jnp.int32, (groups, bins), 0)).astype(jnp.float32).astype(jnp.bfloat16)

    def whiten_channel(ch):
        values = held_ref[ch].astype(jnp.float32)
        power = jnp.sum(values * values, axis=-1, keepdims=True) / bins + 1e-06
        return (values * taper * lax.rsqrt(power)).astype(jnp.bfloat16)

    def place_channel(ch, white):
        real, imag = white[:, :bins], white[:, bins:]
        main = jnp.concatenate([real[:head], imag[:head]], axis=0).astype(jnp.float32).T
        spread = []
        for slot in range(per_dev):
            chosen = lane // groups == slot
            spread += [jnp.where(chosen, part[head:], jnp.zeros_like(part[head:])) for part in (real, imag)]
        tail = lax.dot_general(
            pick, jnp.concatenate(spread, axis=0), (((1,), (1,)), ((), ())), preferred_element_type=jnp.float32
        )
        for slot in range(per_dev):
            part = main[slot * groups:(slot + 1) * groups]
            rows_ref[pl.ds(slot * chans + ch, groups, stride=stride), :] = part
        rows_ref[pl.ds(per_dev * chans + ch, groups, stride=stride), :] = tail

    ready = []
    for step in range(fetches):
        copies[step].wait()
        fresh = [(ch, whiten_channel(ch)) for ch in range(step * batch, (step + 1) * batch)]
        for ch, white in ready:
            place_channel(ch, white)
        ready = fresh
    for ch, white in ready:
        place_channel(ch, white)
    for first in range(0, groups, 4):
        rows = [rows_ref[pl.ds(group * stride, size), :].astype(jnp.bfloat16) for group in range(first, first + 4)]
        for place, part in enumerate(rows):
            out_ref[first + place] = part.reshape(out_ref.shape[1:])


def swap_parts(rows, half):
    lanes = rows.shape[-1]
    values = rows.astype(jnp.float32)
    lane = lax.broadcasted_iota(jnp.int32, values.shape, 1)
    first = (lane % (2 * half)) < half
    ahead = pltpu.roll(values, lanes - half, 1)
    behind = pltpu.roll(values, half, 1)
    return jnp.where(first, ahead, -behind).astype(jnp.bfloat16)


def cross_kernel(order, days, in_ref, out_ref):
    groups, parts, chans, lanes = in_ref.shape
    blocks = groups // days
    per_dev = parts - 1
    total = blocks * chans
    far = out_ref.shape[-1]
    narrow = lanes // per_dev // 2

    def rows(day, part):
        return jnp.concatenate([in_ref[order[block][day], part] for block in range(blocks)], axis=0)

    tails = [rows(day, per_dev) for day in range(days)]
    tails_swapped = [swap_parts(tail, narrow) for tail in tails]
    far_tail = jnp.concatenate(tails, axis=1)
    lane = lax.broadcasted_iota(jnp.int32, (2 * total, lanes), 1) // (2 * narrow)
    dims = (((1,), (1,)), ((), ()))
    for slot in range(per_dev):
        mains = [rows(day, slot) for day in range(days)]
        far_main = jnp.concatenate(mains, axis=1)
        turned = [swap_parts(m, lanes // 2) for m in mains]
        near_main = [jnp.concatenate(pair, axis=0) for pair in zip(mains, turned)]
        near_tail = [jnp.concatenate(pair, axis=0) for pair in zip(tails, tails_swapped)]
        near_tail = [jnp.where(lane == slot, t, jnp.zeros_like(t)) for t in near_tail]
        cross = lax.dot_general(
            jnp.concatenate(near_main, axis=1), far_main, dims, preferred_element_type=jnp.float32
        ) + lax.dot_general(
            jnp.concatenate(near_tail, axis=1), far_tail, dims, preferred_element_type=jnp.float32
        )
        cross = cross.astype(out_ref.dtype)
        for kind in range(2):
            for block in range(blocks):
                start = kind * total + block * chans
                for half in range(days):
                    piece = cross[start:start + chans, half * far:(half + 1) * far]
                    out_ref[order[block][half], 2 * slot + kind] = piece


def lags_kernel(cross_ref, high_ref, low_ref, out_ref, rows_ref, lag_ref, sent):
    chans = out_ref.shape[1]
    depth = high_ref.shape[0]
    table = jnp.concatenate([high_ref[...], low_ref[...]], axis=0)
    parts, pieces = sent.shape
    batch = chans // parts
    run = out_ref.shape[0] // pieces
    stride = batch + 1

    def fill(step, rows):
        for row in rows:
            values = cross_ref[pl.ds(row * chans, chans), :].astype(jnp.float32)
            rows_ref[step, pl.ds(row * stride, batch), :] = values[step * batch:(step + 1) * batch]

    fill(0, range(depth))
    copies = []
    for step in range(parts):
        turned = []
        for place in range(batch):
            part = rows_ref[step, pl.ds(place, depth, stride=stride), :].astype(jnp.bfloat16).T
            turned.append(jnp.concatenate([part, part], axis=1))
        for piece in range(pieces):
            done = pl.ds(piece * run, run)
            for place, part in enumerate(turned):
                lag = jnp.dot(part[piece * run:(piece + 1) * run], table, preferred_element_type=jnp.float32)
                lag_ref[done, step * batch + place, :] = lag
            place = (done, pl.ds(step * batch, batch))
            copies.append(pltpu.make_async_copy(lag_ref.at[place], out_ref.at[place], sent.at[step, piece]))
            copies[-1].start()
            if step + 1 < parts:
                share = depth // pieces
                fill(step + 1, range(piece * share, (piece + 1) * share))
    for copy in copies:
        copy.wait()


def call(kernel, out_shape, scratch, in_spaces, out_space, *operands, vmem=VMEM_LIMIT):
    return pl.pallas_call(
        kernel,
        out_shape=out_shape,
        in_specs=[pl.BlockSpec(memory_space=space) for space in in_spaces],
        out_specs=pl.BlockSpec(memory_space=out_space),
        scratch_shapes=scratch,
        compiler_params=pltpu.CompilerParams(vmem_limit_bytes=vmem),
    )(*operands)


def shards(axes, order, spectra):
    _, chans, windows, width = spectra.shape
    bins = width // 2
    n_chan, n_day = order.shape
    groups = n_chan * n_day
    per_dev = bins // groups
    far = n_chan * chans // n_day

    packed = call(
        functools.partial(pack_kernel, groups, per_dev),
        jax.ShapeDtypeStruct((groups, per_dev + 1, chans, bins), jnp.bfloat16),
        [
            pltpu.VMEM((chans, windows, width), jnp.bfloat16),
            pltpu.VMEM((groups * ((per_dev + 1) * chans + 1), bins), jnp.float32),
            pltpu.SemaphoreType.DMA((FETCHES,)),
        ],
        [pltpu.HBM],
        pltpu.VMEM,
        spectra[0],
        vmem=PACK_VMEM_LIMIT,
    )
    mine = lax.all_to_all(packed, axes, 0, 0, tiled=True)
    cross = call(
        functools.partial(cross_kernel, order.tolist(), n_day),
        jax.ShapeDtypeStruct((groups, 2 * per_dev, chans, far), jnp.bfloat16),
        [],
        [pltpu.VMEM],
        pltpu.VMEM,
        mine,
    )
    cross = lax.all_to_all(cross, axes, 0, 0, tiled=True)
    high, low = lag_table(bins, per_dev, groups, 1.0 / (windows * n_day))
    return call(
        lags_kernel,
        jax.ShapeDtypeStruct((far, chans, width), jnp.float32),
        [
            pltpu.VMEM((SENDS[0], width * (chans // SENDS[0] + 1), far), jnp.float32),
            pltpu.VMEM((far, chans, width), jnp.float32),
            pltpu.SemaphoreType.DMA(SENDS),
        ],
        [pltpu.VMEM] * 3,
        pltpu.HBM,
        cross.reshape(width * chans, far),
        jnp.asarray(high),
        jnp.asarray(low),
    )


def solution(mesh):
    n_chan, n_day = mesh.shape["chan"], mesh.shape["day"]
    outer = 4 if n_chan % 4 == 0 else 1
    inner = n_chan // outer
    split_mesh = jax.sharding.Mesh(mesh.devices.reshape(outer, inner, n_day), ("outer", "inner", "day"))
    order = np.arange(n_chan * n_day).reshape(n_day, inner, outer).transpose(2, 1, 0).reshape(n_chan, n_day)

    def run(spectra):
        bins = spectra.shape[-1] // 2
        if bins % (n_chan * n_day):
            return jax.shard_map(
                gathered_shards,
                mesh=mesh,
                in_specs=(P("day", "chan", None, None),),
                out_specs=P("day", "chan", None),
                check_vma=False,
            )(spectra)
        return jax.shard_map(
            functools.partial(shards, ("day", "inner", "outer"), order),
            mesh=split_mesh,
            in_specs=(P("day", ("outer", "inner"), None, None),),
            out_specs=P("day", ("outer", "inner"), None),
            check_vma=False,
        )(spectra)

    return run
```

```python
import functools

import jax
import jax.numpy as jnp
import numpy as np
from jax import lax
from jax.experimental import pallas as pl
from jax.experimental.pallas import tpu as pltpu
from jax.sharding import PartitionSpec as P

VMEM_LIMIT = 48 * 1024 * 1024
PACK_VMEM_LIMIT = 53 * 1024 * 1024
FETCHES = 2
SENDS = 2
TALL = 2


def freq_taper(bins):
    freq_index = jnp.arange(bins, dtype=jnp.float32)
    half_taper = 0.54 - 0.46 * jnp.cos(2.0 * jnp.pi * (freq_index + 0.5) / bins)
    return jnp.concatenate([half_taper, half_taper])


def whiten(spectra):
    values = spectra.astype(jnp.float32)
    bins = values.shape[-1] // 2
    band_power = jnp.sum(values * values, axis=-1, keepdims=True) / bins + 1e-06
    return (values * freq_taper(bins) / jnp.sqrt(band_power)).astype(jnp.bfloat16)


def lag_matrix(bins):
    lag_count = 2 * bins
    freq_index = jnp.arange(bins, dtype=jnp.int32)
    lag_index = jnp.arange(lag_count, dtype=jnp.int32) - bins
    wound = jnp.mod(freq_index[:, None] * lag_index[None, :], lag_count)
    phase_angle = 2.0 * jnp.pi / lag_count * wound.astype(jnp.float32)
    return jnp.concatenate([jnp.cos(phase_angle), -jnp.sin(phase_angle)], axis=0)


def cross_spectra(far_rows, near_rows):
    bins = far_rows.shape[-1] // 2
    windows = far_rows.shape[-2]
    far_re, far_im = (far_rows[..., :bins], far_rows[..., bins:])
    near_re, near_im = (near_rows[..., :bins], near_rows[..., bins:])
    real_part = jnp.einsum("jwf,iwf->jif", far_re, near_re, preferred_element_type=jnp.float32)
    real_part = real_part + jnp.einsum(
        "jwf,iwf->jif", far_im, near_im, preferred_element_type=jnp.float32
    )
    imag_part = jnp.einsum("jwf,iwf->jif", far_re, near_im, preferred_element_type=jnp.float32)
    imag_part = imag_part - jnp.einsum(
        "jwf,iwf->jif", far_im, near_re, preferred_element_type=jnp.float32
    )
    return jnp.concatenate([real_part, imag_part], axis=-1) / windows


def to_lags(cross, table):
    flat = cross.reshape(-1, cross.shape[-1])
    lagged = jnp.dot(
        flat, table, precision=lax.Precision.HIGHEST, preferred_element_type=jnp.float32
    )
    return lagged.reshape(cross.shape[:-1] + (table.shape[1],))


def gathered_shards(spectra):
    local_white = whiten(spectra)[0]
    gathered = lax.all_gather(local_white, "chan", axis=0, tiled=True)
    table = lag_matrix(local_white.shape[-1] // 2)
    day_count = lax.axis_size("day")
    return lax.psum_scatter(
        to_lags(cross_spectra(gathered, local_white), table) / day_count,
        "day",
        scatter_dimension=0,
        tiled=True,
    )


def lag_table(bins, per_dev, groups, scale):
    lags = 2 * bins
    freq = (np.arange(per_dev)[None, :] * groups + np.arange(groups)[:, None]).reshape(-1)
    wound = (freq[:, None] * (np.arange(lags)[None, :] - bins)) % lags
    angle = 2.0 * np.pi / lags * wound
    table = (np.stack([np.cos(angle), -np.sin(angle)], axis=1) * scale).reshape(2 * bins, lags)
    table = table.astype(np.float32)
    high = table.astype(jnp.bfloat16)
    low = (table - high.astype(np.float32)).astype(jnp.bfloat16)
    return high, low


def pack_kernel(groups, per_dev, spectra_ref, out_ref, held_ref, rows_ref, arrived):
    chans, windows, width = held_ref.shape
    bins = width // 2
    head = bins // 2
    size = (per_dev + 1) * chans
    stride = size + 1
    fetches = arrived.shape[0]
    batch = chans // fetches
    copies = []
    for step in range(fetches):
        part = pl.ds(step * batch, batch)
        copies.append(pltpu.make_async_copy(spectra_ref.at[part], held_ref.at[part], arrived.at[step]))
        copies[-1].start()
    freq = (lax.broadcasted_iota(jnp.int32, (1, width), 1) % bins).astype(jnp.float32)
    taper = 0.54 - 0.46 * jnp.cos(2.0 * jnp.pi * (freq + 0.5) / bins)
    lane = lax.broadcasted_iota(jnp.int32, (windows - head, bins), 1)
    pick = lax.broadcasted_iota(jnp.int32, (groups, bins), 1) % groups
    pick = (pick == lax.broadcasted_iota(jnp.int32, (groups, bins), 0)).astype(jnp.float32).astype(jnp.bfloat16)

    def whiten_channel(ch):
        values = held_ref[ch].astype(jnp.float32)
        power = jnp.sum(values * values, axis=-1, keepdims=True) / bins + 1e-06
        return (values * taper * lax.rsqrt(power)).astype(jnp.bfloat16)

    def place_channel(ch, white):
        real, imag = white[:, :bins], white[:, bins:]
        main = jnp.concatenate([real[:head], imag[:head]], axis=0).astype(jnp.float32).T
        spread = []
        for slot in range(per_dev):
            chosen = lane // groups == slot
            spread += [jnp.where(chosen, part[head:], jnp.zeros_like(part[head:])) for part in (real, imag)]
        tail = lax.dot_general(
            pick, jnp.concatenate(spread, axis=0), (((1,), (1,)), ((), ())), preferred_element_type=jnp.float32
        )
        for slot in range(per_dev):
            part = main[slot * groups:(slot + 1) * groups]
            rows_ref[pl.ds(slot * chans + ch, groups, stride=stride), :] = part
        rows_ref[pl.ds(per_dev * chans + ch, groups, stride=stride), :] = tail

    ready = []
    for step in range(fetches):
        copies[step].wait()
        fresh = [(ch, whiten_channel(ch)) for ch in range(step * batch, (step + 1) * batch)]
        for ch, white in ready:
            place_channel(ch, white)
        ready = fresh
    for ch, white in ready:
        place_channel(ch, white)
    for first in range(0, groups, 4):
        rows = [rows_ref[pl.ds(group * stride, size), :].astype(jnp.bfloat16) for group in range(first, first + 4)]
        for place, part in enumerate(rows):
            out_ref[first + place] = part.reshape(out_ref.shape[1:])


def swap_parts(rows, half):
    lanes = rows.shape[-1]
    values = rows.astype(jnp.float32)
    lane = lax.broadcasted_iota(jnp.int32, values.shape, 1)
    first = (lane % (2 * half)) < half
    ahead = pltpu.roll(values, lanes - half, 1)
    behind = pltpu.roll(values, half, 1)
    return jnp.where(first, ahead, -behind).astype(jnp.bfloat16)


def cross_kernel(order, days, in_ref, out_ref):
    groups, parts, chans, lanes = in_ref.shape
    blocks = groups // days
    per_dev = parts - 1
    total = blocks * chans
    far = out_ref.shape[-1]
    narrow = lanes // per_dev // 2

    def rows(day, part):
        return jnp.concatenate([in_ref[order[block][day], part] for block in range(blocks)], axis=0)

    tails = [rows(day, per_dev) for day in range(days)]
    tails_swapped = [swap_parts(tail, narrow) for tail in tails]
    far_tail = jnp.concatenate(tails, axis=1)
    lane = lax.broadcasted_iota(jnp.int32, (2 * total, lanes), 1) // (2 * narrow)
    dims = (((1,), (1,)), ((), ()))
    for slot in range(per_dev):
        mains = [rows(day, slot) for day in range(days)]
        far_main = jnp.concatenate(mains, axis=1)
        turned = [swap_parts(m, lanes // 2) for m in mains]
        near_main = [jnp.concatenate(pair, axis=0) for pair in zip(mains, turned)]
        near_tail = [jnp.concatenate(pair, axis=0) for pair in zip(tails, tails_swapped)]
        near_tail = [jnp.where(lane == slot, t, jnp.zeros_like(t)) for t in near_tail]
        cross = lax.dot_general(
            jnp.concatenate(near_main, axis=1), far_main, dims, preferred_element_type=jnp.float32
        ) + lax.dot_general(
            jnp.concatenate(near_tail, axis=1), far_tail, dims, preferred_element_type=jnp.float32
        )
        cross = cross.astype(out_ref.dtype)
        for kind in range(2):
            for block in range(blocks):
                start = kind * total + block * chans
                for half in range(days):
                    piece = cross[start:start + chans, half * far:(half + 1) * far]
                    out_ref[order[block][half], 2 * slot + kind] = piece


def lags_kernel(cross_ref, high_ref, low_ref, out_ref, rows_ref, lag_ref, sent):
    far, chans, _ = out_ref.shape
    depth = high_ref.shape[0]
    table = jnp.concatenate([high_ref[...], low_ref[...]], axis=0)
    parts = sent.shape[0]
    batch = chans // parts
    stride = chans + 1
    for row in range(depth):
        rows_ref[pl.ds(row * stride, chans), :] = cross_ref[pl.ds(row * chans, chans), :].astype(jnp.float32)
    copies = []

    def load(first):
        part = [rows_ref[pl.ds(ch, depth, stride=stride), :].astype(jnp.bfloat16).T for ch in range(first, first + TALL)]
        part = jnp.concatenate(part, axis=0)
        return jnp.concatenate([part, part], axis=1)

    def store(first, lag):
        for place in range(TALL):
            lag_ref[:, first + place, :] = lag[place * far:(place + 1) * far]
        if (first + TALL) % batch == 0:
            step = first // batch
            done = pl.ds(step * batch, batch)
            copies.append(pltpu.make_async_copy(lag_ref.at[:, done], out_ref.at[:, done], sent.at[step]))
            copies[-1].start()

    part, lag = load(0), None
    for ch in range(0, chans, TALL):
        following = load(ch + TALL) if ch + TALL < chans else None
        fresh = jnp.dot(part, table, preferred_element_type=jnp.float32)
        if ch:
            store(ch - TALL, lag)
        part, lag = following, fresh
    store(chans - TALL, lag)
    for copy in copies:
        copy.wait()


def call(kernel, out_shape, scratch, in_spaces, out_space, *operands, vmem=VMEM_LIMIT):
    return pl.pallas_call(
        kernel,
        out_shape=out_shape,
        in_specs=[pl.BlockSpec(memory_space=space) for space in in_spaces],
        out_specs=pl.BlockSpec(memory_space=out_space),
        scratch_shapes=scratch,
        compiler_params=pltpu.CompilerParams(vmem_limit_bytes=vmem),
    )(*operands)


def shards(axes, order, spectra):
    _, chans, windows, width = spectra.shape
    bins = width // 2
    n_chan, n_day = order.shape
    groups = n_chan * n_day
    per_dev = bins // groups
    far = n_chan * chans // n_day

    packed = call(
        functools.partial(pack_kernel, groups, per_dev),
        jax.ShapeDtypeStruct((groups, per_dev + 1, chans, bins), jnp.bfloat16),
        [
            pltpu.VMEM((chans, windows, width), jnp.bfloat16),
            pltpu.VMEM((groups * ((per_dev + 1) * chans + 1), bins), jnp.float32),
            pltpu.SemaphoreType.DMA((FETCHES,)),
        ],
        [pltpu.HBM],
        pltpu.VMEM,
        spectra[0],
        vmem=PACK_VMEM_LIMIT,
    )
    mine = lax.all_to_all(packed, axes, 0, 0, tiled=True)
    cross = call(
        functools.partial(cross_kernel, order.tolist(), n_day),
        jax.ShapeDtypeStruct((groups, 2 * per_dev, chans, far), jnp.bfloat16),
        [],
        [pltpu.VMEM],
        pltpu.VMEM,
        mine,
    )
    cross = lax.all_to_all(cross, axes, 0, 0, tiled=True)
    high, low = lag_table(bins, per_dev, groups, 1.0 / (windows * n_day))
    return call(
        lags_kernel,
        jax.ShapeDtypeStruct((far, chans, width), jnp.float32),
        [
            pltpu.VMEM((width * (chans + 1), far), jnp.float32),
            pltpu.VMEM((far, chans, width), jnp.float32),
            pltpu.SemaphoreType.DMA((SENDS,)),
        ],
        [pltpu.VMEM] * 3,
        pltpu.HBM,
        cross.reshape(width * chans, far),
        jnp.asarray(high),
        jnp.asarray(low),
    )


def solution(mesh):
    n_chan, n_day = mesh.shape["chan"], mesh.shape["day"]
    outer = 4 if n_chan % 4 == 0 else 1
    inner = n_chan // outer
    split_mesh = jax.sharding.Mesh(mesh.devices.reshape(outer, inner, n_day), ("outer", "inner", "day"))
    order = np.arange(n_chan * n_day).reshape(n_day, inner, outer).transpose(2, 1, 0).reshape(n_chan, n_day)

    def run(spectra):
        bins = spectra.shape[-1] // 2
        if bins % (n_chan * n_day):
            return jax.shard_map(
                gathered_shards,
                mesh=mesh,
                in_specs=(P("day", "chan", None, None),),
                out_specs=P("day", "chan", None),
                check_vma=False,
            )(spectra)
        return jax.shard_map(
            functools.partial(shards, ("day", "inner", "outer"), order),
            mesh=split_mesh,
            in_specs=(P("day", ("outer", "inner"), None, None),),
            out_specs=P("day", ("outer", "inner"), None),
            check_vma=False,
        )(spectra)

    return run
```

```python
import functools

import jax
import jax.numpy as jnp
import numpy as np
from jax import lax
from jax.experimental import pallas as pl
from jax.experimental.pallas import tpu as pltpu
from jax.sharding import PartitionSpec as P

VMEM_LIMIT = 48 * 1024 * 1024
PACK_VMEM_LIMIT = 53 * 1024 * 1024
FETCHES = 2
SENDS = 2


def freq_taper(bins):
    freq_index = jnp.arange(bins, dtype=jnp.float32)
    half_taper = 0.54 - 0.46 * jnp.cos(2.0 * jnp.pi * (freq_index + 0.5) / bins)
    return jnp.concatenate([half_taper, half_taper])


def whiten(spectra):
    values = spectra.astype(jnp.float32)
    bins = values.shape[-1] // 2
    band_power = jnp.sum(values * values, axis=-1, keepdims=True) / bins + 1e-06
    return (values * freq_taper(bins) / jnp.sqrt(band_power)).astype(jnp.bfloat16)


def lag_matrix(bins):
    lag_count = 2 * bins
    freq_index = jnp.arange(bins, dtype=jnp.int32)
    lag_index = jnp.arange(lag_count, dtype=jnp.int32) - bins
    wound = jnp.mod(freq_index[:, None] * lag_index[None, :], lag_count)
    phase_angle = 2.0 * jnp.pi / lag_count * wound.astype(jnp.float32)
    return jnp.concatenate([jnp.cos(phase_angle), -jnp.sin(phase_angle)], axis=0)


def cross_spectra(far_rows, near_rows):
    bins = far_rows.shape[-1] // 2
    windows = far_rows.shape[-2]
    far_re, far_im = (far_rows[..., :bins], far_rows[..., bins:])
    near_re, near_im = (near_rows[..., :bins], near_rows[..., bins:])
    real_part = jnp.einsum("jwf,iwf->jif", far_re, near_re, preferred_element_type=jnp.float32)
    real_part = real_part + jnp.einsum(
        "jwf,iwf->jif", far_im, near_im, preferred_element_type=jnp.float32
    )
    imag_part = jnp.einsum("jwf,iwf->jif", far_re, near_im, preferred_element_type=jnp.float32)
    imag_part = imag_part - jnp.einsum(
        "jwf,iwf->jif", far_im, near_re, preferred_element_type=jnp.float32
    )
    return jnp.concatenate([real_part, imag_part], axis=-1) / windows


def to_lags(cross, table):
    flat = cross.reshape(-1, cross.shape[-1])
    lagged = jnp.dot(
        flat, table, precision=lax.Precision.HIGHEST, preferred_element_type=jnp.float32
    )
    return lagged.reshape(cross.shape[:-1] + (table.shape[1],))


def gathered_shards(spectra):
    local_white = whiten(spectra)[0]
    gathered = lax.all_gather(local_white, "chan", axis=0, tiled=True)
    table = lag_matrix(local_white.shape[-1] // 2)
    day_count = lax.axis_size("day")
    return lax.psum_scatter(
        to_lags(cross_spectra(gathered, local_white), table) / day_count,
        "day",
        scatter_dimension=0,
        tiled=True,
    )


def lag_table(bins, per_dev, groups, scale):
    lags = 2 * bins
    freq = (np.arange(per_dev)[None, :] * groups + np.arange(groups)[:, None]).reshape(-1)
    wound = (freq[:, None] * (np.arange(lags)[None, :] - bins)) % lags
    angle = 2.0 * np.pi / lags * wound
    table = (np.stack([np.cos(angle), -np.sin(angle)], axis=1) * scale).reshape(2 * bins, lags)
    table = table.astype(np.float32)
    high = table.astype(jnp.bfloat16)
    low = (table - high.astype(np.float32)).astype(jnp.bfloat16)
    return high, low


def pack_kernel(groups, per_dev, spectra_ref, out_ref, held_ref, rows_ref, arrived):
    chans, windows, width = held_ref.shape
    bins = width // 2
    head = bins // 2
    size = (per_dev + 1) * chans
    stride = size + 1
    fetches = arrived.shape[0]
    batch = chans // fetches
    copies = []
    for step in range(fetches):
        part = pl.ds(step * batch, batch)
        copies.append(pltpu.make_async_copy(spectra_ref.at[part], held_ref.at[part], arrived.at[step]))
        copies[-1].start()
    freq = (lax.broadcasted_iota(jnp.int32, (1, width), 1) % bins).astype(jnp.float32)
    taper = 0.54 - 0.46 * jnp.cos(2.0 * jnp.pi * (freq + 0.5) / bins)
    lane = lax.broadcasted_iota(jnp.int32, (windows - head, bins), 1)
    pick = lax.broadcasted_iota(jnp.int32, (groups, bins), 1) % groups
    pick = (pick == lax.broadcasted_iota(jnp.int32, (groups, bins), 0)).astype(jnp.float32).astype(jnp.bfloat16)

    def whiten_channel(ch):
        values = held_ref[ch].astype(jnp.float32)
        power = jnp.sum(values * values, axis=-1, keepdims=True) / bins + 1e-06
        return (values * taper * lax.rsqrt(power)).astype(jnp.bfloat16)

    def place_channel(ch, white):
        real, imag = white[:, :bins], white[:, bins:]
        main = jnp.concatenate([real[:head], imag[:head]], axis=0).astype(jnp.float32).T
        spread = []
        for slot in range(per_dev):
            chosen = lane // groups == slot
            spread += [jnp.where(chosen, part[head:], jnp.zeros_like(part[head:])) for part in (real, imag)]
        tail = lax.dot_general(
            pick, jnp.concatenate(spread, axis=0), (((1,), (1,)), ((), ())), preferred_element_type=jnp.float32
        )
        for slot in range(per_dev):
            part = main[slot * groups:(slot + 1) * groups]
            rows_ref[pl.ds(slot * chans + ch, groups, stride=stride), :] = part
        rows_ref[pl.ds(per_dev * chans + ch, groups, stride=stride), :] = tail

    ready = []
    for step in range(fetches):
        copies[step].wait()
        fresh = [(ch, whiten_channel(ch)) for ch in range(step * batch, (step + 1) * batch)]
        for ch, white in ready:
            place_channel(ch, white)
        early = batch // 2 if step + 1 < fetches else 0
        for ch, white in fresh[:early]:
            place_channel(ch, white)
        ready = fresh[early:]
    for ch, white in ready:
        place_channel(ch, white)
    for first in range(0, groups, 8):
        rows = [rows_ref[pl.ds(group * stride, size), :].astype(jnp.bfloat16) for group in range(first, first + 8)]
        for place, part in enumerate(rows):
            out_ref[first + place] = part.reshape(out_ref.shape[1:])


def swap_parts(rows, half):
    lanes = rows.shape[-1]
    values = rows.astype(jnp.float32)
    lane = lax.broadcasted_iota(jnp.int32, values.shape, 1)
    first = (lane % (2 * half)) < half
    ahead = pltpu.roll(values, lanes - half, 1)
    behind = pltpu.roll(values, half, 1)
    return jnp.where(first, ahead, -behind).astype(jnp.bfloat16)


def cross_kernel(order, days, in_ref, out_ref):
    groups, parts, chans, lanes = in_ref.shape
    blocks = groups // days
    per_dev = parts - 1
    total = blocks * chans
    far = out_ref.shape[-1]
    narrow = lanes // per_dev // 2

    def rows(day, part):
        return jnp.concatenate([in_ref[order[block][day], part] for block in range(blocks)], axis=0)

    tails = [rows(day, per_dev) for day in range(days)]
    tails_swapped = [swap_parts(tail, narrow) for tail in tails]
    far_tail = jnp.concatenate(tails, axis=1)
    lane = lax.broadcasted_iota(jnp.int32, (2 * total, lanes), 1) // (2 * narrow)
    dims = (((1,), (1,)), ((), ()))
    for slot in range(per_dev):
        mains = [rows(day, slot) for day in range(days)]
        far_main = jnp.concatenate(mains, axis=1)
        turned = [swap_parts(m, lanes // 2) for m in mains]
        near_main = [jnp.concatenate(pair, axis=0) for pair in zip(mains, turned)]
        near_tail = [jnp.concatenate(pair, axis=0) for pair in zip(tails, tails_swapped)]
        near_tail = [jnp.where(lane == slot, t, jnp.zeros_like(t)) for t in near_tail]
        cross = lax.dot_general(
            jnp.concatenate(near_main, axis=1), far_main, dims, preferred_element_type=jnp.float32
        ) + lax.dot_general(
            jnp.concatenate(near_tail, axis=1), far_tail, dims, preferred_element_type=jnp.float32
        )
        cross = cross.astype(out_ref.dtype)
        for kind in range(2):
            for block in range(blocks):
                start = kind * total + block * chans
                for half in range(days):
                    piece = cross[start:start + chans, half * far:(half + 1) * far]
                    out_ref[order[block][half], 2 * slot + kind] = piece


def lags_kernel(cross_ref, high_ref, low_ref, out_ref, rows_ref, lag_ref, sent):
    chans = out_ref.shape[1]
    depth = high_ref.shape[0]
    high, low = high_ref[...], low_ref[...]
    dims = (((0,), (0,)), ((), ()))
    parts = sent.shape[0]
    batch = chans // parts
    stride = chans + 1
    for row in range(depth):
        rows_ref[pl.ds(row * stride, chans), :] = cross_ref[pl.ds(row * chans, chans), :].astype(jnp.float32)
    copies = []

    def load(ch):
        return rows_ref[pl.ds(ch, depth, stride=stride), :].astype(jnp.bfloat16)

    def store(ch, lag):
        lag_ref[:, ch, :] = lag
        if (ch + 1) % batch == 0:
            step = ch // batch
            done = pl.ds(step * batch, batch)
            copies.append(pltpu.make_async_copy(lag_ref.at[:, done], out_ref.at[:, done], sent.at[step]))
            copies[-1].start()

    part, lag = load(0), None
    for ch in range(chans):
        following = load(ch + 1) if ch + 1 < chans else None
        fresh = lax.dot_general(part, high, dims, preferred_element_type=jnp.float32)
        fresh = fresh + lax.dot_general(part, low, dims, preferred_element_type=jnp.float32)
        if ch:
            store(ch - 1, lag)
        part, lag = following, fresh
    store(chans - 1, lag)
    for copy in copies:
        copy.wait()


def call(kernel, out_shape, scratch, in_spaces, out_space, *operands, vmem=VMEM_LIMIT):
    return pl.pallas_call(
        kernel,
        out_shape=out_shape,
        in_specs=[pl.BlockSpec(memory_space=space) for space in in_spaces],
        out_specs=pl.BlockSpec(memory_space=out_space),
        scratch_shapes=scratch,
        compiler_params=pltpu.CompilerParams(vmem_limit_bytes=vmem),
    )(*operands)


def shards(axes, order, spectra):
    _, chans, windows, width = spectra.shape
    bins = width // 2
    n_chan, n_day = order.shape
    groups = n_chan * n_day
    per_dev = bins // groups
    far = n_chan * chans // n_day

    packed = call(
        functools.partial(pack_kernel, groups, per_dev),
        jax.ShapeDtypeStruct((groups, per_dev + 1, chans, bins), jnp.bfloat16),
        [
            pltpu.VMEM((chans, windows, width), jnp.bfloat16),
            pltpu.VMEM((groups * ((per_dev + 1) * chans + 1), bins), jnp.float32),
            pltpu.SemaphoreType.DMA((FETCHES,)),
        ],
        [pltpu.HBM],
        pltpu.VMEM,
        spectra[0],
        vmem=PACK_VMEM_LIMIT,
    )
    mine = lax.all_to_all(packed, axes, 0, 0, tiled=True)
    cross = call(
        functools.partial(cross_kernel, order.tolist(), n_day),
        jax.ShapeDtypeStruct((groups, 2 * per_dev, chans, far), jnp.bfloat16),
        [],
        [pltpu.VMEM],
        pltpu.VMEM,
        mine,
    )
    cross = lax.all_to_all(cross, axes, 0, 0, tiled=True)
    high, low = lag_table(bins, per_dev, groups, 1.0 / (windows * n_day))
    return call(
        lags_kernel,
        jax.ShapeDtypeStruct((far, chans, width), jnp.float32),
        [
            pltpu.VMEM((width * (chans + 1), far), jnp.float32),
            pltpu.VMEM((far, chans, width), jnp.float32),
            pltpu.SemaphoreType.DMA((SENDS,)),
        ],
        [pltpu.VMEM] * 3,
        pltpu.HBM,
        cross.reshape(width * chans, far),
        jnp.asarray(high),
        jnp.asarray(low),
    )


def solution(mesh):
    n_chan, n_day = mesh.shape["chan"], mesh.shape["day"]
    outer = 4 if n_chan % 4 == 0 else 1
    inner = n_chan // outer
    split_mesh = jax.sharding.Mesh(mesh.devices.reshape(outer, inner, n_day), ("outer", "inner", "day"))
    order = np.arange(n_chan * n_day).reshape(n_day, inner, outer).transpose(2, 1, 0).reshape(n_chan, n_day)

    def run(spectra):
        bins = spectra.shape[-1] // 2
        if bins % (n_chan * n_day):
            return jax.shard_map(
                gathered_shards,
                mesh=mesh,
                in_specs=(P("day", "chan", None, None),),
                out_specs=P("day", "chan", None),
                check_vma=False,
            )(spectra)
        return jax.shard_map(
            functools.partial(shards, ("day", "inner", "outer"), order),
            mesh=split_mesh,
            in_specs=(P("day", ("outer", "inner"), None, None),),
            out_specs=P("day", ("outer", "inner"), None),
            check_vma=False,
        )(spectra)

    return run
```

```python
import functools

import jax
import jax.numpy as jnp
import numpy as np
from jax import lax
from jax.experimental import pallas as pl
from jax.experimental.pallas import tpu as pltpu
from jax.sharding import PartitionSpec as P

VMEM_LIMIT = 48 * 1024 * 1024
PACK_VMEM_LIMIT = 53 * 1024 * 1024
FETCHES = 2
SENDS = 2


def freq_taper(bins):
    freq_index = jnp.arange(bins, dtype=jnp.float32)
    half_taper = 0.54 - 0.46 * jnp.cos(2.0 * jnp.pi * (freq_index + 0.5) / bins)
    return jnp.concatenate([half_taper, half_taper])


def whiten(spectra):
    values = spectra.astype(jnp.float32)
    bins = values.shape[-1] // 2
    band_power = jnp.sum(values * values, axis=-1, keepdims=True) / bins + 1e-06
    return (values * freq_taper(bins) / jnp.sqrt(band_power)).astype(jnp.bfloat16)


def lag_matrix(bins):
    lag_count = 2 * bins
    freq_index = jnp.arange(bins, dtype=jnp.int32)
    lag_index = jnp.arange(lag_count, dtype=jnp.int32) - bins
    wound = jnp.mod(freq_index[:, None] * lag_index[None, :], lag_count)
    phase_angle = 2.0 * jnp.pi / lag_count * wound.astype(jnp.float32)
    return jnp.concatenate([jnp.cos(phase_angle), -jnp.sin(phase_angle)], axis=0)


def cross_spectra(far_rows, near_rows):
    bins = far_rows.shape[-1] // 2
    windows = far_rows.shape[-2]
    far_re, far_im = (far_rows[..., :bins], far_rows[..., bins:])
    near_re, near_im = (near_rows[..., :bins], near_rows[..., bins:])
    real_part = jnp.einsum("jwf,iwf->jif", far_re, near_re, preferred_element_type=jnp.float32)
    real_part = real_part + jnp.einsum(
        "jwf,iwf->jif", far_im, near_im, preferred_element_type=jnp.float32
    )
    imag_part = jnp.einsum("jwf,iwf->jif", far_re, near_im, preferred_element_type=jnp.float32)
    imag_part = imag_part - jnp.einsum(
        "jwf,iwf->jif", far_im, near_re, preferred_element_type=jnp.float32
    )
    return jnp.concatenate([real_part, imag_part], axis=-1) / windows


def to_lags(cross, table):
    flat = cross.reshape(-1, cross.shape[-1])
    lagged = jnp.dot(
        flat, table, precision=lax.Precision.HIGHEST, preferred_element_type=jnp.float32
    )
    return lagged.reshape(cross.shape[:-1] + (table.shape[1],))


def gathered_shards(spectra):
    local_white = whiten(spectra)[0]
    gathered = lax.all_gather(local_white, "chan", axis=0, tiled=True)
    table = lag_matrix(local_white.shape[-1] // 2)
    day_count = lax.axis_size("day")
    return lax.psum_scatter(
        to_lags(cross_spectra(gathered, local_white), table) / day_count,
        "day",
        scatter_dimension=0,
        tiled=True,
    )


def lag_table(bins, per_dev, groups, scale):
    lags = 2 * bins
    freq = (np.arange(per_dev)[None, :] * groups + np.arange(groups)[:, None]).reshape(-1)
    wound = (freq[:, None] * (np.arange(lags)[None, :] - bins)) % lags
    angle = 2.0 * np.pi / lags * wound
    table = (np.stack([np.cos(angle), -np.sin(angle)], axis=1) * scale).reshape(2 * bins, lags)
    table = table.astype(np.float32)
    high = table.astype(jnp.bfloat16)
    low = (table - high.astype(np.float32)).astype(jnp.bfloat16)
    return high, low


def pack_kernel(groups, per_dev, spectra_ref, out_ref, held_ref, rows_ref, arrived):
    chans, windows, width = held_ref.shape
    bins = width // 2
    head = bins // 2
    size = (per_dev + 1) * chans
    stride = size + 1
    fetches = arrived.shape[0]
    batch = chans // fetches
    copies = []
    for step in range(fetches):
        part = pl.ds(step * batch, batch)
        copies.append(pltpu.make_async_copy(spectra_ref.at[part], held_ref.at[part], arrived.at[step]))
        copies[-1].start()
    freq = (lax.broadcasted_iota(jnp.int32, (1, width), 1) % bins).astype(jnp.float32)
    taper = 0.54 - 0.46 * jnp.cos(2.0 * jnp.pi * (freq + 0.5) / bins)
    lane = lax.broadcasted_iota(jnp.int32, (windows - head, bins), 1)
    pick = lax.broadcasted_iota(jnp.int32, (groups, bins), 1) % groups
    pick = (pick == lax.broadcasted_iota(jnp.int32, (groups, bins), 0)).astype(jnp.float32).astype(jnp.bfloat16)

    def whiten_channel(ch):
        values = held_ref[ch].astype(jnp.float32)
        power = jnp.sum(values * values, axis=-1, keepdims=True) / bins + 1e-06
        return (values * taper * lax.rsqrt(power)).astype(jnp.bfloat16)

    def place_channel(ch, white):
        real, imag = white[:, :bins], white[:, bins:]
        main = jnp.concatenate([real[:head], imag[:head]], axis=0).astype(jnp.float32).T
        spread = []
        for slot in range(per_dev):
            chosen = lane // groups == slot
            spread += [jnp.where(chosen, part[head:], jnp.zeros_like(part[head:])) for part in (real, imag)]
        tail = lax.dot_general(
            pick, jnp.concatenate(spread, axis=0), (((1,), (1,)), ((), ())), preferred_element_type=jnp.float32
        )
        for slot in range(per_dev):
            part = main[slot * groups:(slot + 1) * groups]
            rows_ref[pl.ds(slot * chans + ch, groups, stride=stride), :] = part
        rows_ref[pl.ds(per_dev * chans + ch, groups, stride=stride), :] = tail

    ready = []
    for step in range(fetches):
        copies[step].wait()
        fresh = [(ch, whiten_channel(ch)) for ch in range(step * batch, (step + 1) * batch)]
        for ch, white in ready:
            place_channel(ch, white)
        ready = fresh
    for ch, white in ready:
        place_channel(ch, white)
    for first in range(0, groups, 4):
        rows = [rows_ref[pl.ds(group * stride, size), :].astype(jnp.bfloat16) for group in range(first, first + 4)]
        for place, part in enumerate(rows):
            out_ref[first + place] = part.reshape(out_ref.shape[1:])


def swap_parts(rows, half):
    lanes = rows.shape[-1]
    values = rows.astype(jnp.float32)
    lane = lax.broadcasted_iota(jnp.int32, values.shape, 1)
    first = (lane % (2 * half)) < half
    ahead = pltpu.roll(values, lanes - half, 1)
    behind = pltpu.roll(values, half, 1)
    return jnp.where(first, ahead, -behind).astype(jnp.bfloat16)


def cross_kernel(order, days, in_ref, out_ref):
    groups, parts, chans, lanes = in_ref.shape
    blocks = groups // days
    per_dev = parts - 1
    total = blocks * chans
    far = out_ref.shape[-1]
    narrow = lanes // per_dev // 2

    def rows(day, part):
        return jnp.concatenate([in_ref[order[block][day], part] for block in range(blocks)], axis=0)

    tails = [rows(day, per_dev) for day in range(days)]
    tails_swapped = [swap_parts(tail, narrow) for tail in tails]
    lane = lax.broadcasted_iota(jnp.int32, (2 * total, lanes), 1) // (2 * narrow)
    dims = (((1,), (1,)), ((), ()))
    for slot in range(per_dev):
        mains = [rows(day, slot) for day in range(days)]
        far_rows = jnp.concatenate(mains + tails, axis=1)
        turned = [swap_parts(m, lanes // 2) for m in mains]
        near_main = [jnp.concatenate(pair, axis=0) for pair in zip(mains, turned)]
        near_tail = [jnp.concatenate(pair, axis=0) for pair in zip(tails, tails_swapped)]
        near_tail = [jnp.where(lane == slot, t, jnp.zeros_like(t)) for t in near_tail]
        near = jnp.concatenate(near_main + near_tail, axis=1)
        cross = lax.dot_general(near, far_rows, dims, preferred_element_type=jnp.float32)
        cross = cross.astype(out_ref.dtype)
        for kind in range(2):
            for block in range(blocks):
                start = kind * total + block * chans
                for half in range(days):
                    piece = cross[start:start + chans, half * far:(half + 1) * far]
                    out_ref[order[block][half], 2 * slot + kind] = piece


def lags_kernel(cross_ref, high_ref, low_ref, out_ref, rows_ref, lag_ref, sent):
    chans = out_ref.shape[1]
    depth = high_ref.shape[0]
    high, low = high_ref[...], low_ref[...]
    dims = (((0,), (0,)), ((), ()))
    parts = sent.shape[0]
    batch = chans // parts
    stride = chans + 1
    for row in range(depth):
        rows_ref[pl.ds(row * stride, chans), :] = cross_ref[pl.ds(row * chans, chans), :].astype(jnp.float32)
    copies = []

    def load(ch):
        return rows_ref[pl.ds(ch, depth, stride=stride), :].astype(jnp.bfloat16)

    def store(ch, lag):
        lag_ref[:, ch, :] = lag
        if (ch + 1) % batch == 0:
            step = ch // batch
            done = pl.ds(step * batch, batch)
            copies.append(pltpu.make_async_copy(lag_ref.at[:, done], out_ref.at[:, done], sent.at[step]))
            copies[-1].start()

    part, lag = load(0), None
    for ch in range(chans):
        following = load(ch + 1) if ch + 1 < chans else None
        fresh = lax.dot_general(part, high, dims, preferred_element_type=jnp.float32)
        fresh = fresh + lax.dot_general(part, low, dims, preferred_element_type=jnp.float32)
        if ch:
            store(ch - 1, lag)
        part, lag = following, fresh
    store(chans - 1, lag)
    for copy in copies:
        copy.wait()


def call(kernel, out_shape, scratch, in_spaces, out_space, *operands, vmem=VMEM_LIMIT):
    return pl.pallas_call(
        kernel,
        out_shape=out_shape,
        in_specs=[pl.BlockSpec(memory_space=space) for space in in_spaces],
        out_specs=pl.BlockSpec(memory_space=out_space),
        scratch_shapes=scratch,
        compiler_params=pltpu.CompilerParams(vmem_limit_bytes=vmem),
    )(*operands)


def shards(axes, order, spectra):
    _, chans, windows, width = spectra.shape
    bins = width // 2
    n_chan, n_day = order.shape
    groups = n_chan * n_day
    per_dev = bins // groups
    far = n_chan * chans // n_day

    packed = call(
        functools.partial(pack_kernel, groups, per_dev),
        jax.ShapeDtypeStruct((groups, per_dev + 1, chans, bins), jnp.bfloat16),
        [
            pltpu.VMEM((chans, windows, width), jnp.bfloat16),
            pltpu.VMEM((groups * ((per_dev + 1) * chans + 1), bins), jnp.float32),
            pltpu.SemaphoreType.DMA((FETCHES,)),
        ],
        [pltpu.HBM],
        pltpu.VMEM,
        spectra[0],
        vmem=PACK_VMEM_LIMIT,
    )
    mine = lax.all_to_all(packed, axes, 0, 0, tiled=True)
    cross = call(
        functools.partial(cross_kernel, order.tolist(), n_day),
        jax.ShapeDtypeStruct((groups, 2 * per_dev, chans, far), jnp.bfloat16),
        [],
        [pltpu.VMEM],
        pltpu.VMEM,
        mine,
    )
    cross = lax.all_to_all(cross, axes, 0, 0, tiled=True)
    high, low = lag_table(bins, per_dev, groups, 1.0 / (windows * n_day))
    return call(
        lags_kernel,
        jax.ShapeDtypeStruct((far, chans, width), jnp.float32),
        [
            pltpu.VMEM((width * (chans + 1), far), jnp.float32),
            pltpu.VMEM((far, chans, width), jnp.float32),
            pltpu.SemaphoreType.DMA((SENDS,)),
        ],
        [pltpu.VMEM] * 3,
        pltpu.HBM,
        cross.reshape(width * chans, far),
        jnp.asarray(high),
        jnp.asarray(low),
    )


def solution(mesh):
    n_chan, n_day = mesh.shape["chan"], mesh.shape["day"]
    outer = 4 if n_chan % 4 == 0 else 1
    inner = n_chan // outer
    split_mesh = jax.sharding.Mesh(mesh.devices.reshape(outer, inner, n_day), ("outer", "inner", "day"))
    order = np.arange(n_chan * n_day).reshape(n_day, inner, outer).transpose(2, 1, 0).reshape(n_chan, n_day)

    def run(spectra):
        bins = spectra.shape[-1] // 2
        if bins % (n_chan * n_day):
            return jax.shard_map(
                gathered_shards,
                mesh=mesh,
                in_specs=(P("day", "chan", None, None),),
                out_specs=P("day", "chan", None),
                check_vma=False,
            )(spectra)
        return jax.shard_map(
            functools.partial(shards, ("day", "inner", "outer"), order),
            mesh=split_mesh,
            in_specs=(P("day", ("outer", "inner"), None, None),),
            out_specs=P("day", ("outer", "inner"), None),
            check_vma=False,
        )(spectra)

    return run
```

```python
import functools

import jax
import jax.numpy as jnp
import numpy as np
from jax import lax
from jax.experimental import pallas as pl
from jax.experimental.pallas import tpu as pltpu
from jax.sharding import PartitionSpec as P

VMEM_LIMIT = 48 * 1024 * 1024
PACK_VMEM_LIMIT = 53 * 1024 * 1024
FETCHES = 2
SENDS = 2


def freq_taper(bins):
    freq_index = jnp.arange(bins, dtype=jnp.float32)
    half_taper = 0.54 - 0.46 * jnp.cos(2.0 * jnp.pi * (freq_index + 0.5) / bins)
    return jnp.concatenate([half_taper, half_taper])


def whiten(spectra):
    values = spectra.astype(jnp.float32)
    bins = values.shape[-1] // 2
    band_power = jnp.sum(values * values, axis=-1, keepdims=True) / bins + 1e-06
    return (values * freq_taper(bins) / jnp.sqrt(band_power)).astype(jnp.bfloat16)


def lag_matrix(bins):
    lag_count = 2 * bins
    freq_index = jnp.arange(bins, dtype=jnp.int32)
    lag_index = jnp.arange(lag_count, dtype=jnp.int32) - bins
    wound = jnp.mod(freq_index[:, None] * lag_index[None, :], lag_count)
    phase_angle = 2.0 * jnp.pi / lag_count * wound.astype(jnp.float32)
    return jnp.concatenate([jnp.cos(phase_angle), -jnp.sin(phase_angle)], axis=0)


def cross_spectra(far_rows, near_rows):
    bins = far_rows.shape[-1] // 2
    windows = far_rows.shape[-2]
    far_re, far_im = (far_rows[..., :bins], far_rows[..., bins:])
    near_re, near_im = (near_rows[..., :bins], near_rows[..., bins:])
    real_part = jnp.einsum("jwf,iwf->jif", far_re, near_re, preferred_element_type=jnp.float32)
    real_part = real_part + jnp.einsum(
        "jwf,iwf->jif", far_im, near_im, preferred_element_type=jnp.float32
    )
    imag_part = jnp.einsum("jwf,iwf->jif", far_re, near_im, preferred_element_type=jnp.float32)
    imag_part = imag_part - jnp.einsum(
        "jwf,iwf->jif", far_im, near_re, preferred_element_type=jnp.float32
    )
    return jnp.concatenate([real_part, imag_part], axis=-1) / windows


def to_lags(cross, table):
    flat = cross.reshape(-1, cross.shape[-1])
    lagged = jnp.dot(
        flat, table, precision=lax.Precision.HIGHEST, preferred_element_type=jnp.float32
    )
    return lagged.reshape(cross.shape[:-1] + (table.shape[1],))


def gathered_shards(spectra):
    local_white = whiten(spectra)[0]
    gathered = lax.all_gather(local_white, "chan", axis=0, tiled=True)
    table = lag_matrix(local_white.shape[-1] // 2)
    day_count = lax.axis_size("day")
    return lax.psum_scatter(
        to_lags(cross_spectra(gathered, local_white), table) / day_count,
        "day",
        scatter_dimension=0,
        tiled=True,
    )


def lag_table(bins, per_dev, groups, scale):
    lags = 2 * bins
    freq = (np.arange(per_dev)[None, :] * groups + np.arange(groups)[:, None]).reshape(-1)
    wound = (freq[:, None] * (np.arange(lags)[None, :] - bins)) % lags
    angle = 2.0 * np.pi / lags * wound
    table = (np.stack([np.cos(angle), -np.sin(angle)], axis=1) * scale).reshape(2 * bins, lags)
    table = table.astype(np.float32)
    high = table.astype(jnp.bfloat16)
    low = (table - high.astype(np.float32)).astype(jnp.bfloat16)
    return high, low


def pack_kernel(groups, per_dev, spectra_ref, out_ref, held_ref, rows_ref, arrived):
    chans, windows, width = held_ref.shape
    bins = width // 2
    head = bins // 2
    size = (per_dev + 1) * chans
    stride = size + 1
    fetches = arrived.shape[0]
    batch = chans // fetches
    copies = []
    for step in range(fetches):
        part = pl.ds(step * batch, batch)
        copies.append(pltpu.make_async_copy(spectra_ref.at[part], held_ref.at[part], arrived.at[step]))
        copies[-1].start()
    freq = (lax.broadcasted_iota(jnp.int32, (1, width), 1) % bins).astype(jnp.float32)
    taper = 0.54 - 0.46 * jnp.cos(2.0 * jnp.pi * (freq + 0.5) / bins)
    lane = lax.broadcasted_iota(jnp.int32, (windows - head, bins), 1)
    pick = lax.broadcasted_iota(jnp.int32, (groups, bins), 1) % groups
    pick = (pick == lax.broadcasted_iota(jnp.int32, (groups, bins), 0)).astype(jnp.float32).astype(jnp.bfloat16)

    def whiten_channel(ch):
        values = held_ref[ch].astype(jnp.float32)
        power = jnp.sum(values * values, axis=-1, keepdims=True) / bins + 1e-06
        return (values * taper * lax.rsqrt(power)).astype(jnp.bfloat16)

    def place_channel(ch, white):
        real, imag = white[:, :bins], white[:, bins:]
        main = jnp.concatenate([real[:head], imag[:head]], axis=0).astype(jnp.float32).T
        spread = []
        for slot in range(per_dev):
            chosen = lane // groups == slot
            spread += [jnp.where(chosen, part[head:], jnp.zeros_like(part[head:])) for part in (real, imag)]
        tail = lax.dot_general(
            pick, jnp.concatenate(spread, axis=0), (((1,), (1,)), ((), ())), preferred_element_type=jnp.float32
        )
        for slot in range(per_dev):
            part = main[slot * groups:(slot + 1) * groups]
            rows_ref[pl.ds(slot * chans + ch, groups, stride=stride), :] = part
        rows_ref[pl.ds(per_dev * chans + ch, groups, stride=stride), :] = tail

    ready = []
    for step in range(fetches):
        copies[step].wait()
        fresh = [(ch, whiten_channel(ch)) for ch in range(step * batch, (step + 1) * batch)]
        for ch, white in ready:
            place_channel(ch, white)
        ready = fresh
    for ch, white in ready:
        place_channel(ch, white)
    for first in range(0, groups, 4):
        rows = [rows_ref[pl.ds(group * stride, size), :].astype(jnp.bfloat16) for group in range(first, first + 4)]
        for place, part in enumerate(rows):
            out_ref[first + place] = part.reshape(out_ref.shape[1:])


def swap_parts(rows, half):
    lanes = rows.shape[-1]
    values = rows.astype(jnp.float32)
    lane = lax.broadcasted_iota(jnp.int32, values.shape, 1)
    first = (lane % (2 * half)) < half
    ahead = pltpu.roll(values, lanes - half, 1)
    behind = pltpu.roll(values, half, 1)
    return jnp.where(first, ahead, -behind).astype(jnp.bfloat16)


def cross_kernel(order, days, in_ref, out_ref):
    groups, parts, chans, lanes = in_ref.shape
    blocks = groups // days
    per_dev = parts - 1
    total = blocks * chans
    far = out_ref.shape[-1]
    narrow = lanes // per_dev // 2

    def rows(day, part):
        return jnp.concatenate([in_ref[order[block][day], part] for block in range(blocks)], axis=0)

    tails = [rows(day, per_dev) for day in range(days)]
    tails_swapped = [swap_parts(tail, narrow) for tail in tails]
    near_tail = [jnp.concatenate(pair, axis=0) for pair in zip(tails, tails_swapped)]
    lane = lax.broadcasted_iota(jnp.int32, (total, lanes), 1) // (2 * narrow)
    dims = (((1,), (1,)), ((), ()))
    for slot in range(per_dev):
        mains = [rows(day, slot) for day in range(days)]
        chosen = [jnp.where(lane == slot, t, jnp.zeros_like(t)) for t in tails]
        far_rows = jnp.concatenate(mains + chosen, axis=1)
        turned = [swap_parts(m, lanes // 2) for m in mains]
        near_main = [jnp.concatenate(pair, axis=0) for pair in zip(mains, turned)]
        near = jnp.concatenate(near_main + near_tail, axis=1)
        cross = lax.dot_general(near, far_rows, dims, preferred_element_type=jnp.float32)
        cross = cross.astype(out_ref.dtype)
        for kind in range(2):
            for block in range(blocks):
                start = kind * total + block * chans
                for half in range(days):
                    piece = cross[start:start + chans, half * far:(half + 1) * far]
                    out_ref[order[block][half], 2 * slot + kind] = piece


def lags_kernel(cross_ref, high_ref, low_ref, out_ref, rows_ref, lag_ref, sent):
    chans = out_ref.shape[1]
    depth = high_ref.shape[0]
    high, low = high_ref[...], low_ref[...]
    dims = (((0,), (0,)), ((), ()))
    parts = sent.shape[0]
    batch = chans // parts
    stride = chans + 1
    for row in range(depth):
        rows_ref[pl.ds(row * stride, chans), :] = cross_ref[pl.ds(row * chans, chans), :].astype(jnp.float32)
    copies = []

    def load(ch):
        return rows_ref[pl.ds(ch, depth, stride=stride), :].astype(jnp.bfloat16)

    def store(ch, lag):
        lag_ref[:, ch, :] = lag
        if (ch + 1) % batch == 0:
            step = ch // batch
            done = pl.ds(step * batch, batch)
            copies.append(pltpu.make_async_copy(lag_ref.at[:, done], out_ref.at[:, done], sent.at[step]))
            copies[-1].start()

    part, lag = load(0), None
    for ch in range(chans):
        following = load(ch + 1) if ch + 1 < chans else None
        fresh = lax.dot_general(part, high, dims, preferred_element_type=jnp.float32)
        fresh = fresh + lax.dot_general(part, low, dims, preferred_element_type=jnp.float32)
        if ch:
            store(ch - 1, lag)
        part, lag = following, fresh
    store(chans - 1, lag)
    for copy in copies:
        copy.wait()


def call(kernel, out_shape, scratch, in_spaces, out_space, *operands, vmem=VMEM_LIMIT):
    return pl.pallas_call(
        kernel,
        out_shape=out_shape,
        in_specs=[pl.BlockSpec(memory_space=space) for space in in_spaces],
        out_specs=pl.BlockSpec(memory_space=out_space),
        scratch_shapes=scratch,
        compiler_params=pltpu.CompilerParams(vmem_limit_bytes=vmem),
    )(*operands)


def shards(axes, order, spectra):
    _, chans, windows, width = spectra.shape
    bins = width // 2
    n_chan, n_day = order.shape
    groups = n_chan * n_day
    per_dev = bins // groups
    far = n_chan * chans // n_day

    packed = call(
        functools.partial(pack_kernel, groups, per_dev),
        jax.ShapeDtypeStruct((groups, per_dev + 1, chans, bins), jnp.bfloat16),
        [
            pltpu.VMEM((chans, windows, width), jnp.bfloat16),
            pltpu.VMEM((groups * ((per_dev + 1) * chans + 1), bins), jnp.float32),
            pltpu.SemaphoreType.DMA((FETCHES,)),
        ],
        [pltpu.HBM],
        pltpu.VMEM,
        spectra[0],
        vmem=PACK_VMEM_LIMIT,
    )
    mine = lax.all_to_all(packed, axes, 0, 0, tiled=True)
    cross = call(
        functools.partial(cross_kernel, order.tolist(), n_day),
        jax.ShapeDtypeStruct((groups, 2 * per_dev, chans, far), jnp.bfloat16),
        [],
        [pltpu.VMEM],
        pltpu.VMEM,
        mine,
    )
    cross = lax.all_to_all(cross, axes, 0, 0, tiled=True)
    high, low = lag_table(bins, per_dev, groups, 1.0 / (windows * n_day))
    return call(
        lags_kernel,
        jax.ShapeDtypeStruct((far, chans, width), jnp.float32),
        [
            pltpu.VMEM((width * (chans + 1), far), jnp.float32),
            pltpu.VMEM((far, chans, width), jnp.float32),
            pltpu.SemaphoreType.DMA((SENDS,)),
        ],
        [pltpu.VMEM] * 3,
        pltpu.HBM,
        cross.reshape(width * chans, far),
        jnp.asarray(high),
        jnp.asarray(low),
    )


def solution(mesh):
    n_chan, n_day = mesh.shape["chan"], mesh.shape["day"]
    outer = 4 if n_chan % 4 == 0 else 1
    inner = n_chan // outer
    split_mesh = jax.sharding.Mesh(mesh.devices.reshape(outer, inner, n_day), ("outer", "inner", "day"))
    order = np.arange(n_chan * n_day).reshape(n_day, inner, outer).transpose(2, 1, 0).reshape(n_chan, n_day)

    def run(spectra):
        bins = spectra.shape[-1] // 2
        if bins % (n_chan * n_day):
            return jax.shard_map(
                gathered_shards,
                mesh=mesh,
                in_specs=(P("day", "chan", None, None),),
                out_specs=P("day", "chan", None),
                check_vma=False,
            )(spectra)
        return jax.shard_map(
            functools.partial(shards, ("day", "inner", "outer"), order),
            mesh=split_mesh,
            in_specs=(P("day", ("outer", "inner"), None, None),),
            out_specs=P("day", ("outer", "inner"), None),
            check_vma=False,
        )(spectra)

    return run
```

```python
import functools

import jax
import jax.numpy as jnp
import numpy as np
from jax import lax
from jax.experimental import pallas as pl
from jax.experimental.pallas import tpu as pltpu
from jax.sharding import PartitionSpec as P

VMEM_LIMIT = 48 * 1024 * 1024
PACK_VMEM_LIMIT = 53 * 1024 * 1024
FETCHES = 1
SENDS = 2


def freq_taper(bins):
    freq_index = jnp.arange(bins, dtype=jnp.float32)
    half_taper = 0.54 - 0.46 * jnp.cos(2.0 * jnp.pi * (freq_index + 0.5) / bins)
    return jnp.concatenate([half_taper, half_taper])


def whiten(spectra):
    values = spectra.astype(jnp.float32)
    bins = values.shape[-1] // 2
    band_power = jnp.sum(values * values, axis=-1, keepdims=True) / bins + 1e-06
    return (values * freq_taper(bins) / jnp.sqrt(band_power)).astype(jnp.bfloat16)


def lag_matrix(bins):
    lag_count = 2 * bins
    freq_index = jnp.arange(bins, dtype=jnp.int32)
    lag_index = jnp.arange(lag_count, dtype=jnp.int32) - bins
    wound = jnp.mod(freq_index[:, None] * lag_index[None, :], lag_count)
    phase_angle = 2.0 * jnp.pi / lag_count * wound.astype(jnp.float32)
    return jnp.concatenate([jnp.cos(phase_angle), -jnp.sin(phase_angle)], axis=0)


def cross_spectra(far_rows, near_rows):
    bins = far_rows.shape[-1] // 2
    windows = far_rows.shape[-2]
    far_re, far_im = (far_rows[..., :bins], far_rows[..., bins:])
    near_re, near_im = (near_rows[..., :bins], near_rows[..., bins:])
    real_part = jnp.einsum("jwf,iwf->jif", far_re, near_re, preferred_element_type=jnp.float32)
    real_part = real_part + jnp.einsum(
        "jwf,iwf->jif", far_im, near_im, preferred_element_type=jnp.float32
    )
    imag_part = jnp.einsum("jwf,iwf->jif", far_re, near_im, preferred_element_type=jnp.float32)
    imag_part = imag_part - jnp.einsum(
        "jwf,iwf->jif", far_im, near_re, preferred_element_type=jnp.float32
    )
    return jnp.concatenate([real_part, imag_part], axis=-1) / windows


def to_lags(cross, table):
    flat = cross.reshape(-1, cross.shape[-1])
    lagged = jnp.dot(
        flat, table, precision=lax.Precision.HIGHEST, preferred_element_type=jnp.float32
    )
    return lagged.reshape(cross.shape[:-1] + (table.shape[1],))


def gathered_shards(spectra):
    local_white = whiten(spectra)[0]
    gathered = lax.all_gather(local_white, "chan", axis=0, tiled=True)
    table = lag_matrix(local_white.shape[-1] // 2)
    day_count = lax.axis_size("day")
    return lax.psum_scatter(
        to_lags(cross_spectra(gathered, local_white), table) / day_count,
        "day",
        scatter_dimension=0,
        tiled=True,
    )


def lag_table(bins, per_dev, groups, scale):
    lags = 2 * bins
    freq = (np.arange(per_dev)[None, :] * groups + np.arange(groups)[:, None]).reshape(-1)
    wound = (freq[:, None] * (np.arange(lags)[None, :] - bins)) % lags
    angle = 2.0 * np.pi / lags * wound
    table = (np.stack([np.cos(angle), -np.sin(angle)], axis=1) * scale).reshape(2 * bins, lags)
    table = table.astype(np.float32)
    high = table.astype(jnp.bfloat16)
    low = (table - high.astype(np.float32)).astype(jnp.bfloat16)
    return high, low


def pack_kernel(groups, per_dev, spectra_ref, out_ref, held_ref, rows_ref, arrived):
    chans, windows, width = held_ref.shape
    bins = width // 2
    head = bins // 2
    size = (per_dev + 1) * chans
    stride = size + 1
    fetches = arrived.shape[0]
    batch = chans // fetches
    copies = []
    for step in range(fetches):
        part = pl.ds(step * batch, batch)
        copies.append(pltpu.make_async_copy(spectra_ref.at[part], held_ref.at[part], arrived.at[step]))
        copies[-1].start()
    freq = (lax.broadcasted_iota(jnp.int32, (1, width), 1) % bins).astype(jnp.float32)
    taper = 0.54 - 0.46 * jnp.cos(2.0 * jnp.pi * (freq + 0.5) / bins)
    lane = lax.broadcasted_iota(jnp.int32, (windows - head, bins), 1)
    pick = lax.broadcasted_iota(jnp.int32, (groups, bins), 1) % groups
    pick = (pick == lax.broadcasted_iota(jnp.int32, (groups, bins), 0)).astype(jnp.float32).astype(jnp.bfloat16)

    def whiten_channel(ch):
        values = held_ref[ch].astype(jnp.float32)
        power = jnp.sum(values * values, axis=-1, keepdims=True) / bins + 1e-06
        return (values * taper * lax.rsqrt(power)).astype(jnp.bfloat16)

    def place_channel(ch, white):
        real, imag = white[:, :bins], white[:, bins:]
        main = jnp.concatenate([real[:head], imag[:head]], axis=0).astype(jnp.float32).T
        spread = []
        for slot in range(per_dev):
            chosen = lane // groups == slot
            spread += [jnp.where(chosen, part[head:], jnp.zeros_like(part[head:])) for part in (real, imag)]
        tail = lax.dot_general(
            pick, jnp.concatenate(spread, axis=0), (((1,), (1,)), ((), ())), preferred_element_type=jnp.float32
        )
        for slot in range(per_dev):
            part = main[slot * groups:(slot + 1) * groups]
            rows_ref[pl.ds(slot * chans + ch, groups, stride=stride), :] = part
        rows_ref[pl.ds(per_dev * chans + ch, groups, stride=stride), :] = tail

    ready = []
    for step in range(fetches):
        copies[step].wait()
        fresh = [(ch, whiten_channel(ch)) for ch in range(step * batch, (step + 1) * batch)]
        for ch, white in ready:
            place_channel(ch, white)
        ready = fresh
    for ch, white in ready:
        place_channel(ch, white)
    for first in range(0, groups, 4):
        rows = [rows_ref[pl.ds(group * stride, size), :].astype(jnp.bfloat16) for group in range(first, first + 4)]
        for place, part in enumerate(rows):
            out_ref[first + place] = part.reshape(out_ref.shape[1:])


def swap_parts(rows, half):
    lanes = rows.shape[-1]
    values = rows.astype(jnp.float32)
    lane = lax.broadcasted_iota(jnp.int32, values.shape, 1)
    first = (lane % (2 * half)) < half
    ahead = pltpu.roll(values, lanes - half, 1)
    behind = pltpu.roll(values, half, 1)
    return jnp.where(first, ahead, -behind).astype(jnp.bfloat16)


def cross_kernel(order, days, in_ref, out_ref):
    groups, parts, chans, lanes = in_ref.shape
    blocks = groups // days
    per_dev = parts - 1
    total = blocks * chans
    far = out_ref.shape[-1]
    narrow = lanes // per_dev // 2

    def rows(day, part):
        return jnp.concatenate([in_ref[order[block][day], part] for block in range(blocks)], axis=0)

    tails = [rows(day, per_dev) for day in range(days)]
    tails_swapped = [swap_parts(tail, narrow) for tail in tails]
    far_tail = jnp.concatenate(tails, axis=1)
    lane = lax.broadcasted_iota(jnp.int32, (2 * total, lanes), 1) // (2 * narrow)
    dims = (((1,), (1,)), ((), ()))
    for slot in range(per_dev):
        mains = [rows(day, slot) for day in range(days)]
        far_main = jnp.concatenate(mains, axis=1)
        turned = [swap_parts(m, lanes // 2) for m in mains]
        near_main = [jnp.concatenate(pair, axis=0) for pair in zip(mains, turned)]
        near_tail = [jnp.concatenate(pair, axis=0) for pair in zip(tails, tails_swapped)]
        near_tail = [jnp.where(lane == slot, t, jnp.zeros_like(t)) for t in near_tail]
        cross = lax.dot_general(
            jnp.concatenate(near_main, axis=1), far_main, dims, preferred_element_type=jnp.float32
        ) + lax.dot_general(
            jnp.concatenate(near_tail, axis=1), far_tail, dims, preferred_element_type=jnp.float32
        )
        cross = cross.astype(out_ref.dtype)
        for kind in range(2):
            for block in range(blocks):
                start = kind * total + block * chans
                for half in range(days):
                    piece = cross[start:start + chans, half * far:(half + 1) * far]
                    out_ref[order[block][half], 2 * slot + kind] = piece


def lags_kernel(cross_ref, high_ref, low_ref, out_ref, rows_ref, lag_ref, sent):
    chans = out_ref.shape[1]
    depth = high_ref.shape[0]
    high, low = high_ref[...], low_ref[...]
    dims = (((0,), (0,)), ((), ()))
    parts = sent.shape[0]
    batch = chans // parts
    stride = chans + 1
    for row in range(depth):
        rows_ref[pl.ds(row * stride, chans), :] = cross_ref[pl.ds(row * chans, chans), :].astype(jnp.float32)
    copies = []

    def load(ch):
        return rows_ref[pl.ds(ch, depth, stride=stride), :].astype(jnp.bfloat16)

    def store(ch, lag):
        lag_ref[:, ch, :] = lag
        if (ch + 1) % batch == 0:
            step = ch // batch
            done = pl.ds(step * batch, batch)
            copies.append(pltpu.make_async_copy(lag_ref.at[:, done], out_ref.at[:, done], sent.at[step]))
            copies[-1].start()

    part, lag = load(0), None
    for ch in range(chans):
        following = load(ch + 1) if ch + 1 < chans else None
        fresh = lax.dot_general(part, high, dims, preferred_element_type=jnp.float32)
        fresh = fresh + lax.dot_general(part, low, dims, preferred_element_type=jnp.float32)
        if ch:
            store(ch - 1, lag)
        part, lag = following, fresh
    store(chans - 1, lag)
    for copy in copies:
        copy.wait()


def call(kernel, out_shape, scratch, in_spaces, out_space, *operands, vmem=VMEM_LIMIT):
    return pl.pallas_call(
        kernel,
        out_shape=out_shape,
        in_specs=[pl.BlockSpec(memory_space=space) for space in in_spaces],
        out_specs=pl.BlockSpec(memory_space=out_space),
        scratch_shapes=scratch,
        compiler_params=pltpu.CompilerParams(vmem_limit_bytes=vmem),
    )(*operands)


def shards(axes, order, spectra):
    _, chans, windows, width = spectra.shape
    bins = width // 2
    n_chan, n_day = order.shape
    groups = n_chan * n_day
    per_dev = bins // groups
    far = n_chan * chans // n_day

    packed = call(
        functools.partial(pack_kernel, groups, per_dev),
        jax.ShapeDtypeStruct((groups, per_dev + 1, chans, bins), jnp.bfloat16),
        [
            pltpu.VMEM((chans, windows, width), jnp.bfloat16),
            pltpu.VMEM((groups * ((per_dev + 1) * chans + 1), bins), jnp.float32),
            pltpu.SemaphoreType.DMA((FETCHES,)),
        ],
        [pltpu.HBM],
        pltpu.VMEM,
        spectra[0],
        vmem=PACK_VMEM_LIMIT,
    )
    mine = lax.all_to_all(packed, axes, 0, 0, tiled=True)
    cross = call(
        functools.partial(cross_kernel, order.tolist(), n_day),
        jax.ShapeDtypeStruct((groups, 2 * per_dev, chans, far), jnp.bfloat16),
        [],
        [pltpu.VMEM],
        pltpu.VMEM,
        mine,
    )
    cross = lax.all_to_all(cross, axes, 0, 0, tiled=True)
    high, low = lag_table(bins, per_dev, groups, 1.0 / (windows * n_day))
    return call(
        lags_kernel,
        jax.ShapeDtypeStruct((far, chans, width), jnp.float32),
        [
            pltpu.VMEM((width * (chans + 1), far), jnp.float32),
            pltpu.VMEM((far, chans, width), jnp.float32),
            pltpu.SemaphoreType.DMA((SENDS,)),
        ],
        [pltpu.VMEM] * 3,
        pltpu.HBM,
        cross.reshape(width * chans, far),
        jnp.asarray(high),
        jnp.asarray(low),
    )


def solution(mesh):
    n_chan, n_day = mesh.shape["chan"], mesh.shape["day"]
    outer = 4 if n_chan % 4 == 0 else 1
    inner = n_chan // outer
    split_mesh = jax.sharding.Mesh(mesh.devices.reshape(outer, inner, n_day), ("outer", "inner", "day"))
    order = np.arange(n_chan * n_day).reshape(n_day, inner, outer).transpose(2, 1, 0).reshape(n_chan, n_day)

    def run(spectra):
        bins = spectra.shape[-1] // 2
        if bins % (n_chan * n_day):
            return jax.shard_map(
                gathered_shards,
                mesh=mesh,
                in_specs=(P("day", "chan", None, None),),
                out_specs=P("day", "chan", None),
                check_vma=False,
            )(spectra)
        return jax.shard_map(
            functools.partial(shards, ("day", "inner", "outer"), order),
            mesh=split_mesh,
            in_specs=(P("day", ("outer", "inner"), None, None),),
            out_specs=P("day", ("outer", "inner"), None),
            check_vma=False,
        )(spectra)

    return run
```
